32 devices in a mesh: groups: 2 (over x), tiles: 16 (over z, y, core).
Axes of the slice: x: 2, y: 2, z: 4, core: 2. Of those that a mesh axis runs over, the one named last changes fastest.
Arguments:
- video_q: bfloat16 [8192, 3072], P(('groups', 'tiles')), parts along dimension 0, may hold values from -88 to 88, as said below
- video_k: bfloat16 [8192, 3072], P(('groups', 'tiles')), parts along dimension 0, may hold values from -4 to 4, as said below
- video_v: bfloat16 [8192, 3072], P(('groups', 'tiles')), parts along dimension 0, may hold values from -5 to 5
- text_q: bfloat16 [512, 3072], P('groups'), parts along dimension 0, may hold values from -88 to 88
- text_k: bfloat16 [512, 3072], P('groups'), parts along dimension 0, may hold values from -5 to 5
- text_v: bfloat16 [512, 3072], P('groups'), parts along dimension 0, may hold values from -5 to 5
- window: int32 [32, 6], P('tiles'), may hold values from 0 to 13, as said below
- counts: int32 [64], P(('groups', 'tiles')), parts along dimension 0, may hold values from 1 to 128, as said below
- text_count: int32 [2], P('groups'), parts along dimension 0, may hold values from 64 to 256
Outputs:
- video_out: bfloat16 [8192, 3072], P(('groups', 'tiles')), parts along dimension 0
- text_out: bfloat16 [512, 3072], P(('groups', 'tiles')), parts along dimension 0
The draws below stay inside these ranges and needn't reach their ends.
There are 2 independent parts, one for each index of `groups`. The reference program is written for one: setup_inputs(seed, part) draws one part's arguments, and reference() takes and returns one part's arrays. A program takes and returns all parts, laid end to end along the dimension named above; an argument that names none is the same for every part. Nothing has to cross between parts.
Inputs may be any that keep to these rules, and one draw needn't show every extreme that they name: `video_q`: queries drawn for the problem. `video_k`: keys drawn for the problem. `window`: each row names 6 different codes, among them always 3, 6, 9 and 12. `counts`: valid tokens are the first slots of a tile.
All inputs are finite; a program needn't handle non-finite values.
Results may differ from the reference program's by a relative error of at most 0.003.
Values may be sent and summed in bfloat16 or wider, within the bound.
No kernel may reach another device: no remote copies, remote signals or barrier semaphores. Data moves between devices by JAX's collectives and lax.ppermute only.
A program may use at most 192 MiB of HBM per device.

```python
import math
import jax
import jax.numpy as jnp
from jax import lax

HEADS = 24
HD = 128
D = 3072
TOK = 128
CT = 2
NR = 4
WIN = 6
TEXT = 256
TILES_ALL = 32
VIDEO = 4096
N_TILES = 16


def base_keys(key):
    keys_drawn = jnp.clip(jax.random.normal(jax.random.fold_in(key, 11), (VIDEO, D), jnp.float32), -4.0, 4.0)
    return keys_drawn


def draw_video_k(key, part):
    return base_keys(key).astype(jnp.bfloat16)


def draw_video_q(key, part):
    drawn = 2.5 * jnp.clip(jax.random.normal(jax.random.fold_in(key, 23), (VIDEO, D), jnp.float32), -4.0, 4.0)
    return drawn.astype(jnp.bfloat16)


def draw_text_q(key, part):
    drawn = 3.5 * jnp.clip(jax.random.normal(jax.random.fold_in(key, 37), (TEXT, D), jnp.float32), -4.0, 4.0)
    return drawn.astype(jnp.bfloat16)


def draw_window(key, part):
    fixed_codes = jnp.broadcast_to(jnp.array([3, 6, 9, 12], jnp.int32), (TILES_ALL, 4))
    other_codes = jnp.array([0, 1, 2, 4, 5, 7, 8, 10, 11, 13], jnp.int32)
    scores = jax.random.randint(jax.random.fold_in(key, 61), (TILES_ALL, 10), 0, 1 << 20, dtype=jnp.int32)
    scores = scores * 16 + jnp.arange(10, dtype=jnp.int32)[None, :]
    _, picked = lax_top(-scores)
    extra = other_codes[picked]
    return jnp.concatenate([fixed_codes, extra], axis=1)[:, :WIN].astype(jnp.int32)


def lax_top(values):
    return jax.lax.top_k(values, WIN - 4)


def draw_counts(key, part):
    tile_ids = jnp.arange(TILES_ALL, dtype=jnp.int32)
    device = tile_ids // CT
    column = tile_ids % CT
    tiles_devices = TILES_ALL // CT
    row_block = (device + tiles_devices // 2 + NR + NR // 2) % tiles_devices % NR
    edge = (row_block == NR - 1) | (column == CT - 1)
    drawn = jax.random.randint(jax.random.fold_in(key, 5), (TILES_ALL,), 1, TOK + 1, dtype=jnp.int32)
    return jnp.where(edge, drawn, TOK).astype(jnp.int32)


def draw_text_count(key, part):
    drawn = jax.random.randint(jax.random.fold_in(key, 41), (1,), TEXT // 4, TEXT, dtype=jnp.int32)
    return jnp.where(part % 2 == 1, TEXT, drawn).astype(jnp.int32)


def level_of(own_key, dims, pieces, smallest, top_value):
    factor_of = 1.0
    for position, shards_of in pieces:
        heights = jax.random.uniform(jax.random.fold_in(jax.random.fold_in(own_key, 6), position), (shards_of,), jnp.float32, smallest / len(pieces), top_value / len(pieces))
        factor_of = factor_of * jnp.repeat(jnp.exp(heights), dims[position] // shards_of).reshape((-1,) + (1,) * (len(dims) - 1 - position))
    return factor_of


def normal_values(rng, extent, scale, limit, split=(), kind=jnp.bfloat16):
    values = scale * jax.random.normal(rng, extent, jnp.float32)
    if split:
        values = values * level_of(rng, extent, split, -0.22, 0.18)
    return jnp.clip(values, -limit, limit).astype(kind)


def setup_inputs(seed: int = 0, part: int = 0) -> dict:
    key_of = jax.random.split(jax.random.key(seed), 10)
    part_splits = jax.random.split(jax.random.fold_in(key_of[9], part), 10)
    video_q = draw_video_q(jax.random.fold_in(jax.random.fold_in(key_of[9], part), 71), part)
    video_k = draw_video_k(jax.random.fold_in(jax.random.fold_in(key_of[9], part), 71), part)
    video_v = normal_values(part_splits[2], (VIDEO, D), 1.0, 5.0, ((0, 16),))
    text_q = draw_text_q(jax.random.fold_in(jax.random.fold_in(key_of[9], part), 71), part)
    text_k = normal_values(part_splits[4], (TEXT, D), 1.0, 5.0)
    text_v = normal_values(part_splits[5], (TEXT, D), 1.0, 5.0)
    window = draw_window(jax.random.fold_in(key_of[9], 71), part)
    counts = draw_counts(jax.random.fold_in(jax.random.fold_in(key_of[9], part), 71), part)
    text_count = draw_text_count(jax.random.fold_in(jax.random.fold_in(key_of[9], part), 71), part)
    return dict(video_q=video_q, video_k=video_k, video_v=video_v, text_q=text_q, text_k=text_k, text_v=text_v, window=window, counts=counts, text_count=text_count)


def reference(video_q, video_k, video_v, text_q, text_k, text_v, window, counts, text_count):
    score_scale = 1.0 / math.sqrt(HD)
    devices_all = N_TILES
    blocks_time = devices_all // NR
    layout_shift = devices_all // 2 + NR + NR // 2
    spread = ((1, 1), (1, 1), (1, 1), (0, 0), (0, 0), (0, 0))
    key_rolled = jnp.roll(video_k.reshape(devices_all, CT, TOK, HEADS, HD), layout_shift, axis=0)
    value_rolled = jnp.roll(video_v.reshape(devices_all, CT, TOK, HEADS, HD), layout_shift, axis=0)
    count_rolled = jnp.roll(counts.reshape(devices_all, CT), layout_shift, axis=0)
    key_grid = jnp.pad(key_rolled.reshape(blocks_time, NR, CT, TOK, HEADS, HD), spread)
    value_grid = jnp.pad(value_rolled.reshape(blocks_time, NR, CT, TOK, HEADS, HD), spread)
    count_grid = jnp.pad(count_rolled.reshape(blocks_time, NR, CT), ((1, 1), (1, 1), (1, 1)))
    query_tiles = video_q.reshape(devices_all, CT, TOK, HEADS, HD)
    window_rows = window.reshape(devices_all, CT, WIN)
    count_rows = counts.reshape(devices_all, CT)
    text_valid = jnp.arange(TEXT, dtype=jnp.int32) < text_count[0]
    time_step = jnp.array([0, -1, 1, 0, 0], jnp.int32)
    row_step = jnp.array([0, 0, 0, -1, 1], jnp.int32)
    text_keys = text_k.reshape(TEXT, HEADS, HD).astype(jnp.float32)
    text_values = text_v.reshape(TEXT, HEADS, HD).astype(jnp.float32)
    slot_ids = jnp.arange(TOK, dtype=jnp.int32)

    def one_device(device):
        spot = ((device + layout_shift) % devices_all).astype(jnp.int32)
        tblock = (spot // NR).astype(jnp.int32)
        rblock = (spot % NR).astype(jnp.int32)
        zero_at = jnp.zeros((), jnp.int32)
        key_near = lax.dynamic_slice(key_grid, (tblock, rblock, zero_at, zero_at, zero_at, zero_at), (3, 3, CT + 2, TOK, HEADS, HD))
        value_near = lax.dynamic_slice(value_grid, (tblock, rblock, zero_at, zero_at, zero_at, zero_at), (3, 3, CT + 2, TOK, HEADS, HD))
        count_near = lax.dynamic_slice(count_grid, (tblock, rblock, zero_at), (3, 3, CT + 2))
        window_codes = window_rows[device]
        cell_codes = jnp.concatenate([jnp.ones((CT, 1), jnp.int32), (window_codes + (window_codes >= 1)).astype(jnp.int32)], axis=1)
        block_of = cell_codes // 3
        column_at = jnp.arange(CT, dtype=jnp.int32)[:, None] + cell_codes % 3
        time_at = 1 + time_step[block_of]
        row_at = 1 + row_step[block_of]
        keys_chosen = key_near[time_at, row_at, column_at].reshape(CT, (WIN + 1) * TOK, HEADS, HD).astype(jnp.float32)
        values_chosen = value_near[time_at, row_at, column_at].reshape(CT, (WIN + 1) * TOK, HEADS, HD).astype(jnp.float32)
        counts_chosen = count_near[time_at, row_at, column_at]
        key_valid = (slot_ids[None, None, :] < counts_chosen[:, :, None]).reshape(CT, (WIN + 1) * TOK)
        queries = query_tiles[device].astype(jnp.float32)
        video_scores = jnp.einsum('cqhd,ckhd->chqk', queries, keys_chosen) * score_scale
        video_scores = jnp.where(key_valid[:, None, None, :], video_scores, -jnp.inf)
        text_scores = jnp.einsum('cqhd,khd->chqk', queries, text_keys) * score_scale
        text_scores = jnp.where(text_valid[None, None, None, :], text_scores, -jnp.inf)
        row_top = jnp.maximum(lax.optimization_barrier(jnp.max(video_scores, axis=-1)), lax.optimization_barrier(jnp.max(text_scores, axis=-1)))[..., None]
        video_probs = jnp.exp(video_scores - row_top)
        text_probs = jnp.exp(text_scores - row_top)
        denom = lax.optimization_barrier(jnp.sum(video_probs, axis=-1)) + lax.optimization_barrier(jnp.sum(text_probs, axis=-1))
        video_round = lax.optimization_barrier(video_probs.astype(jnp.bfloat16)).astype(jnp.float32)
        text_round = lax.optimization_barrier(text_probs.astype(jnp.bfloat16)).astype(jnp.float32)
        numer = jnp.einsum('chqk,ckhd->cqhd', video_round, values_chosen) + jnp.einsum('chqk,khd->cqhd', text_round, text_values)
        result = numer / jnp.transpose(denom, (0, 2, 1))[..., None]
        query_valid = slot_ids[None, :] < count_rows[device][:, None]
        return jnp.where(query_valid[:, :, None, None], result, 0.0).astype(jnp.bfloat16)
    device_ids = jnp.arange(devices_all, dtype=jnp.int32)
    video_out = lax.map(one_device, device_ids).reshape(VIDEO, D)
    key_blocks = video_k.reshape(devices_all, CT * TOK, HEADS, HD)
    value_blocks = video_v.reshape(devices_all, CT * TOK, HEADS, HD)
    valid_blocks = (slot_ids[None, None, :] < count_rows[:, :, None]).reshape(devices_all, CT * TOK)
    text_queries = text_q.reshape(TEXT, HEADS, HD).astype(jnp.float32)

    def block_scores(device):
        scores = jnp.einsum('qhd,khd->hqk', text_queries, key_blocks[device].astype(jnp.float32)) * score_scale
        return jnp.where(valid_blocks[device][None, None, :], scores, -jnp.inf)

    def block_top(device):
        return lax.optimization_barrier(jnp.max(block_scores(device), axis=-1))
    global_top = lax.optimization_barrier(jnp.max(lax.map(block_top, device_ids), axis=0))

    def accumulate(carry, device):
        weights = jnp.exp(block_scores(device) - global_top[..., None])
        denom_part = lax.optimization_barrier(jnp.sum(weights, axis=-1))
        weights_round = lax.optimization_barrier(weights.astype(jnp.bfloat16)).astype(jnp.float32)
        numer_part = jnp.einsum('hqk,khd->qhd', weights_round, value_blocks[device].astype(jnp.float32))
        return ((carry[0] + numer_part, carry[1] + denom_part.T), None)
    start_sums = (jnp.zeros((TEXT, HEADS, HD), jnp.float32), jnp.zeros((TEXT, HEADS), jnp.float32))
    (numer_all, denom_all), _ = lax.scan(accumulate, start_sums, device_ids)
    text_result = numer_all / denom_all[..., None]
    text_out = jnp.where(text_valid[:, None, None], text_result, 0.0).astype(jnp.bfloat16).reshape(TEXT, D)
    return (video_out, text_out)
```

```python
import functools
import math

import jax
import jax.numpy as jnp
from jax import lax
from jax.experimental import pallas as pl
from jax.experimental.pallas import tpu as pltpu
from jax.sharding import PartitionSpec as P

HEADS = 24
HD = 128
NR = 4
CELLS = 7
CHUNKS = 6
VMEM_BYTES = 40 * 1024 * 1024
LOG2E = 1.4426950408889634


def tile_pairs(n):
    shift = n // 2 + NR + NR // 2
    times = n // NR

    def at(t, r):
        return (t * NR + r - shift) % n

    rows = range(NR)
    pairs = {}
    pairs["earlier"] = [(at(t - 1, r), at(t, r)) for t in range(1, times) for r in rows]
    pairs["later"] = [(at(t + 1, r), at(t, r)) for t in range(times - 1) for r in rows]
    pairs["above"] = [(at(t, r - 1), at(t, r)) for t in range(times) for r in (1, 3)]
    pairs["above"].append((at(times - 1, 1), at(times - 1, 2)))
    pairs["below"] = [(at(t, r + 1), at(t, r)) for t in range(times) for r in (0, 2)]
    pairs["below"].append((at(0, 2), at(0, 1)))
    pairs["above_far"] = [(at(t + 1, 1), at(t, 2)) for t in range(times - 1)]
    pairs["below_far"] = [(at(t - 1, 2), at(t, 1)) for t in range(1, times)]
    return pairs


def dot_nt(a, b):
    return lax.dot_general(a, b, (((1,), (1,)), ((), ())), preferred_element_type=jnp.float32)


def video_kernel(table, q, k_own, v_own, earlier, later, above, below, above_far, below_far,
                 text_k, text_v, *rest):
    out, k_all, v_all, k_cat, v_cat = rest[-5:]
    tok = q.shape[0] // 2
    text = text_k.shape[0]
    video_keys = CELLS * tok
    scale = LOG2E / math.sqrt(HD)

    def put(block, k, v):
        for c in range(2):
            rows = pl.ds(c * tok, tok)
            k_all[2 * block + c] = k[rows, :]
            v_all[2 * block + c] = v[rows, :]

    def put_packed(block, ref):
        put(block, ref.at[pl.ds(0, 2 * tok)], ref.at[pl.ds(2 * tok, 2 * tok)])

    put(0, k_own, v_own)
    put_packed(1, earlier)
    put_packed(2, later)
    far_above = table[2 * CELLS * 2 + 3]
    far_below = table[2 * CELLS * 2 + 4]

    @pl.when(far_above == 1)
    def _():
        put_packed(3, above_far)

    @pl.when(far_above == 0)
    def _():
        put_packed(3, above)

    @pl.when(far_below == 1)
    def _():
        put_packed(4, below_far)

    @pl.when(far_below == 0)
    def _():
        put_packed(4, below)

    lane = lax.broadcasted_iota(jnp.int32, (1, tok), 1)
    text_lane = lax.broadcasted_iota(jnp.int32, (1, text), 1)
    text_bias = jnp.where(text_lane < table[2 * CELLS * 2 + 2], 0.0, -jnp.inf)
    slot = lax.broadcasted_iota(jnp.int32, (tok, 1), 0)
    for c in range(2):
        biases = []
        for j in range(CELLS):
            cell = table[c * CELLS + j]
            count = table[(2 + c) * CELLS + j]
            k_cat[c, pl.ds(j * tok, tok), :] = k_all[cell]
            v_cat[c, pl.ds(j * tok, tok), :] = v_all[cell]
            biases.append(jnp.where(lane < count, 0.0, -jnp.inf))
        k_cat[c, pl.ds(video_keys, text), :] = text_k[...]
        v_cat[c, pl.ds(video_keys, text), :] = text_v[...]
        biases.append(text_bias)
        bias = jnp.concatenate(biases, axis=1)
        s = dot_nt(q[pl.ds(c * tok, tok), :], k_cat[c]) + bias
        top = jnp.max(s, axis=1, keepdims=True)
        p = jnp.exp2((s - top) * scale)
        denom = jnp.sum(p, axis=1, keepdims=True)
        acc = jnp.dot(p.astype(jnp.bfloat16), v_cat[c], preferred_element_type=jnp.float32)
        valid = slot < table[2 * CELLS * 2 + c]
        out[pl.ds(c * tok, tok), :] = jnp.where(valid, acc / denom, 0.0).astype(out.dtype)


def video_call(chunk, heads, table, q, k, v, near, text_k, text_v, carried):
    rows, width = q.shape
    text = text_k.shape[0]
    tok = rows // 2
    first = chunk * heads
    whole = lambda h: (0, first + h)
    part = lambda h: (0, h)
    own_spec = pl.BlockSpec((rows, HD), whole)
    near_spec = pl.BlockSpec((2 * rows, HD), part)
    text_spec = pl.BlockSpec((text, HD), whole)
    in_specs = [pl.BlockSpec(memory_space=pltpu.SMEM), own_spec, own_spec, own_spec]
    in_specs += [near_spec] * 6 + [text_spec] * 2
    operands = [table, q, k, v, *near, text_k, text_v]
    aliases = {}
    if carried is not None:
        aliases = {len(operands): 0}
        operands.append(carried)
        in_specs.append(pl.BlockSpec(memory_space=pl.ANY))
    keys = CELLS * tok + text
    return pl.pallas_call(
        video_kernel,
        grid=(heads,),
        in_specs=in_specs,
        out_specs=pl.BlockSpec((rows, HD), whole),
        out_shape=jax.ShapeDtypeStruct((rows, width), q.dtype),
        scratch_shapes=[
            pltpu.VMEM((10, tok, HD), q.dtype),
            pltpu.VMEM((10, tok, HD), q.dtype),
            pltpu.VMEM((2, keys, HD), q.dtype),
            pltpu.VMEM((2, keys, HD), q.dtype),
        ],
        input_output_aliases=aliases,
        compiler_params=pltpu.CompilerParams(vmem_limit_bytes=VMEM_BYTES),
        cost_estimate=pl.CostEstimate(
            flops=heads * rows * keys * HD * 4,
            bytes_accessed=heads * rows * HD * 40,
            transcendentals=heads * rows * keys,
        ),
        name="video_attention",
    )(*operands)


def key_bias(counts, tok, rows):
    lane = lax.broadcasted_iota(jnp.int32, (1, tok), 1)
    return jnp.concatenate(
        [jnp.where(lane < counts[c], 0.0, -jnp.inf) for c in range(rows // tok)], axis=1
    )


def text_top_kernel(counts, q, k, top):
    h = pl.program_id(0)
    rows = k.shape[0]
    s = dot_nt(q[...], k[...]) * (1.0 / math.sqrt(HD)) + key_bias(counts, rows // 2, rows)
    lane = lax.broadcasted_iota(jnp.int32, top.shape, 1)
    own = jnp.max(s, axis=1, keepdims=True)

    @pl.when(h == 0)
    def _():
        top[...] = jnp.zeros_like(top)

    top[...] = jnp.where(lane == h, own, top[...])


def text_sum_kernel(counts, q, k, v, top, out, denoms):
    h = pl.program_id(0)
    rows = k.shape[0]
    lane = lax.broadcasted_iota(jnp.int32, top.shape, 1)

    @pl.when(h == 0)
    def _():
        denoms[...] = jnp.zeros_like(denoms)

    @pl.when(h < HEADS)
    def _():
        s = dot_nt(q[...], k[...]) * (1.0 / math.sqrt(HD)) + key_bias(counts, rows // 2, rows)
        own = jnp.sum(jnp.where(lane == h, top[...], 0.0), axis=1, keepdims=True)
        w = jnp.exp(s - own)
        denoms[...] = jnp.where(lane == h, jnp.sum(w, axis=1, keepdims=True), denoms[...])
        out[...] = jnp.dot(w.astype(jnp.bfloat16), v[...], preferred_element_type=jnp.float32)

    @pl.when(h == HEADS)
    def _():
        out[...] = denoms[...]


def text_partials(counts, q, k, v):
    text = q.shape[0]
    rows = k.shape[0]
    smem = pl.BlockSpec(memory_space=pltpu.SMEM)
    q_spec = pl.BlockSpec((text, HD), lambda h: (0, jnp.minimum(h, HEADS - 1)))
    k_spec = pl.BlockSpec((rows, HD), lambda h: (0, jnp.minimum(h, HEADS - 1)))
    flat = pl.BlockSpec((text, HD), lambda h: (0, 0))
    params = pltpu.CompilerParams(vmem_limit_bytes=VMEM_BYTES)
    work = HEADS * text * rows
    top = pl.pallas_call(
        text_top_kernel,
        grid=(HEADS,),
        in_specs=[smem, q_spec, k_spec],
        out_specs=flat,
        out_shape=jax.ShapeDtypeStruct((text, HD), jnp.float32),
        compiler_params=params,
        cost_estimate=pl.CostEstimate(
            flops=2 * work * HD, bytes_accessed=4 * text * HEADS * HD, transcendentals=0
        ),
        name="text_top",
    )(counts, q, k)
    top = lax.pmax(top, "tiles")
    return pl.pallas_call(
        text_sum_kernel,
        grid=(HEADS + 1,),
        in_specs=[smem, q_spec, k_spec, k_spec, flat],
        out_specs=pl.BlockSpec((text, HD), lambda h: (0, h)),
        out_shape=jax.ShapeDtypeStruct((text, (HEADS + 1) * HD), jnp.float32),
        scratch_shapes=[pltpu.VMEM((text, HD), jnp.float32)],
        compiler_params=params,
        cost_estimate=pl.CostEstimate(
            flops=4 * work * HD, bytes_accessed=10 * text * HEADS * HD, transcendentals=work
        ),
        name="text_sum",
    )(counts, q, k, v, top)


def cell_table(window, counts, all_counts, text_count, spot, n):
    times = n // NR
    t, r = spot // NR, spot % NR
    shift = n // 2 + NR + NR // 2
    steps_t = jnp.array([0, -1, 1, 0, 0], jnp.int32)
    steps_r = jnp.array([0, 0, 0, -1, 1], jnp.int32)
    near_t, near_r = t + steps_t, r + steps_r
    inside = (near_t >= 0) & (near_t < times) & (near_r >= 0) & (near_r < NR)
    place = (near_t * NR + near_r - shift) % n
    near_counts = jnp.where(inside[:, None], all_counts[place], 0)
    columns = counts.shape[0]
    codes = jnp.concatenate(
        [jnp.ones((columns, 1), jnp.int32), window + (window >= 1)], axis=1
    ).astype(jnp.int32)
    block = codes // 3
    column = jnp.arange(columns, dtype=jnp.int32)[:, None] + codes % 3 - 1
    held = (column >= 0) & (column < columns)
    column = jnp.clip(column, 0, columns - 1)
    cell = block * columns + column
    valid = jnp.where(held, near_counts.reshape(-1)[cell], 0)
    flags = jnp.stack([(r == 2) & (t < times - 1), (r == 1) & (t > 0)]).astype(jnp.int32)
    return jnp.concatenate([cell.reshape(-1), valid.reshape(-1), counts, text_count, flags])


def per_device(n, video_q, video_k, video_v, text_q, text_k, text_v, window, counts, text_count):
    rows, width = video_q.shape
    text = text_q.shape[0]
    pairs = tile_pairs(n)
    position = lax.axis_index("tiles")
    spot = (position + n // 2 + NR + NR // 2) % n
    all_counts = lax.all_gather(counts, "tiles")
    table = cell_table(window, counts, all_counts, text_count, spot, n)

    partials = text_partials(counts, text_q, video_k, video_v)
    sums = lax.psum_scatter(partials, "tiles", scatter_dimension=0, tiled=True)

    heads = HEADS // CHUNKS
    step = heads * HD
    video_out = None
    for chunk in range(CHUNKS):
        cols = slice(chunk * step, (chunk + 1) * step)
        packed = jnp.concatenate([video_k[:, cols], video_v[:, cols]], axis=0)
        near = {}
        for name in ("earlier", "later", "above", "below"):
            near[name] = lax.ppermute(packed, "tiles", pairs[name])
        above_far = lax.ppermute(near["earlier"], "tiles", pairs["above_far"])
        below_far = lax.ppermute(near["later"], "tiles", pairs["below_far"])
        sides = [near["earlier"], near["later"], near["above"], near["below"], above_far, below_far]
        video_out = video_call(
            chunk, heads, table, video_q, video_k, video_v, sides, text_k, text_v, video_out
        )

    share = text // n
    denoms = sums[:, width : width + HEADS]
    text_result = sums[:, :width].reshape(share, HEADS, HD) / denoms[:, :, None]
    row_ids = position * share + jnp.arange(share, dtype=jnp.int32)
    text_out = jnp.where((row_ids < text_count[0])[:, None, None], text_result, 0.0)
    text_out = text_out.astype(jnp.bfloat16).reshape(share, width)
    return (video_out, text_out)


def solution(mesh):
    tiles = mesh.shape["tiles"]
    return jax.shard_map(
        functools.partial(per_device, tiles),
        mesh=mesh,
        in_specs=(
            P(("groups", "tiles"), None),
            P(("groups", "tiles"), None),
            P(("groups", "tiles"), None),
            P("groups", None),
            P("groups", None),
            P("groups", None),
            P("tiles", None),
            P(("groups", "tiles")),
            P("groups"),
        ),
        out_specs=(P(("groups", "tiles"), None), P(("groups", "tiles"), None)),
        check_vma=False,
    )
```

```python
import functools
import math

import jax
import jax.numpy as jnp
from jax import lax
from jax.experimental import pallas as pl
from jax.experimental.pallas import tpu as pltpu
from jax.sharding import PartitionSpec as P

HEADS = 24
HD = 128
NR = 4
BLOCKS = 5
STEP_HEADS = 2
CHUNK_HEADS = (8, 6, 6, 4)
DIVERTED = (False, True, True, False)
PAD_ROWS = 16
VMEM_BYTES = 48 * 1024 * 1024
LOG2E = 1.4426950408889634
SOURCES = ("own", "earlier", "later", "relayed", "above", "below")


def spot_shift(n):
    return n // 2 + NR + NR // 2


def plan_moves(n, diverted):
    shift, times = spot_shift(n), n // NR
    last = times - 1

    def at(t, r):
        return (t * NR + r - shift) % n

    moves = {
        "earlier": {at(t - 1, r): at(t, r) for t in range(1, times) for r in range(NR)},
        "later": {at(t + 1, r): at(t, r) for t in range(last) for r in range(NR)},
        "above": {at(t, r - 1): at(t, r) for t in range(times) for r in (1, 3)},
        "below": {at(t, r + 1): at(t, r) for t in range(times) for r in (0, 2)},
    }
    relay_earlier = {at(t + 1, 1): at(t, 2) for t in range(last)}
    relay_later = {at(t - 1, 2): at(t, 1) for t in range(1, times)}
    if times == 4:
        moves["later"][at(0, 2)] = at(3, 2)
        relay_later[at(3, 2)] = at(0, 1)
        moves["later"][at(3, 3)] = at(3, 0)
        relay_later[at(3, 0)] = at(2, 3)
        if diverted:
            moves["earlier"][at(2, 2)] = at(0, 0)
            relay_earlier[at(0, 0)] = at(3, 2)
            moves["earlier"][at(2, 3)] = at(0, 1)
            relay_earlier[at(0, 1)] = at(3, 3)
            moves["earlier"][at(3, 1)] = at(3, 2)
        else:
            moves["earlier"][at(3, 1)] = at(0, 1)
            relay_earlier[at(0, 1)] = at(3, 2)
    else:
        moves["above"][at(last, 1)] = at(last, 2)
        moves["below"][at(0, 2)] = at(0, 1)
    assert not set(relay_earlier) & set(relay_later)
    moves["relayed"] = {**relay_earlier, **relay_later}
    held = {"own": {d: d for d in range(n)}}
    for name in ("earlier", "later", "above", "below"):
        held[name] = {dst: src for src, dst in moves[name].items()}
    held["relayed"] = {dst: held["earlier"].get(src) for src, dst in relay_earlier.items()}
    held["relayed"].update({dst: held["later"].get(src) for src, dst in relay_later.items()})
    choice = []
    for device in range(n):
        spot = (device + shift) % n
        t, r = spot // NR, spot % NR
        row = []
        for dt, dr in ((-1, 0), (1, 0), (0, -1), (0, 1)):
            found = -1
            if 0 <= t + dt < times and 0 <= r + dr < NR:
                wanted = at(t + dt, r + dr)
                found = [i for i, s in enumerate(SOURCES) if held[s].get(device) == wanted][0]
            row.append(found)
        choice.append(row)
    for move in moves.values():
        assert len(set(move.values())) == len(move)
    pairs = {name: sorted(move.items()) for name, move in moves.items()}
    return pairs, [int(d in relay_later) for d in range(n)], choice


def dot_nt(a, b):
    return lax.dot_general(a, b, (((1,), (1,)), ((), ())), preferred_element_type=jnp.float32)


def dot_nn(a, b):
    return jnp.dot(a, b, preferred_element_type=jnp.float32)


def lane_tiles(x):
    return [x[:, i : i + HD] for i in range(0, x.shape[1], HD)]


def row_reduce(op, final, pieces):
    tiles = [tile for piece in pieces for tile in lane_tiles(piece)]
    return final(functools.reduce(op, tiles), axis=1, keepdims=True)


TABLE_COUNTS, TABLE_TEXT, TABLE_CHOICE = 4, 6, 7


def video_kernel(kind, table, q, k_own, v_own, *rest):
    packed = {"earlier": rest[0], "later": rest[1], "above": rest[4], "below": rest[5]}
    relayed_k, relayed_v, text_k, text_v = rest[2], rest[3], rest[6], rest[7]
    out, k_all, v_all, bias_all = rest[-4:]
    tok = q.shape[0] // 2
    text = text_k.shape[0]
    scale = LOG2E / math.sqrt(HD)
    near = BLOCKS * tok
    dead = 2 * BLOCKS
    lane = lax.broadcasted_iota(jnp.int32, (8, tok), 1)
    lane_f = lane.astype(jnp.float32)

    def put(block, k, v, v_row):
        for i in range(STEP_HEADS):
            cols = pl.ds(i * HD, HD)
            for c in range(2):
                rows = pl.ds((c * BLOCKS + block) * tok, tok)
                k_all[i, rows, :] = k[pl.ds(c * tok, tok), cols]
                v_all[i, rows, :] = v[pl.ds(v_row + c * tok, tok), cols]

    def put_limits(block, tail):
        limits = tail[...].astype(jnp.float32)
        for c in range(2):
            bias_all[c * BLOCKS + block] = jnp.where(lane_f < limits[c : c + 1, :], 0.0, -jnp.inf)

    put(0, k_own, v_own, 0)
    for c in range(2):
        bias_all[c * BLOCKS] = jnp.where(lane < table[TABLE_COUNTS + c], 0.0, -jnp.inf)
    tail = (pl.ds(2 * tok, PAD_ROWS), pl.ds(0, HD))
    options = {1: ("earlier",), 2: ("later",), 3: ("above", "earlier"), 4: ("below", "later")}
    zeros = jnp.zeros((tok, HD), k_all.dtype)
    for block in range(1, BLOCKS):
        chosen = table[TABLE_CHOICE + 4 * kind + block - 1]
        for name in options[block]:

            @pl.when(chosen == SOURCES.index(name))
            def _(ref=packed[name], block=block):
                put(block, ref, ref, 2 * tok + PAD_ROWS)
                put_limits(block, ref.at[tail])

        @pl.when(chosen == SOURCES.index("relayed"))
        def _(block=block):
            put(block, relayed_k, relayed_v, 0)
            put_limits(block, relayed_k.at[tail])

        @pl.when(chosen < 0)
        def _(block=block):
            for c in range(2):
                bias_all[c * BLOCKS + block] = jnp.full((8, tok), -jnp.inf, jnp.float32)
                for i in range(STEP_HEADS):
                    rows = pl.ds((c * BLOCKS + block) * tok, tok)
                    k_all[i, rows, :] = zeros
                    v_all[i, rows, :] = zeros

    bias_all[dead] = jnp.full((8, tok), -jnp.inf, jnp.float32)
    for i in range(STEP_HEADS):
        k_all[i, pl.ds(dead * tok, tok), :] = zeros
        v_all[i, pl.ds(dead * tok, tok), :] = zeros

    text_lane = lax.broadcasted_iota(jnp.int32, (1, text), 1)
    text_bias = jnp.where(text_lane < table[TABLE_TEXT], 0.0, -jnp.inf)
    slot = lax.broadcasted_iota(jnp.int32, (tok, 1), 0)
    for i in range(STEP_HEADS):
        cols = pl.ds(i * HD, HD)
        for c in range(2):
            query = q[pl.ds(c * tok, tok), cols]
            fixed = pl.ds(c * near, near)
            fixed_bias = jnp.concatenate(
                [bias_all[c * BLOCKS + b][0:1] for b in range(BLOCKS)], axis=1
            )
            scores = [dot_nt(query, k_all[i, fixed, :]) + fixed_bias]
            values = [v_all[i, fixed, :]]
            for j in range(2):
                cell = table[2 * c + j]
                rows = pl.ds(pl.multiple_of(cell * tok, tok), tok)
                scores.append(dot_nt(query, k_all[i, rows, :]) + bias_all[cell][0:1])
                values.append(v_all[i, rows, :])
            scores.append(dot_nt(query, text_k[:, cols]) + text_bias)
            values.append(text_v[:, cols])
            top = row_reduce(jnp.maximum, jnp.max, scores)
            probs = [jnp.exp2((s - top) * scale) for s in scores]
            denom = row_reduce(jnp.add, jnp.sum, probs)
            acc = sum(dot_nn(p.astype(jnp.bfloat16), v) for p, v in zip(probs, values))
            valid = slot < table[TABLE_COUNTS + c]
            out[pl.ds(c * tok, tok), cols] = jnp.where(valid, acc / denom, 0.0).astype(out.dtype)


def video_call(kind, first, heads, table, q, k, v, near, text_k, text_v, carried):
    rows, width = q.shape
    text = text_k.shape[0]
    tok = rows // 2
    step = STEP_HEADS * HD
    base = first // STEP_HEADS
    whole = lambda h: (0, base + h)
    part = lambda h: (0, h)
    own_spec = pl.BlockSpec((rows, step), whole)
    part_spec = pl.BlockSpec((2 * rows + PAD_ROWS, step), part)
    whole_spec = pl.BlockSpec((2 * rows + PAD_ROWS, step), whole)
    text_spec = pl.BlockSpec((text, step), whole)
    in_specs = [pl.BlockSpec(memory_space=pltpu.SMEM), own_spec, own_spec, own_spec]
    in_specs += [part_spec] * 2
    in_specs += [pl.BlockSpec((rows + PAD_ROWS, step), part), pl.BlockSpec((rows, step), part)]
    in_specs += [whole_spec] * 2 + [text_spec] * 2
    operands = [table, q, k, v, *near, text_k, text_v]
    aliases = {}
    if carried is not None:
        aliases = {len(operands): 0}
        operands.append(carried)
        in_specs.append(pl.BlockSpec(memory_space=pl.ANY))
    cells = 2 * BLOCKS + 1
    keys = 7 * tok + text
    return pl.pallas_call(
        functools.partial(video_kernel, kind),
        grid=(heads // STEP_HEADS,),
        in_specs=in_specs,
        out_specs=own_spec,
        out_shape=jax.ShapeDtypeStruct((rows, width), q.dtype),
        scratch_shapes=[
            pltpu.VMEM((STEP_HEADS, cells * tok, HD), q.dtype),
            pltpu.VMEM((STEP_HEADS, cells * tok, HD), q.dtype),
            pltpu.VMEM((cells, 8, tok), jnp.float32),
        ],
        input_output_aliases=aliases,
        compiler_params=pltpu.CompilerParams(vmem_limit_bytes=VMEM_BYTES),
        cost_estimate=pl.CostEstimate(
            flops=heads * rows * keys * HD // 4,
            bytes_accessed=heads * rows * HD,
            transcendentals=0,
        ),
        name="video_attention",
    )(*operands)


STAT_SUMS = 32


def text_kernel(order, counts, q, k, v, keep, send, top, denom):
    step = pl.program_id(0)
    rows = k.shape[0]
    text = q.shape[0]
    half = text // 2
    share = text // order.shape[0]
    lane = lax.broadcasted_iota(jnp.int32, (text, HD), 1)

    @pl.when(step == 0)
    def _():
        top[...] = jnp.zeros_like(top)
        denom[...] = jnp.zeros_like(denom)

    @pl.when(step < HEADS // STEP_HEADS)
    def _():
        slot = lax.broadcasted_iota(jnp.int32, (1, rows // 2), 1)
        bias = jnp.concatenate(
            [jnp.where(slot < counts[c], 0.0, -jnp.inf) for c in range(2)], axis=1
        )
        for i in range(STEP_HEADS):
            cols = pl.ds(i * HD, HD)
            head = step * STEP_HEADS + i
            query = jnp.concatenate(
                [
                    q[pl.ds(pl.multiple_of(order[j] * share, share), share), cols]
                    for j in range(order.shape[0])
                ],
                axis=0,
            )
            s = dot_nt(query, k[:, cols]) * (1.0 / math.sqrt(HD)) + bias
            m = row_reduce(jnp.maximum, jnp.max, [s])
            w = jnp.exp(s - m)
            l = row_reduce(jnp.add, jnp.sum, [w])
            high = w.astype(jnp.bfloat16)
            low = (w - high.astype(jnp.float32)).astype(jnp.bfloat16)
            acc = dot_nn(high, v[:, cols]) + dot_nn(low, v[:, cols])
            top[...] = jnp.where(lane == head, m, top[...])
            denom[...] = jnp.where(lane == head + STAT_SUMS, l, denom[...])
            keep[:, cols] = acc[:half]
            send[:, cols] = acc[half:]

    @pl.when(step == HEADS // STEP_HEADS)
    def _():
        stats = top[...] + denom[...]
        keep[:, pl.ds(0, HD)] = stats[:half]
        send[:, pl.ds(0, HD)] = stats[half:]


def text_local(order, counts, q, k, v):
    text = q.shape[0]
    rows = k.shape[0]
    step = STEP_HEADS * HD
    last = HEADS // STEP_HEADS - 1
    smem = pl.BlockSpec(memory_space=pltpu.SMEM)
    q_spec = pl.BlockSpec((text, step), lambda h: (0, jnp.minimum(h, last)))
    k_spec = pl.BlockSpec((rows, step), lambda h: (0, jnp.minimum(h, last)))
    out_spec = pl.BlockSpec((text // 2, step), lambda h: (0, h))
    shape = jax.ShapeDtypeStruct((text // 2, HEADS * HD + step), jnp.float32)
    work = HEADS * text * rows
    return pl.pallas_call(
        text_kernel,
        grid=(last + 2,),
        in_specs=[smem, smem, q_spec, k_spec, k_spec],
        out_specs=[out_spec, out_spec],
        out_shape=[shape, shape],
        scratch_shapes=[pltpu.VMEM((text, HD), jnp.float32)] * 2,
        compiler_params=pltpu.CompilerParams(vmem_limit_bytes=VMEM_BYTES),
        cost_estimate=pl.CostEstimate(
            flops=work * HD // 4, bytes_accessed=text * HEADS * HD, transcendentals=0
        ),
        name="text_partials",
    )(order, counts, q, k, v)


def merge_kernel(finish, *refs):
    width = HEADS * HD
    stat_cols = pl.ds(width, HD)
    keep, got = refs[:2]
    mine = keep[:, stat_cols]
    theirs = got[:, stat_cols]
    lane = lax.broadcasted_iota(jnp.int32, mine.shape, 1)
    is_top = lane < STAT_SUMS
    top = jnp.maximum(mine, theirs)
    a = jnp.exp(jnp.where(is_top, mine - top, 0.0))
    b = jnp.exp(jnp.where(is_top, theirs - top, 0.0))
    sums = []
    for h in range(HEADS):
        at = slice(h, h + 1)
        to = slice(STAT_SUMS + h, STAT_SUMS + h + 1)
        sums.append(mine[:, to] * a[:, at] + theirs[:, to] * b[:, at])
    if finish:
        limit, out = refs[2:]
        share = out.shape[0]
        row = lax.broadcasted_iota(jnp.int32, (share, 1), 0)
        valid = row < limit[0]
        for h in range(HEADS):
            cols = pl.ds(h * HD, HD)
            at = slice(h, h + 1)
            acc = keep[:, cols] * a[:, at] + got[:, cols] * b[:, at]
            out[:, cols] = jnp.where(valid, acc / sums[h], 0.0).astype(out.dtype)
        return
    next_keep, next_send = refs[2:]
    half = next_keep.shape[0]
    stats = jnp.where(is_top, top, 0.0)
    for h in range(HEADS):
        cols = pl.ds(h * HD, HD)
        at = slice(h, h + 1)
        acc = keep[:, cols] * a[:, at] + got[:, cols] * b[:, at]
        stats = jnp.where(lane == STAT_SUMS + h, sums[h], stats)
        next_keep[:, cols] = acc[:half]
        next_send[:, cols] = acc[half:]
    next_keep[:, stat_cols] = stats[:half]
    next_send[:, stat_cols] = stats[half:]


def text_merge(keep, got):
    half = keep.shape[0] // 2
    shape = jax.ShapeDtypeStruct((half, (HEADS + 1) * HD), jnp.float32)
    return pl.pallas_call(
        functools.partial(merge_kernel, False),
        out_shape=[shape, shape],
        compiler_params=pltpu.CompilerParams(vmem_limit_bytes=VMEM_BYTES),
        name="text_merge",
    )(keep, got)


def text_finish(keep, got, limit):
    share = keep.shape[0]
    vmem = pl.BlockSpec(memory_space=pltpu.VMEM)
    return pl.pallas_call(
        functools.partial(merge_kernel, True),
        in_specs=[vmem, vmem, pl.BlockSpec(memory_space=pltpu.SMEM)],
        out_shape=jax.ShapeDtypeStruct((share, HEADS * HD), jnp.bfloat16),
        compiler_params=pltpu.CompilerParams(vmem_limit_bytes=VMEM_BYTES),
        name="text_finish",
    )(keep, got, limit)


def slot_order(n, position):
    bits = n.bit_length() - 1
    mirrored = [int(format(i, f"0{bits}b")[::-1], 2) for i in range(n)]
    return jnp.array(mirrored, jnp.int32) ^ position.astype(jnp.int32)


def text_plain(position, n, text_count, q, k, v, counts):
    text, width = q.shape
    share = text // n
    keys = k.reshape(-1, HEADS, HD)
    values = v.reshape(-1, HEADS, HD)
    slots = jnp.arange(k.shape[0] // counts.shape[0], dtype=jnp.int32)
    valid = (slots[None, :] < counts[:, None]).reshape(-1)
    scores = jnp.einsum(
        "qhd,khd->hqk", q.reshape(text, HEADS, HD), keys, preferred_element_type=jnp.float32
    ) * (1.0 / math.sqrt(HD))
    scores = jnp.where(valid[None, None, :], scores, -jnp.inf)
    top = lax.pmax(jnp.max(scores, axis=-1), "tiles")
    weights = jnp.exp(scores - top[..., None])
    denom = jnp.sum(weights, axis=-1).T
    numer = jnp.einsum(
        "hqk,khd->qhd", weights.astype(jnp.bfloat16), values, preferred_element_type=jnp.float32
    ).reshape(text, width)
    numer = lax.psum_scatter(numer, "tiles", scatter_dimension=0, tiled=True)
    denom = lax.psum_scatter(denom, "tiles", scatter_dimension=0, tiled=True)
    result = numer.reshape(share, HEADS, HD) / denom[:, :, None]
    row_ids = position * share + jnp.arange(share, dtype=jnp.int32)
    result = jnp.where((row_ids < text_count[0])[:, None, None], result, 0.0)
    return result.astype(jnp.bfloat16).reshape(share, width)


def make_table(window, counts, text_count, choices, position):
    columns = counts.shape[0]
    extra = (window % 3 != 0) | (window == 0)
    rank = jnp.cumsum(extra.astype(jnp.int32), axis=1) * extra
    codes = jnp.stack([jnp.sum(jnp.where(rank == j, window, 0), axis=1) for j in (1, 2)], axis=1)
    cells = codes + (codes >= 1)
    own = jnp.arange(columns, dtype=jnp.int32)[:, None]
    column = own + cells % 3 - 1
    inside = (column >= 0) & (column < columns)
    extra_cells = jnp.where(inside, column * BLOCKS + cells // 3, columns * BLOCKS)
    chosen = lax.dynamic_index_in_dim(jnp.array(choices, jnp.int32), position, 0, False)
    parts = [extra_cells.reshape(-1), counts, text_count, chosen]
    return jnp.concatenate([part.astype(jnp.int32) for part in parts])


def tie(value, *others):
    return lax.optimization_barrier((value, *others))[0]


def per_device(n, video_q, video_k, video_v, text_q, text_k, text_v, window, counts, text_count):
    rows, width = video_q.shape
    text = text_q.shape[0]
    position = lax.axis_index("tiles")
    plans = [plan_moves(n, kind) for kind in (False, True)]
    choices = [plans[0][2][d] + plans[1][2][d] for d in range(n)]
    sends_later = jnp.array(plans[0][1], jnp.int32)[position] == 1
    table = make_table(window, counts, text_count, choices, position)

    limits = jnp.concatenate([counts, jnp.zeros((PAD_ROWS - counts.shape[0],), jnp.int32)])
    limits = jnp.broadcast_to(limits.astype(jnp.bfloat16)[:, None], (PAD_ROWS, width))

    def pack(cols):
        return jnp.concatenate([video_k[:, cols], limits[:, cols], video_v[:, cols]], axis=0)

    starts = [sum(CHUNK_HEADS[:i]) for i in range(len(CHUNK_HEADS))]
    direct, outs = [], []

    def send(i, *before):
        cols = slice(starts[i] * HD, (starts[i] + CHUNK_HEADS[i]) * HD)
        mine = tie(pack(cols), *before)
        pairs = plans[DIVERTED[i]][0]
        direct.append([lax.ppermute(mine, "tiles", pairs[x]) for x in ("earlier", "later")])

    send(0)
    everything = pack(slice(0, width))
    sides = [lax.ppermute(everything, "tiles", plans[0][0][x]) for x in ("above", "below")]
    halving = text % (PAD_ROWS * n) == 0 and n & (n - 1) == 0
    stages = n.bit_length() - 1
    parts = []
    if halving:
        order = tie(slot_order(n, position), *sides)
        parts = [text_local(order, counts, text_q, video_k, video_v)]

    def exchanged(i):
        return lax.ppermute(parts[i][1], "tiles", [(d, d ^ (1 << i)) for d in range(n)])

    def merge(*before):
        i = len(parts) - 1
        if 0 <= i < stages - 1:
            parts.append(text_merge(tie(parts[i][0], *before), exchanged(i)))

    for i in range(len(CHUNK_HEADS)):
        pairs = plans[DIVERTED[i]][0]
        if i + 1 < len(CHUNK_HEADS):
            before = outs[-1:] + ([parts[-1][0]] if halving else [])
            send(i + 1, *direct[i], *before)
        up, down = direct[i]
        if i + 1 == len(CHUNK_HEADS):
            before = outs[-1:]
            if halving:
                limit = text_count - position.astype(jnp.int32) * (text // n)
                text_out = text_finish(parts[-1][0], exchanged(stages - 1), limit)
                before.append(text_out)
            up, down = tie(up, *before), tie(down, *before)
        relays = [
            lax.ppermute(jnp.where(sends_later, down[half], up[half]), "tiles", pairs["relayed"])
            for half in (slice(0, rows + PAD_ROWS), slice(rows + PAD_ROWS, None))
        ]
        merge(*relays)
        outs.append(
            video_call(
                int(DIVERTED[i]), starts[i], CHUNK_HEADS[i], table, video_q, video_k, video_v,
                [*direct[i], *relays, *sides], text_k, text_v, outs[-1] if outs else None,
            )
        )
        merge(outs[-1])
    if not halving:
        text_out = text_plain(position, n, text_count, text_q, video_k, video_v, counts)
    return (outs[-1], text_out)


def solution(mesh):
    tiles = mesh.shape["tiles"]
    return jax.shard_map(
        functools.partial(per_device, tiles),
        mesh=mesh,
        in_specs=(
            P(("groups", "tiles"), None),
            P(("groups", "tiles"), None),
            P(("groups", "tiles"), None),
            P("groups", None),
            P("groups", None),
            P("groups", None),
            P("tiles", None),
            P(("groups", "tiles")),
            P("groups"),
        ),
        out_specs=(P(("groups", "tiles"), None), P(("groups", "tiles"), None)),
        check_vma=False,
    )
```

```python
import functools
import math

import jax
import jax.numpy as jnp
from jax import lax
from jax.experimental import pallas as pl
from jax.experimental.pallas import tpu as pltpu
from jax.sharding import PartitionSpec as P

HEADS = 24
HD = 128
NR = 4
BLOCKS = 5
STEP_HEADS = 2
CHUNK_HEADS = (8, 6, 6, 4)
DIVERTED = (False, True, True, False)
PAD_ROWS = 16
VMEM_BYTES = 48 * 1024 * 1024
LOG2E = 1.4426950408889634
SOURCES = ("own", "earlier", "later", "relayed", "beside")


def spot_shift(n):
    return n // 2 + NR + NR // 2


def plan_moves(n, diverted):
    shift, times = spot_shift(n), n // NR
    last = times - 1

    def at(t, r):
        return (t * NR + r - shift) % n

    moves = {
        "earlier": {at(t - 1, r): at(t, r) for t in range(1, times) for r in range(NR)},
        "later": {at(t + 1, r): at(t, r) for t in range(last) for r in range(NR)},
        "beside": {at(t, r): at(t, r ^ 1) for t in range(times) for r in range(NR)},
    }
    relay_earlier = {at(t + 1, 1): at(t, 2) for t in range(last)}
    relay_later = {at(t - 1, 2): at(t, 1) for t in range(1, times)}
    moves["later"][at(0, 2)] = at(last, 2)
    relay_later[at(last, 2)] = at(0, 1)
    if times == 4:
        moves["later"][at(3, 3)] = at(3, 0)
        relay_later[at(3, 0)] = at(2, 3)
    if times == 4 and diverted:
        moves["earlier"][at(2, 2)] = at(0, 0)
        relay_earlier[at(0, 0)] = at(3, 2)
        moves["earlier"][at(2, 3)] = at(0, 1)
        relay_earlier[at(0, 1)] = at(3, 3)
        moves["earlier"][at(3, 1)] = at(3, 2)
    else:
        moves["earlier"][at(last, 1)] = at(0, 1)
        relay_earlier[at(0, 1)] = at(last, 2)
    assert not set(relay_earlier) & set(relay_later)
    moves["relayed"] = {**relay_earlier, **relay_later}
    held = {"own": {d: d for d in range(n)}}
    for name in ("earlier", "later", "beside"):
        held[name] = {dst: src for src, dst in moves[name].items()}
    held["relayed"] = {dst: held["earlier"].get(src) for src, dst in relay_earlier.items()}
    held["relayed"].update({dst: held["later"].get(src) for src, dst in relay_later.items()})
    choice = []
    for device in range(n):
        spot = (device + shift) % n
        t, r = spot // NR, spot % NR
        row = []
        for dt, dr in ((-1, 0), (1, 0), (0, -1), (0, 1)):
            found = -1
            if 0 <= t + dt < times and 0 <= r + dr < NR:
                wanted = at(t + dt, r + dr)
                found = [i for i, s in enumerate(SOURCES) if held[s].get(device) == wanted][0]
            row.append(found)
        choice.append(row)
    for move in moves.values():
        assert len(set(move.values())) == len(move)
    pairs = {name: sorted(move.items()) for name, move in moves.items()}
    return pairs, [int(d in relay_later) for d in range(n)], choice


def dot_nt(a, b):
    return lax.dot_general(a, b, (((1,), (1,)), ((), ())), preferred_element_type=jnp.float32)


def dot_nn(a, b):
    return jnp.dot(a, b, preferred_element_type=jnp.float32)


def lane_tiles(x):
    return [x[:, i : i + HD] for i in range(0, x.shape[1], HD)]


def row_reduce(op, final, pieces):
    tiles = [tile for piece in pieces for tile in lane_tiles(piece)]
    return final(functools.reduce(op, tiles), axis=1, keepdims=True)


TABLE_COUNTS, TABLE_BESIDE, TABLE_TEXT, TABLE_CHOICE = 4, 6, 8, 9


def video_kernel(kind, table, q, k_own, v_own, *rest):
    packed = {"earlier": rest[0], "later": rest[1]}
    relayed_k, relayed_v, beside_k, beside_v, text_k, text_v = rest[2:8]
    out, k_all, v_all, bias_all = rest[-4:]
    tok = q.shape[0] // 2
    text = text_k.shape[0]
    scale = LOG2E / math.sqrt(HD)
    near = BLOCKS * tok
    dead = 2 * BLOCKS
    lane = lax.broadcasted_iota(jnp.int32, (8, tok), 1)
    lane_f = lane.astype(jnp.float32)

    def put(block, k, v, v_row):
        for i in range(STEP_HEADS):
            cols = pl.ds(i * HD, HD)
            for c in range(2):
                rows = pl.ds((c * BLOCKS + block) * tok, tok)
                k_all[i, rows, :] = k[pl.ds(c * tok, tok), cols]
                v_all[i, rows, :] = v[pl.ds(v_row + c * tok, tok), cols]

    def put_limits(block, tail):
        limits = tail[...].astype(jnp.float32)
        for c in range(2):
            bias_all[c * BLOCKS + block] = jnp.where(lane_f < limits[c : c + 1, :], 0.0, -jnp.inf)

    def put_counts(block, at):
        for c in range(2):
            bias_all[c * BLOCKS + block] = jnp.where(lane < table[at + c], 0.0, -jnp.inf)

    put(0, k_own, v_own, 0)
    put_counts(0, TABLE_COUNTS)
    tail = (pl.ds(2 * tok, PAD_ROWS), pl.ds(0, HD))
    options = {1: ("earlier",), 2: ("later",), 3: ("earlier",), 4: ("later",)}
    zeros = jnp.zeros((tok, HD), k_all.dtype)
    for block in range(1, BLOCKS):
        chosen = table[TABLE_CHOICE + 4 * kind + block - 1]
        for name in options[block]:

            @pl.when(chosen == SOURCES.index(name))
            def _(ref=packed[name], block=block):
                put(block, ref, ref, 2 * tok + PAD_ROWS)
                put_limits(block, ref.at[tail])

        @pl.when(chosen == SOURCES.index("relayed"))
        def _(block=block):
            put(block, relayed_k, relayed_v, 0)
            put_limits(block, relayed_k.at[tail])

        if block > 2:

            @pl.when(chosen == SOURCES.index("beside"))
            def _(block=block):
                put(block, beside_k, beside_v, 0)
                put_counts(block, TABLE_BESIDE)

        @pl.when(chosen < 0)
        def _(block=block):
            for c in range(2):
                bias_all[c * BLOCKS + block] = jnp.full((8, tok), -jnp.inf, jnp.float32)
                for i in range(STEP_HEADS):
                    rows = pl.ds((c * BLOCKS + block) * tok, tok)
                    k_all[i, rows, :] = zeros
                    v_all[i, rows, :] = zeros

    bias_all[dead] = jnp.full((8, tok), -jnp.inf, jnp.float32)
    for i in range(STEP_HEADS):
        k_all[i, pl.ds(dead * tok, tok), :] = zeros
        v_all[i, pl.ds(dead * tok, tok), :] = zeros

    text_lane = lax.broadcasted_iota(jnp.int32, (1, text), 1)
    text_bias = jnp.where(text_lane < table[TABLE_TEXT], 0.0, -jnp.inf)
    slot = lax.broadcasted_iota(jnp.int32, (tok, 1), 0)
    for i in range(STEP_HEADS):
        cols = pl.ds(i * HD, HD)
        for c in range(2):
            query = q[pl.ds(c * tok, tok), cols]
            fixed = pl.ds(c * near, near)
            fixed_bias = jnp.concatenate(
                [bias_all[c * BLOCKS + b][0:1] for b in range(BLOCKS)], axis=1
            )
            scores = [dot_nt(query, k_all[i, fixed, :]) + fixed_bias]
            values = [v_all[i, fixed, :]]
            for j in range(2):
                cell = table[2 * c + j]
                rows = pl.ds(pl.multiple_of(cell * tok, tok), tok)
                scores.append(dot_nt(query, k_all[i, rows, :]) + bias_all[cell][0:1])
                values.append(v_all[i, rows, :])
            scores.append(dot_nt(query, text_k[:, cols]) + text_bias)
            values.append(text_v[:, cols])
            top = row_reduce(jnp.maximum, jnp.max, scores)
            probs = [jnp.exp2((s - top) * scale) for s in scores]
            denom = row_reduce(jnp.add, jnp.sum, probs)
            acc = sum(dot_nn(p.astype(jnp.bfloat16), v) for p, v in zip(probs, values))
            valid = slot < table[TABLE_COUNTS + c]
            out[pl.ds(c * tok, tok), cols] = jnp.where(valid, acc / denom, 0.0).astype(out.dtype)


def video_call(kind, first, heads, table, q, k, v, near, text_k, text_v, carried):
    rows, width = q.shape
    text = text_k.shape[0]
    tok = rows // 2
    step = STEP_HEADS * HD
    base = first // STEP_HEADS
    whole = lambda h: (0, base + h)
    part = lambda h: (0, h)
    own_spec = pl.BlockSpec((rows, step), whole)
    part_spec = pl.BlockSpec((2 * rows + PAD_ROWS, step), part)
    text_spec = pl.BlockSpec((text, step), whole)
    in_specs = [pl.BlockSpec(memory_space=pltpu.SMEM), own_spec, own_spec, own_spec]
    in_specs += [part_spec] * 2
    in_specs += [pl.BlockSpec((rows + PAD_ROWS, step), part), pl.BlockSpec((rows, step), part)]
    in_specs += [own_spec] * 2 + [text_spec] * 2
    operands = [table, q, k, v, *near, text_k, text_v]
    aliases = {}
    if carried is not None:
        aliases = {len(operands): 0}
        operands.append(carried)
        in_specs.append(pl.BlockSpec(memory_space=pl.ANY))
    cells = 2 * BLOCKS + 1
    keys = 7 * tok + text
    return pl.pallas_call(
        functools.partial(video_kernel, kind),
        grid=(heads // STEP_HEADS,),
        in_specs=in_specs,
        out_specs=own_spec,
        out_shape=jax.ShapeDtypeStruct((rows, width), q.dtype),
        scratch_shapes=[
            pltpu.VMEM((STEP_HEADS, cells * tok, HD), q.dtype),
            pltpu.VMEM((STEP_HEADS, cells * tok, HD), q.dtype),
            pltpu.VMEM((cells, 8, tok), jnp.float32),
        ],
        input_output_aliases=aliases,
        compiler_params=pltpu.CompilerParams(vmem_limit_bytes=VMEM_BYTES),
        cost_estimate=pl.CostEstimate(
            flops=heads * rows * keys * HD // 4,
            bytes_accessed=heads * rows * HD,
            transcendentals=0,
        ),
        name="video_attention",
    )(*operands)


STAT_SUMS = 32
PAIR_HEADS = HEADS // 2


def text_kernel(order, counts, q, k, v, k_beside, v_beside, keep, send, top, denom):
    step = pl.program_id(0)
    rows = k.shape[0]
    text = q.shape[0]
    half = text // 2
    places = order.shape[0] - 1
    share = text // places
    lane = lax.broadcasted_iota(jnp.int32, (text, HD), 1)

    @pl.when(step == 0)
    def _():
        top[...] = jnp.zeros_like(top)
        denom[...] = jnp.zeros_like(denom)

    @pl.when(step < PAIR_HEADS // STEP_HEADS)
    def _():
        slot = lax.broadcasted_iota(jnp.int32, (1, rows // 2), 1)
        bias = [
            jnp.concatenate(
                [jnp.where(slot < counts[at + c], 0.0, -jnp.inf) for c in range(2)], axis=1
            )
            for at in (0, 2)
        ]
        for i in range(STEP_HEADS):
            cols = pl.ds(i * HD, HD)
            head = step * STEP_HEADS + i
            query = jnp.concatenate(
                [
                    q[pl.ds(pl.multiple_of(order[j] * share, share), share), cols]
                    for j in range(places)
                ],
                axis=0,
            )
            scores = [
                dot_nt(query, keys[:, cols]) * (1.0 / math.sqrt(HD)) + bound
                for keys, bound in zip((k, k_beside), bias)
            ]
            m = row_reduce(jnp.maximum, jnp.max, scores)
            weights = [jnp.exp(s - m) for s in scores]
            l = row_reduce(jnp.add, jnp.sum, weights)
            acc = 0.0
            for w, values in zip(weights, (v, v_beside)):
                high = w.astype(jnp.bfloat16)
                low = (w - high.astype(jnp.float32)).astype(jnp.bfloat16)
                acc = acc + dot_nn(high, values[:, cols]) + dot_nn(low, values[:, cols])
            top[...] = jnp.where(lane == head, m, top[...])
            denom[...] = jnp.where(lane == head + STAT_SUMS, l, denom[...])
            keep[:, cols] = acc[:half]
            send[:, cols] = acc[half:]

    @pl.when(step == PAIR_HEADS // STEP_HEADS)
    def _():
        stats = top[...] + denom[...]
        keep[:, pl.ds(0, HD)] = stats[:half]
        send[:, pl.ds(0, HD)] = stats[half:]


def text_local(order, counts, q, k, v, k_beside, v_beside):
    text = q.shape[0]
    rows = k.shape[0]
    step = STEP_HEADS * HD
    last = PAIR_HEADS // STEP_HEADS - 1
    at = lambda h, order, counts: (0, order[order.shape[0] - 1] + jnp.minimum(h, last))
    k_spec = pl.BlockSpec((rows, step), at)
    out_spec = pl.BlockSpec((text // 2, step), lambda h, order, counts: (0, h))
    shape = jax.ShapeDtypeStruct((text // 2, PAIR_HEADS * HD + step), jnp.float32)
    return pl.pallas_call(
        text_kernel,
        grid_spec=pltpu.PrefetchScalarGridSpec(
            num_scalar_prefetch=2,
            grid=(last + 2,),
            in_specs=[pl.BlockSpec((text, step), at)] + [k_spec] * 4,
            out_specs=[out_spec, out_spec],
            scratch_shapes=[pltpu.VMEM((text, HD), jnp.float32)] * 2,
        ),
        out_shape=[shape, shape],
        compiler_params=pltpu.CompilerParams(vmem_limit_bytes=VMEM_BYTES),
        cost_estimate=pl.CostEstimate(
            flops=text * rows * HD, bytes_accessed=text * HEADS * HD, transcendentals=0
        ),
        name="text_partials",
    )(order, counts, q, k, v, k_beside, v_beside)


def merge_kernel(finish, *refs):
    width = PAIR_HEADS * HD
    stat_cols = pl.ds(width, HD)
    keep, got = refs[:2]
    mine = keep[:, stat_cols]
    theirs = got[:, stat_cols]
    lane = lax.broadcasted_iota(jnp.int32, mine.shape, 1)
    is_top = lane < STAT_SUMS
    top = jnp.maximum(mine, theirs)
    a = jnp.exp(jnp.where(is_top, mine - top, 0.0))
    b = jnp.exp(jnp.where(is_top, theirs - top, 0.0))
    first, second = refs[-2:]
    half = first.shape[0]
    stats = jnp.where(is_top, top, 0.0)
    if finish:
        limits = refs[2]
        row = lax.broadcasted_iota(jnp.int32, (2 * half, 1), 0)
        valid = row < jnp.where(row < half, limits[0], limits[1] + half)
    for h in range(PAIR_HEADS):
        cols = pl.ds(h * HD, HD)
        at = slice(h, h + 1)
        to = slice(STAT_SUMS + h, STAT_SUMS + h + 1)
        total = mine[:, to] * a[:, at] + theirs[:, to] * b[:, at]
        acc = keep[:, cols] * a[:, at] + got[:, cols] * b[:, at]
        if finish:
            acc = jnp.where(valid, acc / total, 0.0)
        else:
            stats = jnp.where(lane == STAT_SUMS + h, total, stats)
        first[:, cols] = acc[:half].astype(first.dtype)
        second[:, cols] = acc[half:].astype(second.dtype)
    if not finish:
        first[:, stat_cols] = stats[:half]
        second[:, stat_cols] = stats[half:]


def text_merge(keep, got):
    shape = jax.ShapeDtypeStruct((keep.shape[0] // 2, (PAIR_HEADS + 1) * HD), jnp.float32)
    return pl.pallas_call(
        functools.partial(merge_kernel, False),
        out_shape=[shape, shape],
        compiler_params=pltpu.CompilerParams(vmem_limit_bytes=VMEM_BYTES),
        name="text_merge",
    )(keep, got)


def text_finish(keep, got, limits):
    shape = jax.ShapeDtypeStruct((keep.shape[0] // 2, PAIR_HEADS * HD), jnp.bfloat16)
    vmem = pl.BlockSpec(memory_space=pltpu.VMEM)
    return pl.pallas_call(
        functools.partial(merge_kernel, True),
        in_specs=[vmem, vmem, pl.BlockSpec(memory_space=pltpu.SMEM)],
        out_shape=[shape, shape],
        compiler_params=pltpu.CompilerParams(vmem_limit_bytes=VMEM_BYTES),
        name="text_finish",
    )(keep, got, limits)


def text_order(n, position):
    bits = n.bit_length() - 1
    masks = [1 << b for b in (*range(1, bits), 0)]
    owners = [
        sum(mask for j, mask in enumerate(masks) if i >> (bits - 1 - j) & 1) for i in range(n)
    ]
    order = jnp.array(owners, jnp.int32) ^ position
    first = position % 2 * (PAIR_HEADS // STEP_HEADS)
    return jnp.concatenate([order, first[None]])


def text_plain(position, n, text_count, q, k, v, counts):
    text, width = q.shape
    share = text // n
    keys = k.reshape(-1, HEADS, HD)
    values = v.reshape(-1, HEADS, HD)
    slots = jnp.arange(k.shape[0] // counts.shape[0], dtype=jnp.int32)
    valid = (slots[None, :] < counts[:, None]).reshape(-1)
    scores = jnp.einsum(
        "qhd,khd->hqk", q.reshape(text, HEADS, HD), keys, preferred_element_type=jnp.float32
    ) * (1.0 / math.sqrt(HD))
    scores = jnp.where(valid[None, None, :], scores, -jnp.inf)
    top = lax.pmax(jnp.max(scores, axis=-1), "tiles")
    weights = jnp.exp(scores - top[..., None])
    denom = jnp.sum(weights, axis=-1).T
    numer = jnp.einsum(
        "hqk,khd->qhd", weights.astype(jnp.bfloat16), values, preferred_element_type=jnp.float32
    ).reshape(text, width)
    numer = lax.psum_scatter(numer, "tiles", scatter_dimension=0, tiled=True)
    denom = lax.psum_scatter(denom, "tiles", scatter_dimension=0, tiled=True)
    result = numer.reshape(share, HEADS, HD) / denom[:, :, None]
    row_ids = position * share + jnp.arange(share, dtype=jnp.int32)
    result = jnp.where((row_ids < text_count[0])[:, None, None], result, 0.0)
    return result.astype(jnp.bfloat16).reshape(share, width)


def make_table(window, counts, counts_beside, text_count, choices, position):
    columns = counts.shape[0]
    extra = (window % 3 != 0) | (window == 0)
    rank = jnp.cumsum(extra.astype(jnp.int32), axis=1) * extra
    codes = jnp.stack([jnp.sum(jnp.where(rank == j, window, 0), axis=1) for j in (1, 2)], axis=1)
    cells = codes + (codes >= 1)
    own = jnp.arange(columns, dtype=jnp.int32)[:, None]
    column = own + cells % 3 - 1
    inside = (column >= 0) & (column < columns)
    extra_cells = jnp.where(inside, column * BLOCKS + cells // 3, columns * BLOCKS)
    chosen = lax.dynamic_index_in_dim(jnp.array(choices, jnp.int32), position, 0, False)
    parts = [extra_cells.reshape(-1), counts, counts_beside, text_count, chosen]
    return jnp.concatenate([part.astype(jnp.int32) for part in parts])


def tie(value, *others):
    return lax.optimization_barrier((value, *others))[0]


def per_device(n, video_q, video_k, video_v, text_q, text_k, text_v, window, counts, text_count):
    rows, width = video_q.shape
    text = text_q.shape[0]
    position = lax.axis_index("tiles").astype(jnp.int32)
    plans = [plan_moves(n, kind) for kind in (False, True)]
    choices = [plans[0][2][d] + plans[1][2][d] for d in range(n)]
    sends_later = jnp.array(plans[0][1], jnp.int32)[position] == 1

    limits = jnp.concatenate([counts, jnp.zeros((PAD_ROWS - counts.shape[0],), jnp.int32)])
    limits = jnp.broadcast_to(limits.astype(jnp.bfloat16)[:, None], (PAD_ROWS, width))

    def pack(cols):
        return jnp.concatenate([video_k[:, cols], limits[:, cols], video_v[:, cols]], axis=0)

    starts = [sum(CHUNK_HEADS[:i]) for i in range(len(CHUNK_HEADS))]
    direct, outs = [], []

    def send(i, *before):
        cols = slice(starts[i] * HD, (starts[i] + CHUNK_HEADS[i]) * HD)
        mine = tie(pack(cols), *before)
        pairs = plans[DIVERTED[i]][0]
        direct.append([lax.ppermute(mine, "tiles", pairs[x]) for x in ("earlier", "later")])

    send(0)
    beside = [
        lax.ppermute(x, "tiles", plans[0][0]["beside"]) for x in (counts, video_k, video_v)
    ]
    send(1, *beside)
    table = make_table(window, counts, beside[0], text_count, choices, position)
    halving = text % (PAD_ROWS * n) == 0 and n & (n - 1) == 0
    stages = n.bit_length() - 1
    parts = []
    if halving:
        order = text_order(n, position)
        both = jnp.concatenate([counts, beside[0]])
        parts.append(text_local(order, both, text_q, video_k, video_v, *beside[1:]))

    def exchanged(i):
        return lax.ppermute(parts[i][1], "tiles", [(d, d ^ (2 << i)) for d in range(n)])

    def merge(*before):
        i = len(parts) - 1
        if 0 <= i < stages - 2:
            parts.append(text_merge(tie(parts[i][0], *before), exchanged(i)))
        elif i == stages - 2:
            share = text // n
            limits = [text_count - place * share for place in (position, position ^ 1)]
            limits = jnp.concatenate(limits)
            parts.append(text_finish(tie(parts[i][0], *before), exchanged(i), limits))

    count = len(CHUNK_HEADS)
    for i in range(count):
        pairs = plans[DIVERTED[i]][0]
        up, down = direct[i]
        before = [parts[0][0]] if halving and i == 0 else outs[-1:]
        up, down = tie(up, *before), tie(down, *before)
        relays = [
            lax.ppermute(jnp.where(sends_later, down[half], up[half]), "tiles", pairs["relayed"])
            for half in (slice(0, rows + PAD_ROWS), slice(rows + PAD_ROWS, None))
        ]
        if i + 2 < count:
            send(i + 2, *direct[i])
        merge(*relays)
        outs.append(
            video_call(
                int(DIVERTED[i]), starts[i], CHUNK_HEADS[i], table, video_q, video_k, video_v,
                [*direct[i], *relays, *beside[1:]], text_k, text_v, outs[-1] if outs else None,
            )
        )
    if halving:
        mine, leave = parts[-1]
        got = lax.ppermute(leave, "tiles", [(d, d ^ 1) for d in range(n)])
        low, high = jnp.concatenate([mine, got], axis=1), jnp.concatenate([got, mine], axis=1)
        text_out = jnp.where(position % 2 == 0, low, high)
    if not halving:
        text_out = text_plain(position, n, text_count, text_q, video_k, video_v, counts)
    return (outs[-1], text_out)


def solution(mesh):
    tiles = mesh.shape["tiles"]
    return jax.shard_map(
        functools.partial(per_device, tiles),
        mesh=mesh,
        in_specs=(
            P(("groups", "tiles"), None),
            P(("groups", "tiles"), None),
            P(("groups", "tiles"), None),
            P("groups", None),
            P("groups", None),
            P("groups", None),
            P("tiles", None),
            P(("groups", "tiles")),
            P("groups"),
        ),
        out_specs=(P(("groups", "tiles"), None), P(("groups", "tiles"), None)),
        check_vma=False,
    )
```

```python
import functools
import math

import jax
import jax.numpy as jnp
from jax import lax
from jax.experimental import pallas as pl
from jax.experimental.pallas import tpu as pltpu
from jax.sharding import PartitionSpec as P

HEADS = 24
HD = 128
NR = 4
BLOCKS = 5
STEP_HEADS = 2
CHUNK_HEADS = (8, 6, 6, 4)
PAD_ROWS = 16
VMEM_BYTES = 48 * 1024 * 1024
LOG2E = 1.4426950408889634
SOURCES = ("own", "earlier", "later", "relayed", "beside")


def spot_shift(n):
    return n // 2 + NR + NR // 2


def plan_moves(n):
    shift, times = spot_shift(n), n // NR
    last = times - 1

    def at(t, r):
        return (t * NR + r - shift) % n

    moves = {
        "earlier": {at(t - 1, r): at(t, r) for t in range(1, times) for r in range(NR)},
        "later": {at(t + 1, r): at(t, r) for t in range(last) for r in range(NR)},
        "beside": {at(t, r): at(t, r ^ 1) for t in range(times) for r in range(NR)},
    }
    relay_earlier = {at(t + 1, 1): at(t, 2) for t in range(last)}
    relay_later = {at(t - 1, 2): at(t, 1) for t in range(1, times)}
    moves["later"][at(0, 2)] = at(last, 2)
    relay_later[at(last, 2)] = at(0, 1)
    moves["earlier"][at(last, 1)] = at(0, 1)
    relay_earlier[at(0, 1)] = at(last, 2)
    assert not set(relay_earlier) & set(relay_later)
    moves["relayed"] = {**relay_earlier, **relay_later}
    held = {"own": {d: d for d in range(n)}}
    for name in ("earlier", "later", "beside"):
        held[name] = {dst: src for src, dst in moves[name].items()}
    held["relayed"] = {dst: held["earlier"].get(src) for src, dst in relay_earlier.items()}
    held["relayed"].update({dst: held["later"].get(src) for src, dst in relay_later.items()})
    choice = []
    for device in range(n):
        spot = (device + shift) % n
        t, r = spot // NR, spot % NR
        row = []
        for dt, dr in ((-1, 0), (1, 0), (0, -1), (0, 1)):
            found = -1
            if 0 <= t + dt < times and 0 <= r + dr < NR:
                wanted = at(t + dt, r + dr)
                found = [i for i, s in enumerate(SOURCES) if held[s].get(device) == wanted][0]
            row.append(found)
        choice.append(row)
    for move in moves.values():
        assert len(set(move.values())) == len(move)
    pairs = {name: sorted(move.items()) for name, move in moves.items()}
    return pairs, [int(d in relay_later) for d in range(n)], choice


def dot_nt(a, b):
    return lax.dot_general(a, b, (((1,), (1,)), ((), ())), preferred_element_type=jnp.float32)


def dot_nn(a, b):
    return jnp.dot(a, b, preferred_element_type=jnp.float32)


def lane_tiles(x):
    return [x[:, i : i + HD] for i in range(0, x.shape[1], HD)]


def row_reduce(op, final, pieces):
    tiles = [tile for piece in pieces for tile in lane_tiles(piece)]
    return final(functools.reduce(op, tiles), axis=1, keepdims=True)


TABLE_COUNTS, TABLE_BESIDE, TABLE_TEXT, TABLE_CHOICE = 4, 6, 8, 9


def video_kernel(table, q, k_own, v_own, *rest):
    packed = {"earlier": rest[0], "later": rest[1]}
    relayed_k, relayed_v, beside_k, beside_v, text_k, text_v = rest[2:8]
    out, k_all, v_all, bias_all = rest[-4:]
    tok = q.shape[0] // 2
    text = text_k.shape[0]
    scale = LOG2E / math.sqrt(HD)
    near = BLOCKS * tok
    dead = 2 * BLOCKS
    lane = lax.broadcasted_iota(jnp.int32, (8, tok), 1)
    lane_f = lane.astype(jnp.float32)

    def put(block, k, v, v_row):
        for i in range(STEP_HEADS):
            cols = pl.ds(i * HD, HD)
            for c in range(2):
                rows = pl.ds((c * BLOCKS + block) * tok, tok)
                k_all[i, rows, :] = k[pl.ds(c * tok, tok), cols]
                v_all[i, rows, :] = v[pl.ds(v_row + c * tok, tok), cols]

    def put_limits(block, tail):
        limits = tail[...].astype(jnp.float32)
        for c in range(2):
            bias_all[c * BLOCKS + block] = jnp.where(lane_f < limits[c : c + 1, :], 0.0, -jnp.inf)

    def put_counts(block, at):
        for c in range(2):
            bias_all[c * BLOCKS + block] = jnp.where(lane < table[at + c], 0.0, -jnp.inf)

    put(0, k_own, v_own, 0)
    put_counts(0, TABLE_COUNTS)
    tail = (pl.ds(2 * tok, PAD_ROWS), pl.ds(0, HD))
    options = {1: ("earlier",), 2: ("later",), 3: ("earlier",), 4: ("later",)}
    zeros = jnp.zeros((tok, HD), k_all.dtype)
    for block in range(1, BLOCKS):
        chosen = table[TABLE_CHOICE + block - 1]
        for name in options[block]:

            @pl.when(chosen == SOURCES.index(name))
            def _(ref=packed[name], block=block):
                put(block, ref, ref, 2 * tok + PAD_ROWS)
                put_limits(block, ref.at[tail])

        @pl.when(chosen == SOURCES.index("relayed"))
        def _(block=block):
            put(block, relayed_k, relayed_v, 0)
            put_limits(block, relayed_k.at[tail])

        if block > 2:

            @pl.when(chosen == SOURCES.index("beside"))
            def _(block=block):
                put(block, beside_k, beside_v, 0)
                put_counts(block, TABLE_BESIDE)

        @pl.when(chosen < 0)
        def _(block=block):
            for c in range(2):
                bias_all[c * BLOCKS + block] = jnp.full((8, tok), -jnp.inf, jnp.float32)
                for i in range(STEP_HEADS):
                    rows = pl.ds((c * BLOCKS + block) * tok, tok)
                    k_all[i, rows, :] = zeros
                    v_all[i, rows, :] = zeros

    bias_all[dead] = jnp.full((8, tok), -jnp.inf, jnp.float32)
    for i in range(STEP_HEADS):
        k_all[i, pl.ds(dead * tok, tok), :] = zeros
        v_all[i, pl.ds(dead * tok, tok), :] = zeros

    text_lane = lax.broadcasted_iota(jnp.int32, (1, text), 1)
    text_bias = jnp.where(text_lane < table[TABLE_TEXT], 0.0, -jnp.inf)
    slot = lax.broadcasted_iota(jnp.int32, (tok, 1), 0)
    for i in range(STEP_HEADS):
        cols = pl.ds(i * HD, HD)
        for c in range(2):
            query = q[pl.ds(c * tok, tok), cols]
            fixed = pl.ds(c * near, near)
            fixed_bias = jnp.concatenate(
                [bias_all[c * BLOCKS + b][0:1] for b in range(BLOCKS)], axis=1
            )
            scores = [dot_nt(query, k_all[i, fixed, :]) + fixed_bias]
            values = [v_all[i, fixed, :]]
            for j in range(2):
                cell = table[2 * c + j]
                rows = pl.ds(pl.multiple_of(cell * tok, tok), tok)
                scores.append(dot_nt(query, k_all[i, rows, :]) + bias_all[cell][0:1])
                values.append(v_all[i, rows, :])
            scores.append(dot_nt(query, text_k[:, cols]) + text_bias)
            values.append(text_v[:, cols])
            top = row_reduce(jnp.maximum, jnp.max, scores)
            probs = [jnp.exp2((s - top) * scale) for s in scores]
            denom = row_reduce(jnp.add, jnp.sum, probs)
            acc = sum(dot_nn(p.astype(jnp.bfloat16), v) for p, v in zip(probs, values))
            valid = slot < table[TABLE_COUNTS + c]
            out[pl.ds(c * tok, tok), cols] = jnp.where(valid, acc / denom, 0.0).astype(out.dtype)


def video_call(first, heads, table, q, k, v, near, text_k, text_v, carried):
    rows, width = q.shape
    text = text_k.shape[0]
    tok = rows // 2
    step = STEP_HEADS * HD
    base = first // STEP_HEADS
    whole = lambda h: (0, base + h)
    part = lambda h: (0, h)
    own_spec = pl.BlockSpec((rows, step), whole)
    part_spec = pl.BlockSpec((2 * rows + PAD_ROWS, step), part)
    text_spec = pl.BlockSpec((text, step), whole)
    in_specs = [pl.BlockSpec(memory_space=pltpu.SMEM), own_spec, own_spec, own_spec]
    in_specs += [part_spec] * 2
    in_specs += [pl.BlockSpec((rows + PAD_ROWS, step), part), pl.BlockSpec((rows, step), part)]
    in_specs += [own_spec] * 2 + [text_spec] * 2
    operands = [table, q, k, v, *near, text_k, text_v]
    aliases = {}
    if carried is not None:
        aliases = {len(operands): 0}
        operands.append(carried)
        in_specs.append(pl.BlockSpec(memory_space=pl.ANY))
    cells = 2 * BLOCKS + 1
    keys = 7 * tok + text
    return pl.pallas_call(
        video_kernel,
        grid=(heads // STEP_HEADS,),
        in_specs=in_specs,
        out_specs=own_spec,
        out_shape=jax.ShapeDtypeStruct((rows, width), q.dtype),
        scratch_shapes=[
            pltpu.VMEM((STEP_HEADS, cells * tok, HD), q.dtype),
            pltpu.VMEM((STEP_HEADS, cells * tok, HD), q.dtype),
            pltpu.VMEM((cells, 8, tok), jnp.float32),
        ],
        input_output_aliases=aliases,
        compiler_params=pltpu.CompilerParams(vmem_limit_bytes=VMEM_BYTES),
        cost_estimate=pl.CostEstimate(
            flops=heads * rows * keys * HD // 4,
            bytes_accessed=heads * rows * HD,
            transcendentals=0,
        ),
        name="video_attention",
    )(*operands)


STAT_SUMS = 32
PAIR_HEADS = HEADS // 2


def text_kernel(order, counts, q, k, v, k_beside, v_beside, keep, send, top, denom):
    step = pl.program_id(0)
    rows = k.shape[0]
    text = q.shape[0]
    half = text // 2
    places = order.shape[0] - 1
    share = text // places
    lane = lax.broadcasted_iota(jnp.int32, (text, HD), 1)

    @pl.when(step == 0)
    def _():
        top[...] = jnp.zeros_like(top)
        denom[...] = jnp.zeros_like(denom)

    @pl.when(step < PAIR_HEADS // STEP_HEADS)
    def _():
        slot = lax.broadcasted_iota(jnp.int32, (1, rows // 2), 1)
        bias = [
            jnp.concatenate(
                [jnp.where(slot < counts[at + c], 0.0, -jnp.inf) for c in range(2)], axis=1
            )
            for at in (0, 2)
        ]
        for i in range(STEP_HEADS):
            cols = pl.ds(i * HD, HD)
            head = step * STEP_HEADS + i
            query = jnp.concatenate(
                [
                    q[pl.ds(pl.multiple_of(order[j] * share, share), share), cols]
                    for j in range(places)
                ],
                axis=0,
            )
            scores = [
                dot_nt(query, keys[:, cols]) * (1.0 / math.sqrt(HD)) + bound
                for keys, bound in zip((k, k_beside), bias)
            ]
            m = row_reduce(jnp.maximum, jnp.max, scores)
            weights = [jnp.exp(s - m) for s in scores]
            l = row_reduce(jnp.add, jnp.sum, weights)
            acc = 0.0
            for w, values in zip(weights, (v, v_beside)):
                high = w.astype(jnp.bfloat16)
                low = (w - high.astype(jnp.float32)).astype(jnp.bfloat16)
                acc = acc + dot_nn(high, values[:, cols]) + dot_nn(low, values[:, cols])
            top[...] = jnp.where(lane == head, m, top[...])
            denom[...] = jnp.where(lane == head + STAT_SUMS, l, denom[...])
            keep[:, cols] = acc[:half]
            send[:, cols] = acc[half:]

    @pl.when(step == PAIR_HEADS // STEP_HEADS)
    def _():
        stats = top[...] + denom[...]
        keep[:, pl.ds(0, HD)] = stats[:half]
        send[:, pl.ds(0, HD)] = stats[half:]


def text_local(order, counts, q, k, v, k_beside, v_beside):
    text = q.shape[0]
    rows = k.shape[0]
    step = STEP_HEADS * HD
    last = PAIR_HEADS // STEP_HEADS - 1
    at = lambda h, order, counts: (0, order[order.shape[0] - 1] + jnp.minimum(h, last))
    k_spec = pl.BlockSpec((rows, step), at)
    out_spec = pl.BlockSpec((text // 2, step), lambda h, order, counts: (0, h))
    shape = jax.ShapeDtypeStruct((text // 2, PAIR_HEADS * HD + step), jnp.float32)
    return pl.pallas_call(
        text_kernel,
        grid_spec=pltpu.PrefetchScalarGridSpec(
            num_scalar_prefetch=2,
            grid=(last + 2,),
            in_specs=[pl.BlockSpec((text, step), at)] + [k_spec] * 4,
            out_specs=[out_spec, out_spec],
            scratch_shapes=[pltpu.VMEM((text, HD), jnp.float32)] * 2,
        ),
        out_shape=[shape, shape],
        compiler_params=pltpu.CompilerParams(vmem_limit_bytes=VMEM_BYTES),
        cost_estimate=pl.CostEstimate(
            flops=text * rows * HD, bytes_accessed=text * HEADS * HD, transcendentals=0
        ),
        name="text_partials",
    )(order, counts, q, k, v, k_beside, v_beside)


def merge_kernel(finish, *refs):
    width = PAIR_HEADS * HD
    stat_cols = pl.ds(width, HD)
    keep, got = refs[:2]
    mine = keep[:, stat_cols]
    theirs = got[:, stat_cols]
    lane = lax.broadcasted_iota(jnp.int32, mine.shape, 1)
    is_top = lane < STAT_SUMS
    top = jnp.maximum(mine, theirs)
    a = jnp.exp(jnp.where(is_top, mine - top, 0.0))
    b = jnp.exp(jnp.where(is_top, theirs - top, 0.0))
    first, second = refs[-2:]
    half = first.shape[0]
    stats = jnp.where(is_top, top, 0.0)
    if finish:
        limits = refs[2]
        row = lax.broadcasted_iota(jnp.int32, (2 * half, 1), 0)
        valid = row < jnp.where(row < half, limits[0], limits[1] + half)
    for h in range(PAIR_HEADS):
        cols = pl.ds(h * HD, HD)
        at = slice(h, h + 1)
        to = slice(STAT_SUMS + h, STAT_SUMS + h + 1)
        total = mine[:, to] * a[:, at] + theirs[:, to] * b[:, at]
        acc = keep[:, cols] * a[:, at] + got[:, cols] * b[:, at]
        if finish:
            acc = jnp.where(valid, acc / total, 0.0)
        else:
            stats = jnp.where(lane == STAT_SUMS + h, total, stats)
        first[:, cols] = acc[:half].astype(first.dtype)
        second[:, cols] = acc[half:].astype(second.dtype)
    if not finish:
        first[:, stat_cols] = stats[:half]
        second[:, stat_cols] = stats[half:]


def text_merge(keep, got):
    shape = jax.ShapeDtypeStruct((keep.shape[0] // 2, (PAIR_HEADS + 1) * HD), jnp.float32)
    return pl.pallas_call(
        functools.partial(merge_kernel, False),
        out_shape=[shape, shape],
        compiler_params=pltpu.CompilerParams(vmem_limit_bytes=VMEM_BYTES),
        name="text_merge",
    )(keep, got)


def text_finish(keep, got, limits):
    shape = jax.ShapeDtypeStruct((keep.shape[0] // 2, PAIR_HEADS * HD), jnp.bfloat16)
    vmem = pl.BlockSpec(memory_space=pltpu.VMEM)
    return pl.pallas_call(
        functools.partial(merge_kernel, True),
        in_specs=[vmem, vmem, pl.BlockSpec(memory_space=pltpu.SMEM)],
        out_shape=[shape, shape],
        compiler_params=pltpu.CompilerParams(vmem_limit_bytes=VMEM_BYTES),
        name="text_finish",
    )(keep, got, limits)


def text_order(n, position):
    bits = n.bit_length() - 1
    masks = [1 << b for b in (*range(1, bits), 0)]
    owners = [
        sum(mask for j, mask in enumerate(masks) if i >> (bits - 1 - j) & 1) for i in range(n)
    ]
    order = jnp.array(owners, jnp.int32) ^ position
    first = position % 2 * (PAIR_HEADS // STEP_HEADS)
    return jnp.concatenate([order, first[None]])


def text_plain(position, n, text_count, q, k, v, counts):
    text, width = q.shape
    share = text // n
    keys = k.reshape(-1, HEADS, HD)
    values = v.reshape(-1, HEADS, HD)
    slots = jnp.arange(k.shape[0] // counts.shape[0], dtype=jnp.int32)
    valid = (slots[None, :] < counts[:, None]).reshape(-1)
    scores = jnp.einsum(
        "qhd,khd->hqk", q.reshape(text, HEADS, HD), keys, preferred_element_type=jnp.float32
    ) * (1.0 / math.sqrt(HD))
    scores = jnp.where(valid[None, None, :], scores, -jnp.inf)
    top = lax.pmax(jnp.max(scores, axis=-1), "tiles")
    weights = jnp.exp(scores - top[..., None])
    denom = jnp.sum(weights, axis=-1).T
    numer = jnp.einsum(
        "hqk,khd->qhd", weights.astype(jnp.bfloat16), values, preferred_element_type=jnp.float32
    ).reshape(text, width)
    numer = lax.psum_scatter(numer, "tiles", scatter_dimension=0, tiled=True)
    denom = lax.psum_scatter(denom, "tiles", scatter_dimension=0, tiled=True)
    result = numer.reshape(share, HEADS, HD) / denom[:, :, None]
    row_ids = position * share + jnp.arange(share, dtype=jnp.int32)
    result = jnp.where((row_ids < text_count[0])[:, None, None], result, 0.0)
    return result.astype(jnp.bfloat16).reshape(share, width)


def make_table(window, counts, counts_beside, text_count, choices, position):
    columns = counts.shape[0]
    extra = (window % 3 != 0) | (window == 0)
    rank = jnp.cumsum(extra.astype(jnp.int32), axis=1) * extra
    codes = jnp.stack([jnp.sum(jnp.where(rank == j, window, 0), axis=1) for j in (1, 2)], axis=1)
    cells = codes + (codes >= 1)
    own = jnp.arange(columns, dtype=jnp.int32)[:, None]
    column = own + cells % 3 - 1
    inside = (column >= 0) & (column < columns)
    extra_cells = jnp.where(inside, column * BLOCKS + cells // 3, columns * BLOCKS)
    chosen = lax.dynamic_index_in_dim(jnp.array(choices, jnp.int32), position, 0, False)
    parts = [extra_cells.reshape(-1), counts, counts_beside, text_count, chosen]
    return jnp.concatenate([part.astype(jnp.int32) for part in parts])


def tie(value, *others):
    return lax.optimization_barrier((value, *others))[0]


def per_device(n, video_q, video_k, video_v, text_q, text_k, text_v, window, counts, text_count):
    rows, width = video_q.shape
    text = text_q.shape[0]
    position = lax.axis_index("tiles").astype(jnp.int32)
    pairs, relays_later, choices = plan_moves(n)
    sends_later = jnp.array(relays_later, jnp.int32)[position] == 1

    limits = jnp.concatenate([counts, jnp.zeros((PAD_ROWS - counts.shape[0],), jnp.int32)])
    limits = jnp.broadcast_to(limits.astype(jnp.bfloat16)[:, None], (PAD_ROWS, width))

    def pack(cols):
        return jnp.concatenate([video_k[:, cols], limits[:, cols], video_v[:, cols]], axis=0)

    starts = [sum(CHUNK_HEADS[:i]) for i in range(len(CHUNK_HEADS))]
    direct, outs = [], []

    def send(i, *before):
        cols = slice(starts[i] * HD, (starts[i] + CHUNK_HEADS[i]) * HD)
        mine = tie(pack(cols), *before)
        direct.append([lax.ppermute(mine, "tiles", pairs[x]) for x in ("earlier", "later")])

    send(0)
    beside = [
        lax.ppermute(x, "tiles", pairs["beside"]) for x in (counts, video_k, video_v)
    ]
    send(1, *beside)
    table = make_table(window, counts, beside[0], text_count, choices, position)
    halving = text % (PAD_ROWS * n) == 0 and n & (n - 1) == 0
    stages = n.bit_length() - 1
    parts = []
    if halving:
        order = text_order(n, position)
        both = jnp.concatenate([counts, beside[0]])
        parts.append(text_local(order, both, text_q, video_k, video_v, *beside[1:]))

    def exchanged(i):
        return lax.ppermute(parts[i][1], "tiles", [(d, d ^ (2 << i)) for d in range(n)])

    def merge(*before):
        i = len(parts) - 1
        if 0 <= i < stages - 2:
            parts.append(text_merge(tie(parts[i][0], *before), exchanged(i)))
        elif i == stages - 2:
            share = text // n
            limits = [text_count - place * share for place in (position, position ^ 1)]
            limits = jnp.concatenate(limits)
            parts.append(text_finish(tie(parts[i][0], *before), exchanged(i), limits))

    merge()
    count = len(CHUNK_HEADS)
    for i in range(count):
        up, down = direct[i]
        before = [parts[-1][0]] if halving and i == 0 else outs[-1:]
        up, down = tie(up, *before), tie(down, *before)
        relays = [
            lax.ppermute(jnp.where(sends_later, down[half], up[half]), "tiles", pairs["relayed"])
            for half in (slice(0, rows + PAD_ROWS), slice(rows + PAD_ROWS, None))
        ]
        if i + 2 < count:
            send(i + 2, *direct[i])
        if i:
            merge(*relays)
        outs.append(
            video_call(
                starts[i], CHUNK_HEADS[i], table, video_q, video_k, video_v,
                [*direct[i], *relays, *beside[1:]], text_k, text_v, outs[-1] if outs else None,
            )
        )
    if halving:
        mine, leave = parts[-1]
        got = lax.ppermute(leave, "tiles", [(d, d ^ 1) for d in range(n)])
        low, high = jnp.concatenate([mine, got], axis=1), jnp.concatenate([got, mine], axis=1)
        text_out = jnp.where(position % 2 == 0, low, high)
    if not halving:
        text_out = text_plain(position, n, text_count, text_q, video_k, video_v, counts)
    return (outs[-1], text_out)


def solution(mesh):
    tiles = mesh.shape["tiles"]
    return jax.shard_map(
        functools.partial(per_device, tiles),
        mesh=mesh,
        in_specs=(
            P(("groups", "tiles"), None),
            P(("groups", "tiles"), None),
            P(("groups", "tiles"), None),
            P("groups", None),
            P("groups", None),
            P("groups", None),
            P("tiles", None),
            P(("groups", "tiles")),
            P("groups"),
        ),
        out_specs=(P(("groups", "tiles"), None), P(("groups", "tiles"), None)),
        check_vma=False,
    )
```

```python
import functools
import math

import jax
import jax.numpy as jnp
from jax import lax
from jax.experimental import pallas as pl
from jax.experimental.pallas import tpu as pltpu
from jax.sharding import PartitionSpec as P

HEADS = 24
HD = 128
NR = 4
BLOCKS = 5
STEP_HEADS = 2
CHUNK_HEADS = (4, 6, 8, 6)
PAD_ROWS = 16
VMEM_BYTES = 48 * 1024 * 1024
LOG2E = 1.4426950408889634
SOURCES = ("own", "earlier", "later", "relayed", "beside")


def spot_shift(n):
    return n // 2 + NR + NR // 2


def plan_moves(n):
    shift, times = spot_shift(n), n // NR
    last = times - 1

    def at(t, r):
        return (t * NR + r - shift) % n

    moves = {
        "earlier": {at(t - 1, r): at(t, r) for t in range(1, times) for r in range(NR)},
        "later": {at(t + 1, r): at(t, r) for t in range(last) for r in range(NR)},
        "beside": {at(t, r): at(t, r ^ 1) for t in range(times) for r in range(NR)},
    }
    relay_earlier = {at(t + 1, 1): at(t, 2) for t in range(last)}
    relay_later = {at(t - 1, 2): at(t, 1) for t in range(1, times)}
    moves["later"][at(0, 2)] = at(last, 2)
    relay_later[at(last, 2)] = at(0, 1)
    moves["earlier"][at(last, 1)] = at(0, 1)
    relay_earlier[at(0, 1)] = at(last, 2)
    assert not set(relay_earlier) & set(relay_later)
    moves["relayed"] = {**relay_earlier, **relay_later}
    held = {"own": {d: d for d in range(n)}}
    for name in ("earlier", "later", "beside"):
        held[name] = {dst: src for src, dst in moves[name].items()}
    held["relayed"] = {dst: held["earlier"].get(src) for src, dst in relay_earlier.items()}
    held["relayed"].update({dst: held["later"].get(src) for src, dst in relay_later.items()})
    choice = []
    for device in range(n):
        spot = (device + shift) % n
        t, r = spot // NR, spot % NR
        row = []
        for dt, dr in ((-1, 0), (1, 0), (0, -1), (0, 1)):
            found = -1
            if 0 <= t + dt < times and 0 <= r + dr < NR:
                wanted = at(t + dt, r + dr)
                found = [i for i, s in enumerate(SOURCES) if held[s].get(device) == wanted][0]
            row.append(found)
        choice.append(row)
    for move in moves.values():
        assert len(set(move.values())) == len(move)
    pairs = {name: sorted(move.items()) for name, move in moves.items()}
    return pairs, [int(d in relay_later) for d in range(n)], choice


def pack_kernel(start, counts, k, v, out, limits, sems):
    rows, width = k.shape[0], out.shape[1]
    cols = pl.ds(start, width)
    copies = [
        pltpu.make_async_copy(k.at[:, cols], out.at[pl.ds(0, rows)], sems.at[0]),
        pltpu.make_async_copy(v.at[:, cols], out.at[pl.ds(rows + PAD_ROWS, rows)], sems.at[1]),
        pltpu.make_async_copy(limits, out.at[pl.ds(rows, PAD_ROWS)], sems.at[2]),
    ]
    copies[0].start()
    copies[1].start()
    row = lax.broadcasted_iota(jnp.int32, limits.shape, 0)
    value = jnp.where(row == 0, counts[0], jnp.where(row == 1, counts[1], 0))
    limits[...] = value.astype(jnp.float32).astype(limits.dtype)
    copies[2].start()
    for copy in copies:
        copy.wait()


def pack(start, width, counts, k, v):
    rows = k.shape[0]
    anywhere = pl.BlockSpec(memory_space=pl.ANY)
    return pl.pallas_call(
        functools.partial(pack_kernel, start),
        in_specs=[pl.BlockSpec(memory_space=pltpu.SMEM), anywhere, anywhere],
        out_specs=anywhere,
        out_shape=jax.ShapeDtypeStruct((2 * rows + PAD_ROWS, width), k.dtype),
        scratch_shapes=[pltpu.VMEM((PAD_ROWS, width), k.dtype), pltpu.SemaphoreType.DMA((3,))],
        compiler_params=pltpu.CompilerParams(vmem_limit_bytes=VMEM_BYTES),
        name="pack_chunk",
    )(counts, k, v)


def choose_kernel(second, a, b, first_out, last_out, sems):
    rows = first_out.shape[0]

    def move(ref):
        copies = [
            pltpu.make_async_copy(ref.at[pl.ds(0, rows)], first_out, sems.at[0]),
            pltpu.make_async_copy(ref.at[pl.ds(rows, last_out.shape[0])], last_out, sems.at[1]),
        ]
        for copy in copies:
            copy.start()
        for copy in copies:
            copy.wait()

    pl.when(second[0] == 0)(lambda: move(a))
    pl.when(second[0] != 0)(lambda: move(b))


def choose(second, a, b, rows):
    anywhere = pl.BlockSpec(memory_space=pl.ANY)
    shapes = [
        jax.ShapeDtypeStruct((part, a.shape[1]), a.dtype) for part in (rows, a.shape[0] - rows)
    ]
    return pl.pallas_call(
        choose_kernel,
        in_specs=[pl.BlockSpec(memory_space=pltpu.SMEM), anywhere, anywhere],
        out_specs=[anywhere, anywhere],
        out_shape=shapes,
        scratch_shapes=[pltpu.SemaphoreType.DMA((2,))],
        compiler_params=pltpu.CompilerParams(vmem_limit_bytes=VMEM_BYTES),
        name="choose_relayed",
    )(second, a, b)


def dot_nt(a, b):
    return lax.dot_general(a, b, (((1,), (1,)), ((), ())), preferred_element_type=jnp.float32)


def dot_nn(a, b):
    return jnp.dot(a, b, preferred_element_type=jnp.float32)


def lane_tiles(x):
    return [x[:, i : i + HD] for i in range(0, x.shape[1], HD)]


def row_reduce(op, final, pieces):
    tiles = [tile for piece in pieces for tile in lane_tiles(piece)]
    return final(functools.reduce(op, tiles), axis=1, keepdims=True)


TABLE_COUNTS, TABLE_BESIDE, TABLE_TEXT, TABLE_CHOICE = 4, 6, 8, 9


def video_kernel(table, q, k_own, v_own, *rest):
    packed = {"earlier": rest[0], "later": rest[1]}
    relayed_k, relayed_v, beside_k, beside_v, text_k, text_v = rest[2:8]
    out, k_all, v_all, bias_all = rest[-4:]
    tok = q.shape[0] // 2
    text = text_k.shape[0]
    scale = LOG2E / math.sqrt(HD)
    near = BLOCKS * tok
    dead = 2 * BLOCKS
    lane = lax.broadcasted_iota(jnp.int32, (8, tok), 1)
    lane_f = lane.astype(jnp.float32)

    def put(block, k, v, v_row):
        for i in range(STEP_HEADS):
            cols = pl.ds(i * HD, HD)
            for c in range(2):
                rows = pl.ds((c * BLOCKS + block) * tok, tok)
                k_all[i, rows, :] = k[pl.ds(c * tok, tok), cols]
                v_all[i, rows, :] = v[pl.ds(v_row + c * tok, tok), cols]

    def put_limits(block, tail):
        limits = tail[...].astype(jnp.float32)
        for c in range(2):
            bias_all[c * BLOCKS + block] = jnp.where(lane_f < limits[c : c + 1, :], 0.0, -jnp.inf)

    def put_counts(block, at):
        for c in range(2):
            bias_all[c * BLOCKS + block] = jnp.where(lane < table[at + c], 0.0, -jnp.inf)

    put(0, k_own, v_own, 0)
    put_counts(0, TABLE_COUNTS)
    tail = (pl.ds(2 * tok, PAD_ROWS), pl.ds(0, HD))
    options = {1: ("earlier",), 2: ("later",), 3: ("earlier",), 4: ("later",)}
    zeros = jnp.zeros((tok, HD), k_all.dtype)
    for block in range(1, BLOCKS):
        chosen = table[TABLE_CHOICE + block - 1]
        for name in options[block]:

            @pl.when(chosen == SOURCES.index(name))
            def _(ref=packed[name], block=block):
                put(block, ref, ref, 2 * tok + PAD_ROWS)
                put_limits(block, ref.at[tail])

        @pl.when(chosen == SOURCES.index("relayed"))
        def _(block=block):
            put(block, relayed_k, relayed_v, 0)
            put_limits(block, relayed_k.at[tail])

        if block > 2:

            @pl.when(chosen == SOURCES.index("beside"))
            def _(block=block):
                put(block, beside_k, beside_v, 0)
                put_counts(block, TABLE_BESIDE)

        @pl.when(chosen < 0)
        def _(block=block):
            for c in range(2):
                bias_all[c * BLOCKS + block] = jnp.full((8, tok), -jnp.inf, jnp.float32)
                for i in range(STEP_HEADS):
                    rows = pl.ds((c * BLOCKS + block) * tok, tok)
                    k_all[i, rows, :] = zeros
                    v_all[i, rows, :] = zeros

    bias_all[dead] = jnp.full((8, tok), -jnp.inf, jnp.float32)
    for i in range(STEP_HEADS):
        k_all[i, pl.ds(dead * tok, tok), :] = zeros
        v_all[i, pl.ds(dead * tok, tok), :] = zeros

    text_lane = lax.broadcasted_iota(jnp.int32, (1, text), 1)
    text_bias = jnp.where(text_lane < table[TABLE_TEXT], 0.0, -jnp.inf)
    slot = lax.broadcasted_iota(jnp.int32, (tok, 1), 0)
    for i in range(STEP_HEADS):
        cols = pl.ds(i * HD, HD)
        for c in range(2):
            query = q[pl.ds(c * tok, tok), cols]
            fixed = pl.ds(c * near, near)
            fixed_bias = jnp.concatenate(
                [bias_all[c * BLOCKS + b][0:1] for b in range(BLOCKS)], axis=1
            )
            scores = [dot_nt(query, k_all[i, fixed, :]) + fixed_bias]
            values = [v_all[i, fixed, :]]
            for j in range(2):
                cell = table[2 * c + j]
                rows = pl.ds(pl.multiple_of(cell * tok, tok), tok)
                scores.append(dot_nt(query, k_all[i, rows, :]) + bias_all[cell][0:1])
                values.append(v_all[i, rows, :])
            scores.append(dot_nt(query, text_k[:, cols]) + text_bias)
            values.append(text_v[:, cols])
            top = row_reduce(jnp.maximum, jnp.max, scores)
            probs = [jnp.exp2((s - top) * scale) for s in scores]
            denom = row_reduce(jnp.add, jnp.sum, probs)
            acc = sum(dot_nn(p.astype(jnp.bfloat16), v) for p, v in zip(probs, values))
            valid = slot < table[TABLE_COUNTS + c]
            out[pl.ds(c * tok, tok), cols] = jnp.where(valid, acc / denom, 0.0).astype(out.dtype)


def video_call(first, heads, table, q, k, v, near, text_k, text_v, carried):
    rows, width = q.shape
    text = text_k.shape[0]
    tok = rows // 2
    step = STEP_HEADS * HD
    base = first // STEP_HEADS
    whole = lambda h: (0, base + h)
    part = lambda h: (0, h)
    own_spec = pl.BlockSpec((rows, step), whole)
    part_spec = pl.BlockSpec((2 * rows + PAD_ROWS, step), part)
    text_spec = pl.BlockSpec((text, step), whole)
    in_specs = [pl.BlockSpec(memory_space=pltpu.SMEM), own_spec, own_spec, own_spec]
    in_specs += [part_spec] * 2
    in_specs += [pl.BlockSpec((rows + PAD_ROWS, step), part), pl.BlockSpec((rows, step), part)]
    in_specs += [own_spec] * 2 + [text_spec] * 2
    operands = [table, q, k, v, *near, text_k, text_v]
    aliases = {}
    if carried is not None:
        aliases = {len(operands): 0}
        operands.append(carried)
        in_specs.append(pl.BlockSpec(memory_space=pl.ANY))
    cells = 2 * BLOCKS + 1
    keys = 7 * tok + text
    return pl.pallas_call(
        video_kernel,
        grid=(heads // STEP_HEADS,),
        in_specs=in_specs,
        out_specs=own_spec,
        out_shape=jax.ShapeDtypeStruct((rows, width), q.dtype),
        scratch_shapes=[
            pltpu.VMEM((STEP_HEADS, cells * tok, HD), q.dtype),
            pltpu.VMEM((STEP_HEADS, cells * tok, HD), q.dtype),
            pltpu.VMEM((cells, 8, tok), jnp.float32),
        ],
        input_output_aliases=aliases,
        compiler_params=pltpu.CompilerParams(vmem_limit_bytes=VMEM_BYTES),
        cost_estimate=pl.CostEstimate(
            flops=heads * rows * keys * HD // 4,
            bytes_accessed=heads * rows * HD,
            transcendentals=0,
        ),
        name="video_attention",
    )(*operands)


STAT_SUMS = 32
PAIR_HEADS = HEADS // 2


def text_kernel(order, counts, q, k, v, k_beside, v_beside, keep, send, top, denom):
    step = pl.program_id(0)
    rows = k.shape[0]
    text = q.shape[0]
    half = text // 2
    places = order.shape[0] - 1
    share = text // places
    lane = lax.broadcasted_iota(jnp.int32, (text, HD), 1)

    @pl.when(step == 0)
    def _():
        top[...] = jnp.zeros_like(top)
        denom[...] = jnp.zeros_like(denom)

    @pl.when(step < PAIR_HEADS // STEP_HEADS)
    def _():
        slot = lax.broadcasted_iota(jnp.int32, (1, rows // 2), 1)
        bias = [
            jnp.concatenate(
                [jnp.where(slot < counts[at + c], 0.0, -jnp.inf) for c in range(2)], axis=1
            )
            for at in (0, 2)
        ]
        for i in range(STEP_HEADS):
            cols = pl.ds(i * HD, HD)
            head = step * STEP_HEADS + i
            query = jnp.concatenate(
                [
                    q[pl.ds(pl.multiple_of(order[j] * share, share), share), cols]
                    for j in range(places)
                ],
                axis=0,
            )
            scores = [
                dot_nt(query, keys[:, cols]) * (1.0 / math.sqrt(HD)) + bound
                for keys, bound in zip((k, k_beside), bias)
            ]
            m = row_reduce(jnp.maximum, jnp.max, scores)
            weights = [jnp.exp(s - m) for s in scores]
            l = row_reduce(jnp.add, jnp.sum, weights)
            acc = 0.0
            for w, values in zip(weights, (v, v_beside)):
                high = w.astype(jnp.bfloat16)
                low = (w - high.astype(jnp.float32)).astype(jnp.bfloat16)
                acc = acc + dot_nn(high, values[:, cols]) + dot_nn(low, values[:, cols])
            top[...] = jnp.where(lane == head, m, top[...])
            denom[...] = jnp.where(lane == head + STAT_SUMS, l, denom[...])
            keep[:, cols] = acc[:half]
            send[:, cols] = acc[half:]

    @pl.when(step == PAIR_HEADS // STEP_HEADS)
    def _():
        stats = top[...] + denom[...]
        keep[:, pl.ds(0, HD)] = stats[:half]
        send[:, pl.ds(0, HD)] = stats[half:]


def text_local(order, counts, q, k, v, k_beside, v_beside):
    text = q.shape[0]
    rows = k.shape[0]
    step = STEP_HEADS * HD
    last = PAIR_HEADS // STEP_HEADS - 1
    at = lambda h, order, counts: (0, order[order.shape[0] - 1] + jnp.minimum(h, last))
    k_spec = pl.BlockSpec((rows, step), at)
    out_spec = pl.BlockSpec((text // 2, step), lambda h, order, counts: (0, h))
    shape = jax.ShapeDtypeStruct((text // 2, PAIR_HEADS * HD + step), jnp.float32)
    return pl.pallas_call(
        text_kernel,
        grid_spec=pltpu.PrefetchScalarGridSpec(
            num_scalar_prefetch=2,
            grid=(last + 2,),
            in_specs=[pl.BlockSpec((text, step), at)] + [k_spec] * 4,
            out_specs=[out_spec, out_spec],
            scratch_shapes=[pltpu.VMEM((text, HD), jnp.float32)] * 2,
        ),
        out_shape=[shape, shape],
        compiler_params=pltpu.CompilerParams(vmem_limit_bytes=VMEM_BYTES),
        cost_estimate=pl.CostEstimate(
            flops=text * rows * HD, bytes_accessed=text * HEADS * HD, transcendentals=0
        ),
        name="text_partials",
    )(order, counts, q, k, v, k_beside, v_beside)


def merge_kernel(finish, *refs):
    width = PAIR_HEADS * HD
    stat_cols = pl.ds(width, HD)
    keep, got = refs[:2]
    mine = keep[:, stat_cols]
    theirs = got[:, stat_cols]
    lane = lax.broadcasted_iota(jnp.int32, mine.shape, 1)
    is_top = lane < STAT_SUMS
    top = jnp.maximum(mine, theirs)
    a = jnp.exp(jnp.where(is_top, mine - top, 0.0))
    b = jnp.exp(jnp.where(is_top, theirs - top, 0.0))
    first, second = refs[-2:]
    half = first.shape[0]
    stats = jnp.where(is_top, top, 0.0)
    if finish:
        limits = refs[2]
        row = lax.broadcasted_iota(jnp.int32, (2 * half, 1), 0)
        valid = row < jnp.where(row < half, limits[0], limits[1] + half)
    for h in range(PAIR_HEADS):
        cols = pl.ds(h * HD, HD)
        at = slice(h, h + 1)
        to = slice(STAT_SUMS + h, STAT_SUMS + h + 1)
        total = mine[:, to] * a[:, at] + theirs[:, to] * b[:, at]
        acc = keep[:, cols] * a[:, at] + got[:, cols] * b[:, at]
        if finish:
            acc = jnp.where(valid, acc / total, 0.0)
        else:
            stats = jnp.where(lane == STAT_SUMS + h, total, stats)
        first[:, cols] = acc[:half].astype(first.dtype)
        second[:, cols] = acc[half:].astype(second.dtype)
    if not finish:
        first[:, stat_cols] = stats[:half]
        second[:, stat_cols] = stats[half:]


def text_merge(keep, got):
    shape = jax.ShapeDtypeStruct((keep.shape[0] // 2, (PAIR_HEADS + 1) * HD), jnp.float32)
    return pl.pallas_call(
        functools.partial(merge_kernel, False),
        out_shape=[shape, shape],
        compiler_params=pltpu.CompilerParams(vmem_limit_bytes=VMEM_BYTES),
        name="text_merge",
    )(keep, got)


def text_finish(keep, got, limits):
    shape = jax.ShapeDtypeStruct((keep.shape[0] // 2, PAIR_HEADS * HD), jnp.bfloat16)
    vmem = pl.BlockSpec(memory_space=pltpu.VMEM)
    return pl.pallas_call(
        functools.partial(merge_kernel, True),
        in_specs=[vmem, vmem, pl.BlockSpec(memory_space=pltpu.SMEM)],
        out_shape=[shape, shape],
        compiler_params=pltpu.CompilerParams(vmem_limit_bytes=VMEM_BYTES),
        name="text_finish",
    )(keep, got, limits)


def text_order(n, position):
    bits = n.bit_length() - 1
    masks = [1 << b for b in (*range(1, bits), 0)]
    owners = [
        sum(mask for j, mask in enumerate(masks) if i >> (bits - 1 - j) & 1) for i in range(n)
    ]
    order = jnp.array(owners, jnp.int32) ^ position
    first = position % 2 * (PAIR_HEADS // STEP_HEADS)
    return jnp.concatenate([order, first[None]])


def text_plain(position, n, text_count, q, k, v, counts):
    text, width = q.shape
    share = text // n
    keys = k.reshape(-1, HEADS, HD)
    values = v.reshape(-1, HEADS, HD)
    slots = jnp.arange(k.shape[0] // counts.shape[0], dtype=jnp.int32)
    valid = (slots[None, :] < counts[:, None]).reshape(-1)
    scores = jnp.einsum(
        "qhd,khd->hqk", q.reshape(text, HEADS, HD), keys, preferred_element_type=jnp.float32
    ) * (1.0 / math.sqrt(HD))
    scores = jnp.where(valid[None, None, :], scores, -jnp.inf)
    top = lax.pmax(jnp.max(scores, axis=-1), "tiles")
    weights = jnp.exp(scores - top[..., None])
    denom = jnp.sum(weights, axis=-1).T
    numer = jnp.einsum(
        "hqk,khd->qhd", weights.astype(jnp.bfloat16), values, preferred_element_type=jnp.float32
    ).reshape(text, width)
    numer = lax.psum_scatter(numer, "tiles", scatter_dimension=0, tiled=True)
    denom = lax.psum_scatter(denom, "tiles", scatter_dimension=0, tiled=True)
    result = numer.reshape(share, HEADS, HD) / denom[:, :, None]
    row_ids = position * share + jnp.arange(share, dtype=jnp.int32)
    result = jnp.where((row_ids < text_count[0])[:, None, None], result, 0.0)
    return result.astype(jnp.bfloat16).reshape(share, width)


def make_table(window, counts, counts_beside, text_count, choices, position):
    columns = counts.shape[0]
    extra = (window % 3 != 0) | (window == 0)
    rank = jnp.cumsum(extra.astype(jnp.int32), axis=1) * extra
    codes = jnp.stack([jnp.sum(jnp.where(rank == j, window, 0), axis=1) for j in (1, 2)], axis=1)
    cells = codes + (codes >= 1)
    own = jnp.arange(columns, dtype=jnp.int32)[:, None]
    column = own + cells % 3 - 1
    inside = (column >= 0) & (column < columns)
    extra_cells = jnp.where(inside, column * BLOCKS + cells // 3, columns * BLOCKS)
    chosen = lax.dynamic_index_in_dim(jnp.array(choices, jnp.int32), position, 0, False)
    parts = [extra_cells.reshape(-1), counts, counts_beside, text_count, chosen]
    return jnp.concatenate([part.astype(jnp.int32) for part in parts])


def tie(value, *others):
    return lax.optimization_barrier((value, *others))[0]


def per_device(n, video_q, video_k, video_v, text_q, text_k, text_v, window, counts, text_count):
    rows, width = video_q.shape
    text = text_q.shape[0]
    position = lax.axis_index("tiles").astype(jnp.int32)
    pairs, relays_later, choices = plan_moves(n)
    sends_later = jnp.array(relays_later, jnp.int32)[position][None]

    starts = [sum(CHUNK_HEADS[:i]) for i in range(len(CHUNK_HEADS))]
    direct, outs = [], []

    def send(i, *before):
        chunk = pack(starts[i] * HD, CHUNK_HEADS[i] * HD, counts, video_k, video_v)
        mine = tie(chunk, *before)
        direct.append([lax.ppermute(mine, "tiles", pairs[x]) for x in ("earlier", "later")])

    send(0)
    beside = [
        lax.ppermute(x, "tiles", pairs["beside"]) for x in (counts, video_k, video_v)
    ]
    send(1, *beside)
    table = make_table(window, counts, beside[0], text_count, choices, position)
    halving = text % (PAD_ROWS * n) == 0 and n & (n - 1) == 0
    stages = n.bit_length() - 1
    parts = []
    if halving:
        order = text_order(n, position)
        both = jnp.concatenate([counts, beside[0]])
        parts.append(text_local(order, both, text_q, video_k, video_v, *beside[1:]))

    def exchanged(i):
        return lax.ppermute(parts[i][1], "tiles", [(d, d ^ (2 << i)) for d in range(n)])

    def merge(*before):
        i = len(parts) - 1
        if 0 <= i < stages - 2:
            parts.append(text_merge(tie(parts[i][0], *before), exchanged(i)))
        elif i == stages - 2:
            share = text // n
            limits = [text_count - place * share for place in (position, position ^ 1)]
            limits = jnp.concatenate(limits)
            parts.append(text_finish(tie(parts[i][0], *before), exchanged(i), limits))

    count = len(CHUNK_HEADS)
    for i in range(count):
        up, down = direct[i]
        before = outs[-1:] + ([parts[-1][0]] if halving else [])
        up, down = tie(up, *before), tie(down, *before)
        relays = [
            lax.ppermute(half, "tiles", pairs["relayed"])
            for half in choose(sends_later, up, down, rows + PAD_ROWS)
        ]
        if i + 2 < count:
            send(i + 2, *direct[i])
        merge(*relays)
        outs.append(
            video_call(
                starts[i], CHUNK_HEADS[i], table, video_q, video_k, video_v,
                [*direct[i], *relays, *beside[1:]], text_k, text_v, outs[-1] if outs else None,
            )
        )
    if halving:
        mine, leave = parts[-1]
        got = lax.ppermute(leave, "tiles", [(d, d ^ 1) for d in range(n)])
        low, high = jnp.concatenate([mine, got], axis=1), jnp.concatenate([got, mine], axis=1)
        text_out = jnp.where(position % 2 == 0, low, high)
    if not halving:
        text_out = text_plain(position, n, text_count, text_q, video_k, video_v, counts)
    return (outs[-1], text_out)


def solution(mesh):
    tiles = mesh.shape["tiles"]
    return jax.shard_map(
        functools.partial(per_device, tiles),
        mesh=mesh,
        in_specs=(
            P(("groups", "tiles"), None),
            P(("groups", "tiles"), None),
            P(("groups", "tiles"), None),
            P("groups", None),
            P("groups", None),
            P("groups", None),
            P("tiles", None),
            P(("groups", "tiles")),
            P("groups"),
        ),
        out_specs=(P(("groups", "tiles"), None), P(("groups", "tiles"), None)),
        check_vma=False,
    )
```

```python
import functools
import math

import jax
import jax.numpy as jnp
from jax import lax
from jax.experimental import pallas as pl
from jax.experimental.pallas import tpu as pltpu
from jax.sharding import PartitionSpec as P

HEADS = 24
HD = 128
NR = 4
BLOCKS = 5
STEP_HEADS = 2
CHUNK_HEADS = (6, 8, 6, 4)
PAD_ROWS = 16
VMEM_BYTES = 48 * 1024 * 1024
LOG2E = 1.4426950408889634
SOURCES = ("own", "earlier", "later", "relayed", "beside")


def spot_shift(n):
    return n // 2 + NR + NR // 2


def plan_moves(n):
    shift, times = spot_shift(n), n // NR
    last = times - 1

    def at(t, r):
        return (t * NR + r - shift) % n

    moves = {
        "earlier": {at(t - 1, r): at(t, r) for t in range(1, times) for r in range(NR)},
        "later": {at(t + 1, r): at(t, r) for t in range(last) for r in range(NR)},
        "beside": {at(t, r): at(t, r ^ 1) for t in range(times) for r in range(NR)},
    }
    relay_earlier = {at(t + 1, 1): at(t, 2) for t in range(last)}
    relay_later = {at(t - 1, 2): at(t, 1) for t in range(1, times)}
    moves["later"][at(0, 2)] = at(last, 2)
    relay_later[at(last, 2)] = at(0, 1)
    moves["earlier"][at(last, 1)] = at(0, 1)
    relay_earlier[at(0, 1)] = at(last, 2)
    assert not set(relay_earlier) & set(relay_later)
    moves["relayed"] = {**relay_earlier, **relay_later}
    held = {"own": {d: d for d in range(n)}}
    for name in ("earlier", "later", "beside"):
        held[name] = {dst: src for src, dst in moves[name].items()}
    held["relayed"] = {dst: held["earlier"].get(src) for src, dst in relay_earlier.items()}
    held["relayed"].update({dst: held["later"].get(src) for src, dst in relay_later.items()})
    choice = []
    for device in range(n):
        spot = (device + shift) % n
        t, r = spot // NR, spot % NR
        row = []
        for dt, dr in ((-1, 0), (1, 0), (0, -1), (0, 1)):
            found = -1
            if 0 <= t + dt < times and 0 <= r + dr < NR:
                wanted = at(t + dt, r + dr)
                found = [i for i, s in enumerate(SOURCES) if held[s].get(device) == wanted][0]
            row.append(found)
        choice.append(row)
    for move in moves.values():
        assert len(set(move.values())) == len(move)
    pairs = {name: sorted(move.items()) for name, move in moves.items()}
    return pairs, [int(d in relay_later) for d in range(n)], choice


def pack_kernel(start, counts, k, v, out, limits, sems):
    rows, width = k.shape[0], out.shape[1]
    cols = pl.ds(start, width)
    copies = [
        pltpu.make_async_copy(k.at[:, cols], out.at[pl.ds(0, rows)], sems.at[0]),
        pltpu.make_async_copy(v.at[:, cols], out.at[pl.ds(rows + PAD_ROWS, rows)], sems.at[1]),
        pltpu.make_async_copy(limits, out.at[pl.ds(rows, PAD_ROWS)], sems.at[2]),
    ]
    copies[0].start()
    copies[1].start()
    row = lax.broadcasted_iota(jnp.int32, limits.shape, 0)
    value = jnp.where(row == 0, counts[0], jnp.where(row == 1, counts[1], 0))
    limits[...] = value.astype(jnp.float32).astype(limits.dtype)
    copies[2].start()
    for copy in copies:
        copy.wait()


def pack(start, width, counts, k, v):
    rows = k.shape[0]
    anywhere = pl.BlockSpec(memory_space=pl.ANY)
    return pl.pallas_call(
        functools.partial(pack_kernel, start),
        in_specs=[pl.BlockSpec(memory_space=pltpu.SMEM), anywhere, anywhere],
        out_specs=anywhere,
        out_shape=jax.ShapeDtypeStruct((2 * rows + PAD_ROWS, width), k.dtype),
        scratch_shapes=[pltpu.VMEM((PAD_ROWS, width), k.dtype), pltpu.SemaphoreType.DMA((3,))],
        compiler_params=pltpu.CompilerParams(vmem_limit_bytes=VMEM_BYTES),
        name="pack_chunk",
    )(counts, k, v)


def choose_kernel(second, a, b, first_out, last_out, sems):
    rows = first_out.shape[0]

    def move(ref):
        copies = [
            pltpu.make_async_copy(ref.at[pl.ds(0, rows)], first_out, sems.at[0]),
            pltpu.make_async_copy(ref.at[pl.ds(rows, last_out.shape[0])], last_out, sems.at[1]),
        ]
        for copy in copies:
            copy.start()
        for copy in copies:
            copy.wait()

    pl.when(second[0] == 0)(lambda: move(a))
    pl.when(second[0] != 0)(lambda: move(b))


def choose(second, a, b, rows):
    anywhere = pl.BlockSpec(memory_space=pl.ANY)
    shapes = [
        jax.ShapeDtypeStruct((part, a.shape[1]), a.dtype) for part in (rows, a.shape[0] - rows)
    ]
    return pl.pallas_call(
        choose_kernel,
        in_specs=[pl.BlockSpec(memory_space=pltpu.SMEM), anywhere, anywhere],
        out_specs=[pl.BlockSpec(memory_space=pltpu.VMEM)] * 2,
        out_shape=shapes,
        scratch_shapes=[pltpu.SemaphoreType.DMA((2,))],
        compiler_params=pltpu.CompilerParams(vmem_limit_bytes=VMEM_BYTES),
        name="choose_relayed",
    )(second, a, b)


def dot_nt(a, b):
    return lax.dot_general(a, b, (((1,), (1,)), ((), ())), preferred_element_type=jnp.float32)


def dot_nn(a, b):
    return jnp.dot(a, b, preferred_element_type=jnp.float32)


def lane_tiles(x):
    return [x[:, i : i + HD] for i in range(0, x.shape[1], HD)]


def row_reduce(op, final, pieces):
    tiles = [tile for piece in pieces for tile in lane_tiles(piece)]
    return final(functools.reduce(op, tiles), axis=1, keepdims=True)


TABLE_COUNTS, TABLE_BESIDE, TABLE_TEXT, TABLE_CHOICE = 4, 6, 8, 9


def video_kernel(table, q, k_own, v_own, *rest):
    packed = {"earlier": rest[0], "later": rest[1]}
    relayed_k, relayed_v, beside_k, beside_v, text_k, text_v = rest[2:8]
    out, k_all, v_all, bias_all = rest[-4:]
    tok = q.shape[0] // 2
    text = text_k.shape[0]
    scale = LOG2E / math.sqrt(HD)
    near = BLOCKS * tok
    dead = 2 * BLOCKS
    lane = lax.broadcasted_iota(jnp.int32, (8, tok), 1)
    lane_f = lane.astype(jnp.float32)

    def put(block, k, v, v_row):
        for i in range(STEP_HEADS):
            cols = pl.ds(i * HD, HD)
            for c in range(2):
                rows = pl.ds((c * BLOCKS + block) * tok, tok)
                k_all[i, rows, :] = k[pl.ds(c * tok, tok), cols]
                v_all[i, rows, :] = v[pl.ds(v_row + c * tok, tok), cols]

    def put_limits(block, tail):
        limits = tail[...].astype(jnp.float32)
        for c in range(2):
            bias_all[c * BLOCKS + block] = jnp.where(lane_f < limits[c : c + 1, :], 0.0, -jnp.inf)

    def put_counts(block, at):
        for c in range(2):
            bias_all[c * BLOCKS + block] = jnp.where(lane < table[at + c], 0.0, -jnp.inf)

    put(0, k_own, v_own, 0)
    put_counts(0, TABLE_COUNTS)
    tail = (pl.ds(2 * tok, PAD_ROWS), pl.ds(0, HD))
    options = {1: ("earlier",), 2: ("later",), 3: ("earlier",), 4: ("later",)}
    zeros = jnp.zeros((tok, HD), k_all.dtype)
    for block in range(1, BLOCKS):
        chosen = table[TABLE_CHOICE + block - 1]
        for name in options[block]:

            @pl.when(chosen == SOURCES.index(name))
            def _(ref=packed[name], block=block):
                put(block, ref, ref, 2 * tok + PAD_ROWS)
                put_limits(block, ref.at[tail])

        @pl.when(chosen == SOURCES.index("relayed"))
        def _(block=block):
            put(block, relayed_k, relayed_v, 0)
            put_limits(block, relayed_k.at[tail])

        if block > 2:

            @pl.when(chosen == SOURCES.index("beside"))
            def _(block=block):
                put(block, beside_k, beside_v, 0)
                put_counts(block, TABLE_BESIDE)

        @pl.when(chosen < 0)
        def _(block=block):
            for c in range(2):
                bias_all[c * BLOCKS + block] = jnp.full((8, tok), -jnp.inf, jnp.float32)
                for i in range(STEP_HEADS):
                    rows = pl.ds((c * BLOCKS + block) * tok, tok)
                    k_all[i, rows, :] = zeros
                    v_all[i, rows, :] = zeros

    bias_all[dead] = jnp.full((8, tok), -jnp.inf, jnp.float32)
    for i in range(STEP_HEADS):
        k_all[i, pl.ds(dead * tok, tok), :] = zeros
        v_all[i, pl.ds(dead * tok, tok), :] = zeros

    text_lane = lax.broadcasted_iota(jnp.int32, (1, text), 1)
    text_bias = jnp.where(text_lane < table[TABLE_TEXT], 0.0, -jnp.inf)
    slot = lax.broadcasted_iota(jnp.int32, (tok, 1), 0)
    for i in range(STEP_HEADS):
        cols = pl.ds(i * HD, HD)
        for c in range(2):
            query = q[pl.ds(c * tok, tok), cols]
            fixed = pl.ds(c * near, near)
            fixed_bias = jnp.concatenate(
                [bias_all[c * BLOCKS + b][0:1] for b in range(BLOCKS)], axis=1
            )
            scores = [dot_nt(query, k_all[i, fixed, :]) + fixed_bias]
            values = [v_all[i, fixed, :]]
            for j in range(2):
                cell = table[2 * c + j]
                rows = pl.ds(pl.multiple_of(cell * tok, tok), tok)
                scores.append(dot_nt(query, k_all[i, rows, :]) + bias_all[cell][0:1])
                values.append(v_all[i, rows, :])
            scores.append(dot_nt(query, text_k[:, cols]) + text_bias)
            values.append(text_v[:, cols])
            top = row_reduce(jnp.maximum, jnp.max, scores)
            probs = [jnp.exp2((s - top) * scale) for s in scores]
            denom = row_reduce(jnp.add, jnp.sum, probs)
            acc = sum(dot_nn(p.astype(jnp.bfloat16), v) for p, v in zip(probs, values))
            valid = slot < table[TABLE_COUNTS + c]
            out[pl.ds(c * tok, tok), cols] = jnp.where(valid, acc / denom, 0.0).astype(out.dtype)


def video_call(first, heads, table, q, k, v, near, text_k, text_v, carried):
    rows, width = q.shape
    text = text_k.shape[0]
    tok = rows // 2
    step = STEP_HEADS * HD
    base = first // STEP_HEADS
    whole = lambda h: (0, base + h)
    part = lambda h: (0, h)
    own_spec = pl.BlockSpec((rows, step), whole)
    part_spec = pl.BlockSpec((2 * rows + PAD_ROWS, step), part)
    text_spec = pl.BlockSpec((text, step), whole)
    in_specs = [pl.BlockSpec(memory_space=pltpu.SMEM), own_spec, own_spec, own_spec]
    in_specs += [part_spec] * 2
    in_specs += [pl.BlockSpec((rows + PAD_ROWS, step), part), pl.BlockSpec((rows, step), part)]
    in_specs += [own_spec] * 2 + [text_spec] * 2
    operands = [table, q, k, v, *near, text_k, text_v]
    aliases = {}
    if carried is not None:
        aliases = {len(operands): 0}
        operands.append(carried)
        in_specs.append(pl.BlockSpec(memory_space=pl.ANY))
    cells = 2 * BLOCKS + 1
    keys = 7 * tok + text
    return pl.pallas_call(
        video_kernel,
        grid=(heads // STEP_HEADS,),
        in_specs=in_specs,
        out_specs=own_spec,
        out_shape=jax.ShapeDtypeStruct((rows, width), q.dtype),
        scratch_shapes=[
            pltpu.VMEM((STEP_HEADS, cells * tok, HD), q.dtype),
            pltpu.VMEM((STEP_HEADS, cells * tok, HD), q.dtype),
            pltpu.VMEM((cells, 8, tok), jnp.float32),
        ],
        input_output_aliases=aliases,
        compiler_params=pltpu.CompilerParams(vmem_limit_bytes=VMEM_BYTES),
        cost_estimate=pl.CostEstimate(
            flops=heads * rows * keys * HD // 4,
            bytes_accessed=heads * rows * HD,
            transcendentals=0,
        ),
        name="video_attention",
    )(*operands)


STAT_SUMS = 32
PAIR_HEADS = HEADS // 2


def text_kernel(order, counts, q, k, v, k_beside, v_beside, keep, send, top, denom):
    step = pl.program_id(0)
    rows = k.shape[0]
    text = q.shape[0]
    half = text // 2
    places = order.shape[0] - 1
    share = text // places
    lane = lax.broadcasted_iota(jnp.int32, (text, HD), 1)

    @pl.when(step == 0)
    def _():
        top[...] = jnp.zeros_like(top)
        denom[...] = jnp.zeros_like(denom)

    @pl.when(step < PAIR_HEADS // STEP_HEADS)
    def _():
        slot = lax.broadcasted_iota(jnp.int32, (1, rows // 2), 1)
        bias = [
            jnp.concatenate(
                [jnp.where(slot < counts[at + c], 0.0, -jnp.inf) for c in range(2)], axis=1
            )
            for at in (0, 2)
        ]
        for i in range(STEP_HEADS):
            cols = pl.ds(i * HD, HD)
            head = step * STEP_HEADS + i
            query = jnp.concatenate(
                [
                    q[pl.ds(pl.multiple_of(order[j] * share, share), share), cols]
                    for j in range(places)
                ],
                axis=0,
            )
            scores = [
                dot_nt(query, keys[:, cols]) * (1.0 / math.sqrt(HD)) + bound
                for keys, bound in zip((k, k_beside), bias)
            ]
            m = row_reduce(jnp.maximum, jnp.max, scores)
            weights = [jnp.exp(s - m) for s in scores]
            l = row_reduce(jnp.add, jnp.sum, weights)
            acc = 0.0
            for w, values in zip(weights, (v, v_beside)):
                high = w.astype(jnp.bfloat16)
                low = (w - high.astype(jnp.float32)).astype(jnp.bfloat16)
                acc = acc + dot_nn(high, values[:, cols]) + dot_nn(low, values[:, cols])
            top[...] = jnp.where(lane == head, m, top[...])
            denom[...] = jnp.where(lane == head + STAT_SUMS, l, denom[...])
            keep[:, cols] = acc[:half]
            send[:, cols] = acc[half:]

    @pl.when(step == PAIR_HEADS // STEP_HEADS)
    def _():
        stats = top[...] + denom[...]
        keep[:, pl.ds(0, HD)] = stats[:half]
        send[:, pl.ds(0, HD)] = stats[half:]


def text_local(order, counts, q, k, v, k_beside, v_beside):
    text = q.shape[0]
    rows = k.shape[0]
    step = STEP_HEADS * HD
    last = PAIR_HEADS // STEP_HEADS - 1
    at = lambda h, order, counts: (0, order[order.shape[0] - 1] + jnp.minimum(h, last))
    k_spec = pl.BlockSpec((rows, step), at)
    out_spec = pl.BlockSpec((text // 2, step), lambda h, order, counts: (0, h))
    shape = jax.ShapeDtypeStruct((text // 2, PAIR_HEADS * HD + step), jnp.float32)
    return pl.pallas_call(
        text_kernel,
        grid_spec=pltpu.PrefetchScalarGridSpec(
            num_scalar_prefetch=2,
            grid=(last + 2,),
            in_specs=[pl.BlockSpec((text, step), at)] + [k_spec] * 4,
            out_specs=[out_spec, out_spec],
            scratch_shapes=[pltpu.VMEM((text, HD), jnp.float32)] * 2,
        ),
        out_shape=[shape, shape],
        compiler_params=pltpu.CompilerParams(vmem_limit_bytes=VMEM_BYTES),
        cost_estimate=pl.CostEstimate(
            flops=text * rows * HD, bytes_accessed=text * HEADS * HD, transcendentals=0
        ),
        name="text_partials",
    )(order, counts, q, k, v, k_beside, v_beside)


def merge_kernel(finish, *refs):
    width = PAIR_HEADS * HD
    stat_cols = pl.ds(width, HD)
    keep, got = refs[:2]
    mine = keep[:, stat_cols]
    theirs = got[:, stat_cols]
    lane = lax.broadcasted_iota(jnp.int32, mine.shape, 1)
    is_top = lane < STAT_SUMS
    top = jnp.maximum(mine, theirs)
    a = jnp.exp(jnp.where(is_top, mine - top, 0.0))
    b = jnp.exp(jnp.where(is_top, theirs - top, 0.0))
    first, second = refs[-2:]
    half = first.shape[0]
    stats = jnp.where(is_top, top, 0.0)
    if finish:
        limits = refs[2]
        row = lax.broadcasted_iota(jnp.int32, (2 * half, 1), 0)
        valid = row < jnp.where(row < half, limits[0], limits[1] + half)
    for h in range(PAIR_HEADS):
        cols = pl.ds(h * HD, HD)
        at = slice(h, h + 1)
        to = slice(STAT_SUMS + h, STAT_SUMS + h + 1)
        total = mine[:, to] * a[:, at] + theirs[:, to] * b[:, at]
        acc = keep[:, cols] * a[:, at] + got[:, cols] * b[:, at]
        if finish:
            acc = jnp.where(valid, acc / total, 0.0)
        else:
            stats = jnp.where(lane == STAT_SUMS + h, total, stats)
        first[:, cols] = acc[:half].astype(first.dtype)
        second[:, cols] = acc[half:].astype(second.dtype)
    if not finish:
        first[:, stat_cols] = stats[:half]
        second[:, stat_cols] = stats[half:]


def text_merge(keep, got):
    shape = jax.ShapeDtypeStruct((keep.shape[0] // 2, (PAIR_HEADS + 1) * HD), jnp.float32)
    return pl.pallas_call(
        functools.partial(merge_kernel, False),
        out_shape=[shape, shape],
        compiler_params=pltpu.CompilerParams(vmem_limit_bytes=VMEM_BYTES),
        name="text_merge",
    )(keep, got)


def text_finish(keep, got, limits):
    shape = jax.ShapeDtypeStruct((keep.shape[0] // 2, PAIR_HEADS * HD), jnp.bfloat16)
    vmem = pl.BlockSpec(memory_space=pltpu.VMEM)
    return pl.pallas_call(
        functools.partial(merge_kernel, True),
        in_specs=[vmem, vmem, pl.BlockSpec(memory_space=pltpu.SMEM)],
        out_shape=[shape, shape],
        compiler_params=pltpu.CompilerParams(vmem_limit_bytes=VMEM_BYTES),
        name="text_finish",
    )(keep, got, limits)


def text_order(n, position):
    bits = n.bit_length() - 1
    masks = [1 << b for b in (*range(1, bits), 0)]
    owners = [
        sum(mask for j, mask in enumerate(masks) if i >> (bits - 1 - j) & 1) for i in range(n)
    ]
    order = jnp.array(owners, jnp.int32) ^ position
    first = position % 2 * (PAIR_HEADS // STEP_HEADS)
    return jnp.concatenate([order, first[None]])


def text_plain(position, n, text_count, q, k, v, counts):
    text, width = q.shape
    share = text // n
    keys = k.reshape(-1, HEADS, HD)
    values = v.reshape(-1, HEADS, HD)
    slots = jnp.arange(k.shape[0] // counts.shape[0], dtype=jnp.int32)
    valid = (slots[None, :] < counts[:, None]).reshape(-1)
    scores = jnp.einsum(
        "qhd,khd->hqk", q.reshape(text, HEADS, HD), keys, preferred_element_type=jnp.float32
    ) * (1.0 / math.sqrt(HD))
    scores = jnp.where(valid[None, None, :], scores, -jnp.inf)
    top = lax.pmax(jnp.max(scores, axis=-1), "tiles")
    weights = jnp.exp(scores - top[..., None])
    denom = jnp.sum(weights, axis=-1).T
    numer = jnp.einsum(
        "hqk,khd->qhd", weights.astype(jnp.bfloat16), values, preferred_element_type=jnp.float32
    ).reshape(text, width)
    numer = lax.psum_scatter(numer, "tiles", scatter_dimension=0, tiled=True)
    denom = lax.psum_scatter(denom, "tiles", scatter_dimension=0, tiled=True)
    result = numer.reshape(share, HEADS, HD) / denom[:, :, None]
    row_ids = position * share + jnp.arange(share, dtype=jnp.int32)
    result = jnp.where((row_ids < text_count[0])[:, None, None], result, 0.0)
    return result.astype(jnp.bfloat16).reshape(share, width)


def make_table(window, counts, counts_beside, text_count, choices, position):
    columns = counts.shape[0]
    extra = (window % 3 != 0) | (window == 0)
    rank = jnp.cumsum(extra.astype(jnp.int32), axis=1) * extra
    codes = jnp.stack([jnp.sum(jnp.where(rank == j, window, 0), axis=1) for j in (1, 2)], axis=1)
    cells = codes + (codes >= 1)
    own = jnp.arange(columns, dtype=jnp.int32)[:, None]
    column = own + cells % 3 - 1
    inside = (column >= 0) & (column < columns)
    extra_cells = jnp.where(inside, column * BLOCKS + cells // 3, columns * BLOCKS)
    chosen = lax.dynamic_index_in_dim(jnp.array(choices, jnp.int32), position, 0, False)
    parts = [extra_cells.reshape(-1), counts, counts_beside, text_count, chosen]
    return jnp.concatenate([part.astype(jnp.int32) for part in parts])


def tie(value, *others):
    return lax.optimization_barrier((value, *others))[0]


def per_device(n, video_q, video_k, video_v, text_q, text_k, text_v, window, counts, text_count):
    rows, width = video_q.shape
    text = text_q.shape[0]
    position = lax.axis_index("tiles").astype(jnp.int32)
    pairs, relays_later, choices = plan_moves(n)
    sends_later = jnp.array(relays_later, jnp.int32)[position][None]

    starts = [sum(CHUNK_HEADS[:i]) for i in range(len(CHUNK_HEADS))]
    direct, outs = [], []

    def send(i, *before):
        chunk = pack(starts[i] * HD, CHUNK_HEADS[i] * HD, counts, video_k, video_v)
        mine = tie(chunk, *before)
        direct.append([lax.ppermute(mine, "tiles", pairs[x]) for x in ("earlier", "later")])

    send(0)
    beside = [
        lax.ppermute(x, "tiles", pairs["beside"]) for x in (counts, video_k, video_v)
    ]
    send(1, *beside)
    table = make_table(window, counts, beside[0], text_count, choices, position)
    halving = text % (PAD_ROWS * n) == 0 and n & (n - 1) == 0
    stages = n.bit_length() - 1
    parts = []
    if halving:
        order = text_order(n, position)
        both = jnp.concatenate([counts, beside[0]])
        parts.append(text_local(order, both, text_q, video_k, video_v, *beside[1:]))

    def exchanged(i):
        return lax.ppermute(parts[i][1], "tiles", [(d, d ^ (2 << i)) for d in range(n)])

    def merge(*before):
        i = len(parts) - 1
        if 0 <= i < stages - 2:
            parts.append(text_merge(tie(parts[i][0], *before), exchanged(i)))
        elif i == stages - 2:
            share = text // n
            limits = [text_count - place * share for place in (position, position ^ 1)]
            limits = jnp.concatenate(limits)
            parts.append(text_finish(tie(parts[i][0], *before), exchanged(i), limits))

    count = len(CHUNK_HEADS)
    for i in range(count):
        up, down = direct[i]
        before = outs[-1:] + ([parts[-1][0]] if halving else [])
        up, down = tie(up, *before), tie(down, *before)
        relays = [
            lax.ppermute(half, "tiles", pairs["relayed"])
            for half in choose(sends_later, up, down, rows + PAD_ROWS)
        ]
        if i + 2 < count:
            send(i + 2, *direct[i])
        merge(*relays)
        outs.append(
            video_call(
                starts[i], CHUNK_HEADS[i], table, video_q, video_k, video_v,
                [*direct[i], *relays, *beside[1:]], text_k, text_v, outs[-1] if outs else None,
            )
        )
    if halving:
        mine, leave = parts[-1]
        got = lax.ppermute(leave, "tiles", [(d, d ^ 1) for d in range(n)])
        low, high = jnp.concatenate([mine, got], axis=1), jnp.concatenate([got, mine], axis=1)
        text_out = jnp.where(position % 2 == 0, low, high)
    if not halving:
        text_out = text_plain(position, n, text_count, text_q, video_k, video_v, counts)
    return (outs[-1], text_out)


def solution(mesh):
    tiles = mesh.shape["tiles"]
    return jax.shard_map(
        functools.partial(per_device, tiles),
        mesh=mesh,
        in_specs=(
            P(("groups", "tiles"), None),
            P(("groups", "tiles"), None),
            P(("groups", "tiles"), None),
            P("groups", None),
            P("groups", None),
            P("groups", None),
            P("tiles", None),
            P(("groups", "tiles")),
            P("groups"),
        ),
        out_specs=(P(("groups", "tiles"), None), P(("groups", "tiles"), None)),
        check_vma=False,
    )
```

```python
import functools
import math

import jax
import jax.numpy as jnp
from jax import lax
from jax.experimental import pallas as pl
from jax.experimental.pallas import tpu as pltpu
from jax.sharding import PartitionSpec as P

HEADS = 24
HD = 128
NR = 4
BLOCKS = 5
STEP_HEADS = 2
CHUNK_HEADS = (8, 6, 6, 4)
PAD_ROWS = 16
VMEM_BYTES = 48 * 1024 * 1024
LOG2E = 1.4426950408889634
SOURCES = ("own", "earlier", "later", "relayed", "beside")


def spot_shift(n):
    return n // 2 + NR + NR // 2


def plan_moves(n):
    shift, times = spot_shift(n), n // NR
    last = times - 1

    def at(t, r):
        return (t * NR + r - shift) % n

    moves = {
        "earlier": {at(t - 1, r): at(t, r) for t in range(1, times) for r in range(NR)},
        "later": {at(t + 1, r): at(t, r) for t in range(last) for r in range(NR)},
        "beside": {at(t, r): at(t, r ^ 1) for t in range(times) for r in range(NR)},
    }
    relay_earlier = {at(t + 1, 1): at(t, 2) for t in range(last)}
    relay_later = {at(t - 1, 2): at(t, 1) for t in range(1, times)}
    moves["later"][at(0, 2)] = at(last, 2)
    relay_later[at(last, 2)] = at(0, 1)
    moves["earlier"][at(last, 1)] = at(0, 1)
    relay_earlier[at(0, 1)] = at(last, 2)
    assert not set(relay_earlier) & set(relay_later)
    moves["relayed"] = {**relay_earlier, **relay_later}
    held = {"own": {d: d for d in range(n)}}
    for name in ("earlier", "later", "beside"):
        held[name] = {dst: src for src, dst in moves[name].items()}
    held["relayed"] = {dst: held["earlier"].get(src) for src, dst in relay_earlier.items()}
    held["relayed"].update({dst: held["later"].get(src) for src, dst in relay_later.items()})
    choice = []
    for device in range(n):
        spot = (device + shift) % n
        t, r = spot // NR, spot % NR
        row = []
        for dt, dr in ((-1, 0), (1, 0), (0, -1), (0, 1)):
            found = -1
            if 0 <= t + dt < times and 0 <= r + dr < NR:
                wanted = at(t + dt, r + dr)
                found = [i for i, s in enumerate(SOURCES) if held[s].get(device) == wanted][0]
            row.append(found)
        choice.append(row)
    for move in moves.values():
        assert len(set(move.values())) == len(move)
    pairs = {name: sorted(move.items()) for name, move in moves.items()}
    return pairs, [int(d in relay_later) for d in range(n)], choice


def pack_kernel(start, counts, k, v, out, limits, sems):
    rows, width = k.shape[0], out.shape[1]
    cols = pl.ds(start, width)
    copies = [
        pltpu.make_async_copy(k.at[:, cols], out.at[pl.ds(0, rows)], sems.at[0]),
        pltpu.make_async_copy(v.at[:, cols], out.at[pl.ds(rows + PAD_ROWS, rows)], sems.at[1]),
        pltpu.make_async_copy(limits, out.at[pl.ds(rows, PAD_ROWS)], sems.at[2]),
    ]
    copies[0].start()
    copies[1].start()
    row = lax.broadcasted_iota(jnp.int32, limits.shape, 0)
    value = jnp.where(row == 0, counts[0], jnp.where(row == 1, counts[1], 0))
    limits[...] = value.astype(jnp.float32).astype(limits.dtype)
    copies[2].start()
    for copy in copies:
        copy.wait()


def pack(start, width, counts, k, v):
    rows = k.shape[0]
    anywhere = pl.BlockSpec(memory_space=pl.ANY)
    return pl.pallas_call(
        functools.partial(pack_kernel, start),
        in_specs=[pl.BlockSpec(memory_space=pltpu.SMEM), anywhere, anywhere],
        out_specs=anywhere,
        out_shape=jax.ShapeDtypeStruct((2 * rows + PAD_ROWS, width), k.dtype),
        scratch_shapes=[pltpu.VMEM((PAD_ROWS, width), k.dtype), pltpu.SemaphoreType.DMA((3,))],
        compiler_params=pltpu.CompilerParams(vmem_limit_bytes=VMEM_BYTES),
        name="pack_chunk",
    )(counts, k, v)


def choose_kernel(second, a, b, first_out, last_out, sems):
    rows = first_out.shape[0]

    def move(ref):
        copies = [
            pltpu.make_async_copy(ref.at[pl.ds(0, rows)], first_out, sems.at[0]),
            pltpu.make_async_copy(ref.at[pl.ds(rows, last_out.shape[0])], last_out, sems.at[1]),
        ]
        for copy in copies:
            copy.start()
        for copy in copies:
            copy.wait()

    pl.when(second[0] == 0)(lambda: move(a))
    pl.when(second[0] != 0)(lambda: move(b))


def choose(second, a, b, rows):
    anywhere = pl.BlockSpec(memory_space=pl.ANY)
    shapes = [
        jax.ShapeDtypeStruct((part, a.shape[1]), a.dtype) for part in (rows, a.shape[0] - rows)
    ]
    return pl.pallas_call(
        choose_kernel,
        in_specs=[pl.BlockSpec(memory_space=pltpu.SMEM), anywhere, anywhere],
        out_specs=[pl.BlockSpec(memory_space=pltpu.VMEM)] * 2,
        out_shape=shapes,
        scratch_shapes=[pltpu.SemaphoreType.DMA((2,))],
        compiler_params=pltpu.CompilerParams(vmem_limit_bytes=VMEM_BYTES),
        name="choose_relayed",
    )(second, a, b)


def dot_nt(a, b):
    return lax.dot_general(a, b, (((1,), (1,)), ((), ())), preferred_element_type=jnp.float32)


def dot_nn(a, b):
    return jnp.dot(a, b, preferred_element_type=jnp.float32)


def lane_tiles(x):
    return [x[:, i : i + HD] for i in range(0, x.shape[1], HD)]


def row_reduce(op, final, pieces):
    tiles = [tile for piece in pieces for tile in lane_tiles(piece)]
    return final(functools.reduce(op, tiles), axis=1, keepdims=True)


TABLE_COUNTS, TABLE_BESIDE, TABLE_TEXT, TABLE_CHOICE = 4, 6, 8, 9


def video_kernel(table, q, k_own, v_own, *rest):
    packed = {"earlier": rest[0], "later": rest[1]}
    relayed_k, relayed_v, beside_k, beside_v, text_k, text_v = rest[2:8]
    out, k_all, v_all, bias_all = rest[-4:]
    tok = q.shape[0] // 2
    text = text_k.shape[0]
    scale = LOG2E / math.sqrt(HD)
    near = BLOCKS * tok
    dead = 2 * BLOCKS
    lane = lax.broadcasted_iota(jnp.int32, (8, tok), 1)
    lane_f = lane.astype(jnp.float32)

    def put(block, k, v, v_row):
        for i in range(STEP_HEADS):
            cols = pl.ds(i * HD, HD)
            for c in range(2):
                rows = pl.ds((c * BLOCKS + block) * tok, tok)
                k_all[i, rows, :] = k[pl.ds(c * tok, tok), cols]
                v_all[i, rows, :] = v[pl.ds(v_row + c * tok, tok), cols]

    def put_limits(block, tail):
        limits = tail[...].astype(jnp.float32)
        for c in range(2):
            bias_all[c * BLOCKS + block] = jnp.where(lane_f < limits[c : c + 1, :], 0.0, -jnp.inf)

    def put_counts(block, at):
        for c in range(2):
            bias_all[c * BLOCKS + block] = jnp.where(lane < table[at + c], 0.0, -jnp.inf)

    put(0, k_own, v_own, 0)
    put_counts(0, TABLE_COUNTS)
    tail = (pl.ds(2 * tok, PAD_ROWS), pl.ds(0, HD))
    options = {1: ("earlier",), 2: ("later",), 3: ("earlier",), 4: ("later",)}
    zeros = jnp.zeros((tok, HD), k_all.dtype)
    for block in range(1, BLOCKS):
        chosen = table[TABLE_CHOICE + block - 1]
        for name in options[block]:

            @pl.when(chosen == SOURCES.index(name))
            def _(ref=packed[name], block=block):
                put(block, ref, ref, 2 * tok + PAD_ROWS)
                put_limits(block, ref.at[tail])

        @pl.when(chosen == SOURCES.index("relayed"))
        def _(block=block):
            put(block, relayed_k, relayed_v, 0)
            put_limits(block, relayed_k.at[tail])

        if block > 2:

            @pl.when(chosen == SOURCES.index("beside"))
            def _(block=block):
                put(block, beside_k, beside_v, 0)
                put_counts(block, TABLE_BESIDE)

        @pl.when(chosen < 0)
        def _(block=block):
            for c in range(2):
                bias_all[c * BLOCKS + block] = jnp.full((8, tok), -jnp.inf, jnp.float32)
                for i in range(STEP_HEADS):
                    rows = pl.ds((c * BLOCKS + block) * tok, tok)
                    k_all[i, rows, :] = zeros
                    v_all[i, rows, :] = zeros

    bias_all[dead] = jnp.full((8, tok), -jnp.inf, jnp.float32)
    for i in range(STEP_HEADS):
        k_all[i, pl.ds(dead * tok, tok), :] = zeros
        v_all[i, pl.ds(dead * tok, tok), :] = zeros

    text_lane = lax.broadcasted_iota(jnp.int32, (1, text), 1)
    text_bias = jnp.where(text_lane < table[TABLE_TEXT], 0.0, -jnp.inf)
    slot = lax.broadcasted_iota(jnp.int32, (tok, 1), 0)
    for i in range(STEP_HEADS):
        cols = pl.ds(i * HD, HD)
        for c in range(2):
            query = q[pl.ds(c * tok, tok), cols]
            fixed = pl.ds(c * near, near)
            fixed_bias = jnp.concatenate(
                [bias_all[c * BLOCKS + b][0:1] for b in range(BLOCKS)], axis=1
            )
            scores = [dot_nt(query, k_all[i, fixed, :]) + fixed_bias]
            values = [v_all[i, fixed, :]]
            for j in range(2):
                cell = table[2 * c + j]
                rows = pl.ds(pl.multiple_of(cell * tok, tok), tok)
                scores.append(dot_nt(query, k_all[i, rows, :]) + bias_all[cell][0:1])
                values.append(v_all[i, rows, :])
            scores.append(dot_nt(query, text_k[:, cols]) + text_bias)
            values.append(text_v[:, cols])
            top = row_reduce(jnp.maximum, jnp.max, scores)
            probs = [jnp.exp2((s - top) * scale) for s in scores]
            denom = row_reduce(jnp.add, jnp.sum, probs)
            acc = sum(dot_nn(p.astype(jnp.bfloat16), v) for p, v in zip(probs, values))
            valid = slot < table[TABLE_COUNTS + c]
            out[pl.ds(c * tok, tok), cols] = jnp.where(valid, acc / denom, 0.0).astype(out.dtype)


def video_call(first, heads, table, q, k, v, near, text_k, text_v, carried):
    rows, width = q.shape
    text = text_k.shape[0]
    tok = rows // 2
    step = STEP_HEADS * HD
    base = first // STEP_HEADS
    whole = lambda h: (0, base + h)
    part = lambda h: (0, h)
    own_spec = pl.BlockSpec((rows, step), whole)
    part_spec = pl.BlockSpec((2 * rows + PAD_ROWS, step), part)
    text_spec = pl.BlockSpec((text, step), whole)
    in_specs = [pl.BlockSpec(memory_space=pltpu.SMEM), own_spec, own_spec, own_spec]
    in_specs += [part_spec] * 2
    in_specs += [pl.BlockSpec((rows + PAD_ROWS, step), part), pl.BlockSpec((rows, step), part)]
    in_specs += [own_spec] * 2 + [text_spec] * 2
    operands = [table, q, k, v, *near, text_k, text_v]
    aliases = {}
    if carried is not None:
        aliases = {len(operands): 0}
        operands.append(carried)
        in_specs.append(pl.BlockSpec(memory_space=pl.ANY))
    cells = 2 * BLOCKS + 1
    keys = 7 * tok + text
    return pl.pallas_call(
        video_kernel,
        grid=(heads // STEP_HEADS,),
        in_specs=in_specs,
        out_specs=own_spec,
        out_shape=jax.ShapeDtypeStruct((rows, width), q.dtype),
        scratch_shapes=[
            pltpu.VMEM((STEP_HEADS, cells * tok, HD), q.dtype),
            pltpu.VMEM((STEP_HEADS, cells * tok, HD), q.dtype),
            pltpu.VMEM((cells, 8, tok), jnp.float32),
        ],
        input_output_aliases=aliases,
        compiler_params=pltpu.CompilerParams(vmem_limit_bytes=VMEM_BYTES),
        cost_estimate=pl.CostEstimate(
            flops=heads * rows * keys * HD // 4,
            bytes_accessed=heads * rows * HD,
            transcendentals=0,
        ),
        name="video_attention",
    )(*operands)


STAT_SUMS = 32
PAIR_HEADS = HEADS // 2


def text_kernel(order, counts, q, k, v, k_beside, v_beside, keep, send, top, denom):
    step = pl.program_id(0)
    rows = k.shape[0]
    text = q.shape[0]
    half = text // 2
    places = order.shape[0] - 1
    share = text // places
    lane = lax.broadcasted_iota(jnp.int32, (text, HD), 1)

    @pl.when(step == 0)
    def _():
        top[...] = jnp.zeros_like(top)
        denom[...] = jnp.zeros_like(denom)

    @pl.when(step < PAIR_HEADS // STEP_HEADS)
    def _():
        slot = lax.broadcasted_iota(jnp.int32, (1, rows // 2), 1)
        bias = [
            jnp.concatenate(
                [jnp.where(slot < counts[at + c], 0.0, -jnp.inf) for c in range(2)], axis=1
            )
            for at in (0, 2)
        ]
        for i in range(STEP_HEADS):
            cols = pl.ds(i * HD, HD)
            head = step * STEP_HEADS + i
            query = jnp.concatenate(
                [
                    q[pl.ds(pl.multiple_of(order[j] * share, share), share), cols]
                    for j in range(places)
                ],
                axis=0,
            )
            scores = [
                dot_nt(query, keys[:, cols]) * (1.0 / math.sqrt(HD)) + bound
                for keys, bound in zip((k, k_beside), bias)
            ]
            m = row_reduce(jnp.maximum, jnp.max, scores)
            weights = [jnp.exp(s - m) for s in scores]
            l = row_reduce(jnp.add, jnp.sum, weights)
            acc = 0.0
            for w, values in zip(weights, (v, v_beside)):
                high = w.astype(jnp.bfloat16)
                low = (w - high.astype(jnp.float32)).astype(jnp.bfloat16)
                acc = acc + dot_nn(high, values[:, cols]) + dot_nn(low, values[:, cols])
            top[...] = jnp.where(lane == head, m, top[...])
            denom[...] = jnp.where(lane == head + STAT_SUMS, l, denom[...])
            keep[:, cols] = acc[:half]
            send[:, cols] = acc[half:]

    @pl.when(step == PAIR_HEADS // STEP_HEADS)
    def _():
        stats = top[...] + denom[...]
        keep[:, pl.ds(0, HD)] = stats[:half]
        send[:, pl.ds(0, HD)] = stats[half:]


def text_local(order, counts, q, k, v, k_beside, v_beside):
    text = q.shape[0]
    rows = k.shape[0]
    step = STEP_HEADS * HD
    last = PAIR_HEADS // STEP_HEADS - 1
    at = lambda h, order, counts: (0, order[order.shape[0] - 1] + jnp.minimum(h, last))
    k_spec = pl.BlockSpec((rows, step), at)
    out_spec = pl.BlockSpec((text // 2, step), lambda h, order, counts: (0, h))
    shape = jax.ShapeDtypeStruct((text // 2, PAIR_HEADS * HD + step), jnp.float32)
    return pl.pallas_call(
        text_kernel,
        grid_spec=pltpu.PrefetchScalarGridSpec(
            num_scalar_prefetch=2,
            grid=(last + 2,),
            in_specs=[pl.BlockSpec((text, step), at)] + [k_spec] * 4,
            out_specs=[out_spec, out_spec],
            scratch_shapes=[pltpu.VMEM((text, HD), jnp.float32)] * 2,
        ),
        out_shape=[shape, shape],
        compiler_params=pltpu.CompilerParams(vmem_limit_bytes=VMEM_BYTES),
        cost_estimate=pl.CostEstimate(
            flops=text * rows * HD, bytes_accessed=text * HEADS * HD, transcendentals=0
        ),
        name="text_partials",
    )(order, counts, q, k, v, k_beside, v_beside)


def merge_kernel(finish, *refs):
    width = PAIR_HEADS * HD
    stat_cols = pl.ds(width, HD)
    keep, got = refs[:2]
    mine = keep[:, stat_cols]
    theirs = got[:, stat_cols]
    lane = lax.broadcasted_iota(jnp.int32, mine.shape, 1)
    is_top = lane < STAT_SUMS
    top = jnp.maximum(mine, theirs)
    a = jnp.exp(jnp.where(is_top, mine - top, 0.0))
    b = jnp.exp(jnp.where(is_top, theirs - top, 0.0))
    first, second = refs[-2:]
    half = first.shape[0]
    stats = jnp.where(is_top, top, 0.0)
    if finish:
        limits = refs[2]
        row = lax.broadcasted_iota(jnp.int32, (2 * half, 1), 0)
        valid = row < jnp.where(row < half, limits[0], limits[1] + half)
    for h in range(PAIR_HEADS):
        cols = pl.ds(h * HD, HD)
        at = slice(h, h + 1)
        to = slice(STAT_SUMS + h, STAT_SUMS + h + 1)
        total = mine[:, to] * a[:, at] + theirs[:, to] * b[:, at]
        acc = keep[:, cols] * a[:, at] + got[:, cols] * b[:, at]
        if finish:
            acc = jnp.where(valid, acc / total, 0.0)
        else:
            stats = jnp.where(lane == STAT_SUMS + h, total, stats)
        first[:, cols] = acc[:half].astype(first.dtype)
        second[:, cols] = acc[half:].astype(second.dtype)
    if not finish:
        first[:, stat_cols] = stats[:half]
        second[:, stat_cols] = stats[half:]


def text_merge(keep, got):
    shape = jax.ShapeDtypeStruct((keep.shape[0] // 2, (PAIR_HEADS + 1) * HD), jnp.float32)
    return pl.pallas_call(
        functools.partial(merge_kernel, False),
        out_shape=[shape, shape],
        compiler_params=pltpu.CompilerParams(vmem_limit_bytes=VMEM_BYTES),
        name="text_merge",
    )(keep, got)


def text_finish(keep, got, limits):
    shape = jax.ShapeDtypeStruct((keep.shape[0] // 2, PAIR_HEADS * HD), jnp.bfloat16)
    vmem = pl.BlockSpec(memory_space=pltpu.VMEM)
    return pl.pallas_call(
        functools.partial(merge_kernel, True),
        in_specs=[vmem, vmem, pl.BlockSpec(memory_space=pltpu.SMEM)],
        out_shape=[shape, shape],
        compiler_params=pltpu.CompilerParams(vmem_limit_bytes=VMEM_BYTES),
        name="text_finish",
    )(keep, got, limits)


def text_order(n, position):
    bits = n.bit_length() - 1
    masks = [1 << b for b in (*range(1, bits), 0)]
    owners = [
        sum(mask for j, mask in enumerate(masks) if i >> (bits - 1 - j) & 1) for i in range(n)
    ]
    order = jnp.array(owners, jnp.int32) ^ position
    first = position % 2 * (PAIR_HEADS // STEP_HEADS)
    return jnp.concatenate([order, first[None]])


def text_plain(position, n, text_count, q, k, v, counts):
    text, width = q.shape
    share = text // n
    keys = k.reshape(-1, HEADS, HD)
    values = v.reshape(-1, HEADS, HD)
    slots = jnp.arange(k.shape[0] // counts.shape[0], dtype=jnp.int32)
    valid = (slots[None, :] < counts[:, None]).reshape(-1)
    scores = jnp.einsum(
        "qhd,khd->hqk", q.reshape(text, HEADS, HD), keys, preferred_element_type=jnp.float32
    ) * (1.0 / math.sqrt(HD))
    scores = jnp.where(valid[None, None, :], scores, -jnp.inf)
    top = lax.pmax(jnp.max(scores, axis=-1), "tiles")
    weights = jnp.exp(scores - top[..., None])
    denom = jnp.sum(weights, axis=-1).T
    numer = jnp.einsum(
        "hqk,khd->qhd", weights.astype(jnp.bfloat16), values, preferred_element_type=jnp.float32
    ).reshape(text, width)
    numer = lax.psum_scatter(numer, "tiles", scatter_dimension=0, tiled=True)
    denom = lax.psum_scatter(denom, "tiles", scatter_dimension=0, tiled=True)
    result = numer.reshape(share, HEADS, HD) / denom[:, :, None]
    row_ids = position * share + jnp.arange(share, dtype=jnp.int32)
    result = jnp.where((row_ids < text_count[0])[:, None, None], result, 0.0)
    return result.astype(jnp.bfloat16).reshape(share, width)


def make_table(window, counts, counts_beside, text_count, choices, position):
    columns = counts.shape[0]
    extra = (window % 3 != 0) | (window == 0)
    rank = jnp.cumsum(extra.astype(jnp.int32), axis=1) * extra
    codes = jnp.stack([jnp.sum(jnp.where(rank == j, window, 0), axis=1) for j in (1, 2)], axis=1)
    cells = codes + (codes >= 1)
    own = jnp.arange(columns, dtype=jnp.int32)[:, None]
    column = own + cells % 3 - 1
    inside = (column >= 0) & (column < columns)
    extra_cells = jnp.where(inside, column * BLOCKS + cells // 3, columns * BLOCKS)
    chosen = lax.dynamic_index_in_dim(jnp.array(choices, jnp.int32), position, 0, False)
    parts = [extra_cells.reshape(-1), counts, counts_beside, text_count, chosen]
    return jnp.concatenate([part.astype(jnp.int32) for part in parts])


def tie(value, *others):
    return lax.optimization_barrier((value, *others))[0]


def per_device(n, video_q, video_k, video_v, text_q, text_k, text_v, window, counts, text_count):
    rows, width = video_q.shape
    text = text_q.shape[0]
    position = lax.axis_index("tiles").astype(jnp.int32)
    pairs, relays_later, choices = plan_moves(n)
    sends_later = jnp.array(relays_later, jnp.int32)[position][None]

    starts = [sum(CHUNK_HEADS[:i]) for i in range(len(CHUNK_HEADS))]
    direct, outs = [], []

    def send(i, *before):
        chunk = pack(starts[i] * HD, CHUNK_HEADS[i] * HD, counts, video_k, video_v)
        mine = tie(chunk, *before)
        direct.append([lax.ppermute(mine, "tiles", pairs[x]) for x in ("earlier", "later")])

    send(0)
    beside = [
        lax.ppermute(x, "tiles", pairs["beside"]) for x in (counts, video_k, video_v)
    ]
    table = make_table(window, counts, beside[0], text_count, choices, position)
    halving = text % (PAD_ROWS * n) == 0 and n & (n - 1) == 0
    stages = n.bit_length() - 1
    parts = []
    if halving:
        order = text_order(n, position)
        both = jnp.concatenate([counts, beside[0]])
        parts.append(text_local(order, both, text_q, video_k, video_v, *beside[1:]))

    def exchanged(i):
        return lax.ppermute(parts[i][1], "tiles", [(d, d ^ (2 << i)) for d in range(n)])

    def merge(*before):
        i = len(parts) - 1
        if 0 <= i < stages - 2:
            parts.append(text_merge(tie(parts[i][0], *before), exchanged(i)))
        elif i == stages - 2:
            share = text // n
            limits = [text_count - place * share for place in (position, position ^ 1)]
            limits = jnp.concatenate(limits)
            parts.append(text_finish(tie(parts[i][0], *before), exchanged(i), limits))

    count = len(CHUNK_HEADS)
    for i in range(count):
        before = outs[-1:] + ([parts[-1][0]] if halving else [])
        if i + 1 < count:
            send(i + 1, *direct[i], *before)
        up, down = tie(direct[i][0], *before), tie(direct[i][1], *before)
        relays = [
            lax.ppermute(half, "tiles", pairs["relayed"])
            for half in choose(sends_later, up, down, rows + PAD_ROWS)
        ]
        outs.append(
            video_call(
                starts[i], CHUNK_HEADS[i], table, video_q, video_k, video_v,
                [*direct[i], *relays, *beside[1:]], text_k, text_v, outs[-1] if outs else None,
            )
        )
        if i < 2:
            merge(*relays)
        if i == 1:
            merge(outs[0])
    if halving:
        mine, leave = parts[-1]
        got = lax.ppermute(leave, "tiles", [(d, d ^ 1) for d in range(n)])
        low, high = jnp.concatenate([mine, got], axis=1), jnp.concatenate([got, mine], axis=1)
        text_out = jnp.where(position % 2 == 0, low, high)
    if not halving:
        text_out = text_plain(position, n, text_count, text_q, video_k, video_v, counts)
    return (outs[-1], text_out)


def solution(mesh):
    tiles = mesh.shape["tiles"]
    return jax.shard_map(
        functools.partial(per_device, tiles),
        mesh=mesh,
        in_specs=(
            P(("groups", "tiles"), None),
            P(("groups", "tiles"), None),
            P(("groups", "tiles"), None),
            P("groups", None),
            P("groups", None),
            P("groups", None),
            P("tiles", None),
            P(("groups", "tiles")),
            P("groups"),
        ),
        out_specs=(P(("groups", "tiles"), None), P(("groups", "tiles"), None)),
        check_vma=False,
    )
```

```python
import functools
import math

import jax
import jax.numpy as jnp
from jax import lax
from jax.experimental import pallas as pl
from jax.experimental.pallas import tpu as pltpu
from jax.sharding import PartitionSpec as P

HEADS = 24
HD = 128
NR = 4
BLOCKS = 5
STEP_HEADS = 2
CHUNK_HEADS = (12, 8, 4)
PAD_ROWS = 16
VMEM_BYTES = 48 * 1024 * 1024
LOG2E = 1.4426950408889634
SOURCES = ("own", "earlier", "later", "relayed", "beside")


def spot_shift(n):
    return n // 2 + NR + NR // 2


def plan_moves(n):
    shift, times = spot_shift(n), n // NR
    last = times - 1

    def at(t, r):
        return (t * NR + r - shift) % n

    moves = {
        "earlier": {at(t - 1, r): at(t, r) for t in range(1, times) for r in range(NR)},
        "later": {at(t + 1, r): at(t, r) for t in range(last) for r in range(NR)},
        "beside": {at(t, r): at(t, r ^ 1) for t in range(times) for r in range(NR)},
    }
    relay_earlier = {at(t + 1, 1): at(t, 2) for t in range(last)}
    relay_later = {at(t - 1, 2): at(t, 1) for t in range(1, times)}
    moves["later"][at(0, 2)] = at(last, 2)
    relay_later[at(last, 2)] = at(0, 1)
    moves["earlier"][at(last, 1)] = at(0, 1)
    relay_earlier[at(0, 1)] = at(last, 2)
    assert not set(relay_earlier) & set(relay_later)
    moves["relayed"] = {**relay_earlier, **relay_later}
    held = {"own": {d: d for d in range(n)}}
    for name in ("earlier", "later", "beside"):
        held[name] = {dst: src for src, dst in moves[name].items()}
    held["relayed"] = {dst: held["earlier"].get(src) for src, dst in relay_earlier.items()}
    held["relayed"].update({dst: held["later"].get(src) for src, dst in relay_later.items()})
    choice = []
    for device in range(n):
        spot = (device + shift) % n
        t, r = spot // NR, spot % NR
        row = []
        for dt, dr in ((-1, 0), (1, 0), (0, -1), (0, 1)):
            found = -1
            if 0 <= t + dt < times and 0 <= r + dr < NR:
                wanted = at(t + dt, r + dr)
                found = [i for i, s in enumerate(SOURCES) if held[s].get(device) == wanted][0]
            row.append(found)
        choice.append(row)
    for move in moves.values():
        assert len(set(move.values())) == len(move)
    pairs = {name: sorted(move.items()) for name, move in moves.items()}
    return pairs, [int(d in relay_later) for d in range(n)], choice


def pack_kernel(start, counts, k, v, out, limits, sems):
    rows, width = k.shape[0], out.shape[1]
    cols = pl.ds(start, width)
    copies = [
        pltpu.make_async_copy(k.at[:, cols], out.at[pl.ds(0, rows)], sems.at[0]),
        pltpu.make_async_copy(v.at[:, cols], out.at[pl.ds(rows + PAD_ROWS, rows)], sems.at[1]),
        pltpu.make_async_copy(limits, out.at[pl.ds(rows, PAD_ROWS)], sems.at[2]),
    ]
    copies[0].start()
    copies[1].start()
    row = lax.broadcasted_iota(jnp.int32, limits.shape, 0)
    value = jnp.where(row == 0, counts[0], jnp.where(row == 1, counts[1], 0))
    limits[...] = value.astype(jnp.float32).astype(limits.dtype)
    copies[2].start()
    for copy in copies:
        copy.wait()


def pack(start, width, counts, k, v):
    rows = k.shape[0]
    anywhere = pl.BlockSpec(memory_space=pl.ANY)
    return pl.pallas_call(
        functools.partial(pack_kernel, start),
        in_specs=[pl.BlockSpec(memory_space=pltpu.SMEM), anywhere, anywhere],
        out_specs=anywhere,
        out_shape=jax.ShapeDtypeStruct((2 * rows + PAD_ROWS, width), k.dtype),
        scratch_shapes=[pltpu.VMEM((PAD_ROWS, width), k.dtype), pltpu.SemaphoreType.DMA((3,))],
        compiler_params=pltpu.CompilerParams(vmem_limit_bytes=VMEM_BYTES),
        name="pack_chunk",
    )(counts, k, v)


def choose_kernel(second, a, b, first_out, last_out, sems):
    rows = first_out.shape[0]

    def move(ref):
        copies = [
            pltpu.make_async_copy(ref.at[pl.ds(0, rows)], first_out, sems.at[0]),
            pltpu.make_async_copy(ref.at[pl.ds(rows, last_out.shape[0])], last_out, sems.at[1]),
        ]
        for copy in copies:
            copy.start()
        for copy in copies:
            copy.wait()

    pl.when(second[0] == 0)(lambda: move(a))
    pl.when(second[0] != 0)(lambda: move(b))


def choose(second, a, b, rows):
    anywhere = pl.BlockSpec(memory_space=pl.ANY)
    shapes = [
        jax.ShapeDtypeStruct((part, a.shape[1]), a.dtype) for part in (rows, a.shape[0] - rows)
    ]
    return pl.pallas_call(
        choose_kernel,
        in_specs=[pl.BlockSpec(memory_space=pltpu.SMEM), anywhere, anywhere],
        out_specs=[pl.BlockSpec(memory_space=pltpu.VMEM)] * 2,
        out_shape=shapes,
        scratch_shapes=[pltpu.SemaphoreType.DMA((2,))],
        compiler_params=pltpu.CompilerParams(vmem_limit_bytes=VMEM_BYTES),
        name="choose_relayed",
    )(second, a, b)


def dot_nt(a, b):
    return lax.dot_general(a, b, (((1,), (1,)), ((), ())), preferred_element_type=jnp.float32)


def dot_nn(a, b):
    return jnp.dot(a, b, preferred_element_type=jnp.float32)


def lane_tiles(x):
    return [x[:, i : i + HD] for i in range(0, x.shape[1], HD)]


def row_reduce(op, final, pieces):
    tiles = [tile for piece in pieces for tile in lane_tiles(piece)]
    return final(functools.reduce(op, tiles), axis=1, keepdims=True)


TABLE_COUNTS, TABLE_BESIDE, TABLE_TEXT, TABLE_CHOICE = 4, 6, 8, 9


def video_kernel(table, q, k_own, v_own, *rest):
    packed = {"earlier": rest[0], "later": rest[1]}
    relayed_k, relayed_v, beside_k, beside_v, text_k, text_v = rest[2:8]
    out, k_all, v_all, bias_all = rest[-4:]
    tok = q.shape[0] // 2
    text = text_k.shape[0]
    scale = LOG2E / math.sqrt(HD)
    near = BLOCKS * tok
    dead = 2 * BLOCKS
    lane = lax.broadcasted_iota(jnp.int32, (8, tok), 1)
    lane_f = lane.astype(jnp.float32)

    def put(block, k, v, v_row):
        for i in range(STEP_HEADS):
            cols = pl.ds(i * HD, HD)
            for c in range(2):
                rows = pl.ds((c * BLOCKS + block) * tok, tok)
                k_all[i, rows, :] = k[pl.ds(c * tok, tok), cols]
                v_all[i, rows, :] = v[pl.ds(v_row + c * tok, tok), cols]

    def put_limits(block, tail):
        limits = tail[...].astype(jnp.float32)
        for c in range(2):
            bias_all[c * BLOCKS + block] = jnp.where(lane_f < limits[c : c + 1, :], 0.0, -jnp.inf)

    def put_counts(block, at):
        for c in range(2):
            bias_all[c * BLOCKS + block] = jnp.where(lane < table[at + c], 0.0, -jnp.inf)

    put(0, k_own, v_own, 0)
    put_counts(0, TABLE_COUNTS)
    tail = (pl.ds(2 * tok, PAD_ROWS), pl.ds(0, HD))
    options = {1: ("earlier",), 2: ("later",), 3: ("earlier",), 4: ("later",)}
    zeros = jnp.zeros((tok, HD), k_all.dtype)
    for block in range(1, BLOCKS):
        chosen = table[TABLE_CHOICE + block - 1]
        for name in options[block]:

            @pl.when(chosen == SOURCES.index(name))
            def _(ref=packed[name], block=block):
                put(block, ref, ref, 2 * tok + PAD_ROWS)
                put_limits(block, ref.at[tail])

        @pl.when(chosen == SOURCES.index("relayed"))
        def _(block=block):
            put(block, relayed_k, relayed_v, 0)
            put_limits(block, relayed_k.at[tail])

        if block > 2:

            @pl.when(chosen == SOURCES.index("beside"))
            def _(block=block):
                put(block, beside_k, beside_v, 0)
                put_counts(block, TABLE_BESIDE)

        @pl.when(chosen < 0)
        def _(block=block):
            for c in range(2):
                bias_all[c * BLOCKS + block] = jnp.full((8, tok), -jnp.inf, jnp.float32)
                for i in range(STEP_HEADS):
                    rows = pl.ds((c * BLOCKS + block) * tok, tok)
                    k_all[i, rows, :] = zeros
                    v_all[i, rows, :] = zeros

    bias_all[dead] = jnp.full((8, tok), -jnp.inf, jnp.float32)
    for i in range(STEP_HEADS):
        k_all[i, pl.ds(dead * tok, tok), :] = zeros
        v_all[i, pl.ds(dead * tok, tok), :] = zeros

    text_lane = lax.broadcasted_iota(jnp.int32, (1, text), 1)
    text_bias = jnp.where(text_lane < table[TABLE_TEXT], 0.0, -jnp.inf)
    slot = lax.broadcasted_iota(jnp.int32, (tok, 1), 0)
    for i in range(STEP_HEADS):
        cols = pl.ds(i * HD, HD)
        for c in range(2):
            query = q[pl.ds(c * tok, tok), cols]
            fixed = pl.ds(c * near, near)
            fixed_bias = jnp.concatenate(
                [bias_all[c * BLOCKS + b][0:1] for b in range(BLOCKS)], axis=1
            )
            scores = [dot_nt(query, k_all[i, fixed, :]) + fixed_bias]
            values = [v_all[i, fixed, :]]
            for j in range(2):
                cell = table[2 * c + j]
                rows = pl.ds(pl.multiple_of(cell * tok, tok), tok)
                scores.append(dot_nt(query, k_all[i, rows, :]) + bias_all[cell][0:1])
                values.append(v_all[i, rows, :])
            scores.append(dot_nt(query, text_k[:, cols]) + text_bias)
            values.append(text_v[:, cols])
            top = row_reduce(jnp.maximum, jnp.max, scores)
            probs = [jnp.exp2((s - top) * scale) for s in scores]
            denom = row_reduce(jnp.add, jnp.sum, probs)
            acc = sum(dot_nn(p.astype(jnp.bfloat16), v) for p, v in zip(probs, values))
            valid = slot < table[TABLE_COUNTS + c]
            out[pl.ds(c * tok, tok), cols] = jnp.where(valid, acc / denom, 0.0).astype(out.dtype)


def video_call(first, heads, table, q, k, v, near, text_k, text_v, carried):
    rows, width = q.shape
    text = text_k.shape[0]
    tok = rows // 2
    step = STEP_HEADS * HD
    base = first // STEP_HEADS
    whole = lambda h: (0, base + h)
    part = lambda h: (0, h)
    own_spec = pl.BlockSpec((rows, step), whole)
    part_spec = pl.BlockSpec((2 * rows + PAD_ROWS, step), part)
    text_spec = pl.BlockSpec((text, step), whole)
    in_specs = [pl.BlockSpec(memory_space=pltpu.SMEM), own_spec, own_spec, own_spec]
    in_specs += [part_spec] * 2
    in_specs += [pl.BlockSpec((rows + PAD_ROWS, step), part), pl.BlockSpec((rows, step), part)]
    in_specs += [own_spec] * 2 + [text_spec] * 2
    operands = [table, q, k, v, *near, text_k, text_v]
    aliases = {}
    if carried is not None:
        aliases = {len(operands): 0}
        operands.append(carried)
        in_specs.append(pl.BlockSpec(memory_space=pl.ANY))
    cells = 2 * BLOCKS + 1
    keys = 7 * tok + text
    return pl.pallas_call(
        video_kernel,
        grid=(heads // STEP_HEADS,),
        in_specs=in_specs,
        out_specs=own_spec,
        out_shape=jax.ShapeDtypeStruct((rows, width), q.dtype),
        scratch_shapes=[
            pltpu.VMEM((STEP_HEADS, cells * tok, HD), q.dtype),
            pltpu.VMEM((STEP_HEADS, cells * tok, HD), q.dtype),
            pltpu.VMEM((cells, 8, tok), jnp.float32),
        ],
        input_output_aliases=aliases,
        compiler_params=pltpu.CompilerParams(vmem_limit_bytes=VMEM_BYTES),
        cost_estimate=pl.CostEstimate(
            flops=heads * rows * keys * HD // 4,
            bytes_accessed=heads * rows * HD,
            transcendentals=0,
        ),
        name="video_attention",
    )(*operands)


STAT_SUMS = 32
PAIR_HEADS = HEADS // 2


def text_kernel(order, counts, q, k, v, k_beside, v_beside, keep, send, top, denom):
    step = pl.program_id(0)
    rows = k.shape[0]
    text = q.shape[0]
    half = text // 2
    places = order.shape[0] - 1
    share = text // places
    lane = lax.broadcasted_iota(jnp.int32, (text, HD), 1)

    @pl.when(step == 0)
    def _():
        top[...] = jnp.zeros_like(top)
        denom[...] = jnp.zeros_like(denom)

    @pl.when(step < PAIR_HEADS // STEP_HEADS)
    def _():
        slot = lax.broadcasted_iota(jnp.int32, (1, rows // 2), 1)
        bias = [
            jnp.concatenate(
                [jnp.where(slot < counts[at + c], 0.0, -jnp.inf) for c in range(2)], axis=1
            )
            for at in (0, 2)
        ]
        for i in range(STEP_HEADS):
            cols = pl.ds(i * HD, HD)
            head = step * STEP_HEADS + i
            query = jnp.concatenate(
                [
                    q[pl.ds(pl.multiple_of(order[j] * share, share), share), cols]
                    for j in range(places)
                ],
                axis=0,
            )
            scores = [
                dot_nt(query, keys[:, cols]) * (1.0 / math.sqrt(HD)) + bound
                for keys, bound in zip((k, k_beside), bias)
            ]
            m = row_reduce(jnp.maximum, jnp.max, scores)
            weights = [jnp.exp(s - m) for s in scores]
            l = row_reduce(jnp.add, jnp.sum, weights)
            acc = 0.0
            for w, values in zip(weights, (v, v_beside)):
                high = w.astype(jnp.bfloat16)
                low = (w - high.astype(jnp.float32)).astype(jnp.bfloat16)
                acc = acc + dot_nn(high, values[:, cols]) + dot_nn(low, values[:, cols])
            top[...] = jnp.where(lane == head, m, top[...])
            denom[...] = jnp.where(lane == head + STAT_SUMS, l, denom[...])
            keep[:, cols] = acc[:half]
            send[:, cols] = acc[half:]

    @pl.when(step == PAIR_HEADS // STEP_HEADS)
    def _():
        stats = top[...] + denom[...]
        keep[:, pl.ds(0, HD)] = stats[:half]
        send[:, pl.ds(0, HD)] = stats[half:]


def text_local(order, counts, q, k, v, k_beside, v_beside):
    text = q.shape[0]
    rows = k.shape[0]
    step = STEP_HEADS * HD
    last = PAIR_HEADS // STEP_HEADS - 1
    at = lambda h, order, counts: (0, order[order.shape[0] - 1] + jnp.minimum(h, last))
    k_spec = pl.BlockSpec((rows, step), at)
    out_spec = pl.BlockSpec((text // 2, step), lambda h, order, counts: (0, h))
    shape = jax.ShapeDtypeStruct((text // 2, PAIR_HEADS * HD + step), jnp.float32)
    return pl.pallas_call(
        text_kernel,
        grid_spec=pltpu.PrefetchScalarGridSpec(
            num_scalar_prefetch=2,
            grid=(last + 2,),
            in_specs=[pl.BlockSpec((text, step), at)] + [k_spec] * 4,
            out_specs=[out_spec, out_spec],
            scratch_shapes=[pltpu.VMEM((text, HD), jnp.float32)] * 2,
        ),
        out_shape=[shape, shape],
        compiler_params=pltpu.CompilerParams(vmem_limit_bytes=VMEM_BYTES),
        cost_estimate=pl.CostEstimate(
            flops=text * rows * HD, bytes_accessed=text * HEADS * HD, transcendentals=0
        ),
        name="text_partials",
    )(order, counts, q, k, v, k_beside, v_beside)


def merge_kernel(finish, *refs):
    width = PAIR_HEADS * HD
    stat_cols = pl.ds(width, HD)
    keep, got = refs[:2]
    mine = keep[:, stat_cols]
    theirs = got[:, stat_cols]
    lane = lax.broadcasted_iota(jnp.int32, mine.shape, 1)
    is_top = lane < STAT_SUMS
    top = jnp.maximum(mine, theirs)
    a = jnp.exp(jnp.where(is_top, mine - top, 0.0))
    b = jnp.exp(jnp.where(is_top, theirs - top, 0.0))
    first, second = refs[-2:]
    half = first.shape[0]
    stats = jnp.where(is_top, top, 0.0)
    if finish:
        limits = refs[2]
        row = lax.broadcasted_iota(jnp.int32, (2 * half, 1), 0)
        valid = row < jnp.where(row < half, limits[0], limits[1] + half)
    for h in range(PAIR_HEADS):
        cols = pl.ds(h * HD, HD)
        at = slice(h, h + 1)
        to = slice(STAT_SUMS + h, STAT_SUMS + h + 1)
        total = mine[:, to] * a[:, at] + theirs[:, to] * b[:, at]
        acc = keep[:, cols] * a[:, at] + got[:, cols] * b[:, at]
        if finish:
            acc = jnp.where(valid, acc / total, 0.0)
        else:
            stats = jnp.where(lane == STAT_SUMS + h, total, stats)
        first[:, cols] = acc[:half].astype(first.dtype)
        second[:, cols] = acc[half:].astype(second.dtype)
    if not finish:
        first[:, stat_cols] = stats[:half]
        second[:, stat_cols] = stats[half:]


def text_merge(keep, got):
    shape = jax.ShapeDtypeStruct((keep.shape[0] // 2, (PAIR_HEADS + 1) * HD), jnp.float32)
    return pl.pallas_call(
        functools.partial(merge_kernel, False),
        out_shape=[shape, shape],
        compiler_params=pltpu.CompilerParams(vmem_limit_bytes=VMEM_BYTES),
        name="text_merge",
    )(keep, got)


def text_finish(keep, got, limits):
    shape = jax.ShapeDtypeStruct((keep.shape[0] // 2, PAIR_HEADS * HD), jnp.bfloat16)
    vmem = pl.BlockSpec(memory_space=pltpu.VMEM)
    return pl.pallas_call(
        functools.partial(merge_kernel, True),
        in_specs=[vmem, vmem, pl.BlockSpec(memory_space=pltpu.SMEM)],
        out_shape=[shape, shape],
        compiler_params=pltpu.CompilerParams(vmem_limit_bytes=VMEM_BYTES),
        name="text_finish",
    )(keep, got, limits)


def text_order(n, position):
    bits = n.bit_length() - 1
    masks = [1 << b for b in (*range(1, bits), 0)]
    owners = [
        sum(mask for j, mask in enumerate(masks) if i >> (bits - 1 - j) & 1) for i in range(n)
    ]
    order = jnp.array(owners, jnp.int32) ^ position
    first = position % 2 * (PAIR_HEADS // STEP_HEADS)
    return jnp.concatenate([order, first[None]])


def text_plain(position, n, text_count, q, k, v, counts):
    text, width = q.shape
    share = text // n
    keys = k.reshape(-1, HEADS, HD)
    values = v.reshape(-1, HEADS, HD)
    slots = jnp.arange(k.shape[0] // counts.shape[0], dtype=jnp.int32)
    valid = (slots[None, :] < counts[:, None]).reshape(-1)
    scores = jnp.einsum(
        "qhd,khd->hqk", q.reshape(text, HEADS, HD), keys, preferred_element_type=jnp.float32
    ) * (1.0 / math.sqrt(HD))
    scores = jnp.where(valid[None, None, :], scores, -jnp.inf)
    top = lax.pmax(jnp.max(scores, axis=-1), "tiles")
    weights = jnp.exp(scores - top[..., None])
    denom = jnp.sum(weights, axis=-1).T
    numer = jnp.einsum(
        "hqk,khd->qhd", weights.astype(jnp.bfloat16), values, preferred_element_type=jnp.float32
    ).reshape(text, width)
    numer = lax.psum_scatter(numer, "tiles", scatter_dimension=0, tiled=True)
    denom = lax.psum_scatter(denom, "tiles", scatter_dimension=0, tiled=True)
    result = numer.reshape(share, HEADS, HD) / denom[:, :, None]
    row_ids = position * share + jnp.arange(share, dtype=jnp.int32)
    result = jnp.where((row_ids < text_count[0])[:, None, None], result, 0.0)
    return result.astype(jnp.bfloat16).reshape(share, width)


def make_table(window, counts, counts_beside, text_count, choices, position):
    columns = counts.shape[0]
    extra = (window % 3 != 0) | (window == 0)
    rank = jnp.cumsum(extra.astype(jnp.int32), axis=1) * extra
    codes = jnp.stack([jnp.sum(jnp.where(rank == j, window, 0), axis=1) for j in (1, 2)], axis=1)
    cells = codes + (codes >= 1)
    own = jnp.arange(columns, dtype=jnp.int32)[:, None]
    column = own + cells % 3 - 1
    inside = (column >= 0) & (column < columns)
    extra_cells = jnp.where(inside, column * BLOCKS + cells // 3, columns * BLOCKS)
    chosen = lax.dynamic_index_in_dim(jnp.array(choices, jnp.int32), position, 0, False)
    parts = [extra_cells.reshape(-1), counts, counts_beside, text_count, chosen]
    return jnp.concatenate([part.astype(jnp.int32) for part in parts])


def tie(value, *others):
    return lax.optimization_barrier((value, *others))[0]


def per_device(n, video_q, video_k, video_v, text_q, text_k, text_v, window, counts, text_count):
    rows, width = video_q.shape
    text = text_q.shape[0]
    position = lax.axis_index("tiles").astype(jnp.int32)
    pairs, relays_later, choices = plan_moves(n)
    sends_later = jnp.array(relays_later, jnp.int32)[position][None]

    starts = [sum(CHUNK_HEADS[:i]) for i in range(len(CHUNK_HEADS))]
    direct, outs = [], []

    def send(i, *before):
        chunk = pack(starts[i] * HD, CHUNK_HEADS[i] * HD, counts, video_k, video_v)
        mine = tie(chunk, *before)
        direct.append([lax.ppermute(mine, "tiles", pairs[x]) for x in ("earlier", "later")])

    send(0)
    beside = [
        lax.ppermute(x, "tiles", pairs["beside"]) for x in (counts, video_k, video_v)
    ]
    table = make_table(window, counts, beside[0], text_count, choices, position)
    halving = text % (PAD_ROWS * n) == 0 and n & (n - 1) == 0
    stages = n.bit_length() - 1
    parts = []
    if halving:
        order = text_order(n, position)
        both = jnp.concatenate([counts, beside[0]])
        parts.append(text_local(order, both, text_q, video_k, video_v, *beside[1:]))

    def exchanged(i):
        return lax.ppermute(parts[i][1], "tiles", [(d, d ^ (2 << i)) for d in range(n)])

    def merge(*before):
        i = len(parts) - 1
        if 0 <= i < stages - 2:
            parts.append(text_merge(tie(parts[i][0], *before), exchanged(i)))
        elif i == stages - 2:
            share = text // n
            limits = [text_count - place * share for place in (position, position ^ 1)]
            limits = jnp.concatenate(limits)
            parts.append(text_finish(tie(parts[i][0], *before), exchanged(i), limits))

    for _ in range(stages - 1):
        merge()
    count = len(CHUNK_HEADS)
    for i in range(count):
        before = outs[i - 1 : i] + ([parts[-1][0]] if halving and i == 0 else [])
        if i + 1 < count:
            send(i + 1, *direct[i], *before)
        up, down = direct[i]
        if i + 1 < count:
            up, down = tie(up, *before), tie(down, *before)
        relays = [
            lax.ppermute(half, "tiles", pairs["relayed"])
            for half in choose(sends_later, up, down, rows + PAD_ROWS)
        ]
        outs.append(
            video_call(
                starts[i], CHUNK_HEADS[i], table, video_q, video_k, video_v,
                [*direct[i], *relays, *beside[1:]], text_k, text_v, outs[-1] if outs else None,
            )
        )
    if halving:
        mine, leave = parts[-1]
        got = lax.ppermute(leave, "tiles", [(d, d ^ 1) for d in range(n)])
        low, high = jnp.concatenate([mine, got], axis=1), jnp.concatenate([got, mine], axis=1)
        text_out = jnp.where(position % 2 == 0, low, high)
    if not halving:
        text_out = text_plain(position, n, text_count, text_q, video_k, video_v, counts)
    return (outs[-1], text_out)


def solution(mesh):
    tiles = mesh.shape["tiles"]
    return jax.shard_map(
        functools.partial(per_device, tiles),
        mesh=mesh,
        in_specs=(
            P(("groups", "tiles"), None),
            P(("groups", "tiles"), None),
            P(("groups", "tiles"), None),
            P("groups", None),
            P("groups", None),
            P("groups", None),
            P("tiles", None),
            P(("groups", "tiles")),
            P("groups"),
        ),
        out_specs=(P(("groups", "tiles"), None), P(("groups", "tiles"), None)),
        check_vma=False,
    )
```

```python
import functools
import math

import jax
import jax.numpy as jnp
from jax import lax
from jax.experimental import pallas as pl
from jax.experimental.pallas import tpu as pltpu
from jax.sharding import PartitionSpec as P

HEADS = 24
HD = 128
NR = 4
BLOCKS = 5
STEP_HEADS = 2
CHUNK_HEADS = (12, 8, 4)
PAD_ROWS = 16
VMEM_BYTES = 48 * 1024 * 1024
LOG2E = 1.4426950408889634
SOURCES = ("own", "earlier", "later", "relayed", "beside")


def spot_shift(n):
    return n // 2 + NR + NR // 2


def plan_moves(n):
    shift, times = spot_shift(n), n // NR
    last = times - 1

    def at(t, r):
        return (t * NR + r - shift) % n

    moves = {
        "earlier": {at(t - 1, r): at(t, r) for t in range(1, times) for r in range(NR)},
        "later": {at(t + 1, r): at(t, r) for t in range(last) for r in range(NR)},
        "beside": {at(t, r): at(t, r ^ 1) for t in range(times) for r in range(NR)},
    }
    relay_earlier = {at(t + 1, 1): at(t, 2) for t in range(last)}
    relay_later = {at(t - 1, 2): at(t, 1) for t in range(1, times)}
    moves["later"][at(0, 2)] = at(last, 2)
    relay_later[at(last, 2)] = at(0, 1)
    moves["earlier"][at(last, 1)] = at(0, 1)
    relay_earlier[at(0, 1)] = at(last, 2)
    assert not set(relay_earlier) & set(relay_later)
    moves["relayed"] = {**relay_earlier, **relay_later}
    held = {"own": {d: d for d in range(n)}}
    for name in ("earlier", "later", "beside"):
        held[name] = {dst: src for src, dst in moves[name].items()}
    held["relayed"] = {dst: held["earlier"].get(src) for src, dst in relay_earlier.items()}
    held["relayed"].update({dst: held["later"].get(src) for src, dst in relay_later.items()})
    choice = []
    for device in range(n):
        spot = (device + shift) % n
        t, r = spot // NR, spot % NR
        row = []
        for dt, dr in ((-1, 0), (1, 0), (0, -1), (0, 1)):
            found = -1
            if 0 <= t + dt < times and 0 <= r + dr < NR:
                wanted = at(t + dt, r + dr)
                found = [i for i, s in enumerate(SOURCES) if held[s].get(device) == wanted][0]
            row.append(found)
        choice.append(row)
    for move in moves.values():
        assert len(set(move.values())) == len(move)
    pairs = {name: sorted(move.items()) for name, move in moves.items()}
    return pairs, [int(d in relay_later) for d in range(n)], choice


def pack_kernel(start, counts, k, v, out, limits, sems):
    rows, width = k.shape[0], out.shape[1]
    cols = pl.ds(start, width)
    copies = [
        pltpu.make_async_copy(k.at[:, cols], out.at[pl.ds(0, rows)], sems.at[0]),
        pltpu.make_async_copy(v.at[:, cols], out.at[pl.ds(rows + PAD_ROWS, rows)], sems.at[1]),
        pltpu.make_async_copy(limits, out.at[pl.ds(rows, PAD_ROWS)], sems.at[2]),
    ]
    copies[0].start()
    copies[1].start()
    row = lax.broadcasted_iota(jnp.int32, limits.shape, 0)
    value = jnp.where(row == 0, counts[0], jnp.where(row == 1, counts[1], 0))
    limits[...] = value.astype(jnp.float32).astype(limits.dtype)
    copies[2].start()
    for copy in copies:
        copy.wait()


def pack(start, width, counts, k, v):
    rows = k.shape[0]
    anywhere = pl.BlockSpec(memory_space=pl.ANY)
    return pl.pallas_call(
        functools.partial(pack_kernel, start),
        in_specs=[pl.BlockSpec(memory_space=pltpu.SMEM), anywhere, anywhere],
        out_specs=anywhere,
        out_shape=jax.ShapeDtypeStruct((2 * rows + PAD_ROWS, width), k.dtype),
        scratch_shapes=[pltpu.VMEM((PAD_ROWS, width), k.dtype), pltpu.SemaphoreType.DMA((3,))],
        compiler_params=pltpu.CompilerParams(vmem_limit_bytes=VMEM_BYTES),
        name="pack_chunk",
    )(counts, k, v)


def choose_kernel(second, a, b, first_out, last_out, sems):
    rows = first_out.shape[0]

    def move(ref):
        copies = [
            pltpu.make_async_copy(ref.at[pl.ds(0, rows)], first_out, sems.at[0]),
            pltpu.make_async_copy(ref.at[pl.ds(rows, last_out.shape[0])], last_out, sems.at[1]),
        ]
        for copy in copies:
            copy.start()
        for copy in copies:
            copy.wait()

    pl.when(second[0] == 0)(lambda: move(a))
    pl.when(second[0] != 0)(lambda: move(b))


def choose(second, a, b, rows):
    anywhere = pl.BlockSpec(memory_space=pl.ANY)
    shapes = [
        jax.ShapeDtypeStruct((part, a.shape[1]), a.dtype) for part in (rows, a.shape[0] - rows)
    ]
    return pl.pallas_call(
        choose_kernel,
        in_specs=[pl.BlockSpec(memory_space=pltpu.SMEM), anywhere, anywhere],
        out_specs=[pl.BlockSpec(memory_space=pltpu.VMEM)] * 2,
        out_shape=shapes,
        scratch_shapes=[pltpu.SemaphoreType.DMA((2,))],
        compiler_params=pltpu.CompilerParams(vmem_limit_bytes=VMEM_BYTES),
        name="choose_relayed",
    )(second, a, b)


def dot_nt(a, b):
    return lax.dot_general(a, b, (((1,), (1,)), ((), ())), preferred_element_type=jnp.float32)


def dot_nn(a, b):
    return jnp.dot(a, b, preferred_element_type=jnp.float32)


def lane_tiles(x):
    return [x[:, i : i + HD] for i in range(0, x.shape[1], HD)]


def row_reduce(op, final, pieces):
    tiles = [tile for piece in pieces for tile in lane_tiles(piece)]
    return final(functools.reduce(op, tiles), axis=1, keepdims=True)


TABLE_COUNTS, TABLE_BESIDE, TABLE_TEXT, TABLE_CHOICE = 4, 6, 8, 9


def video_kernel(table, q, k_own, v_own, *rest):
    packed = {"earlier": rest[0], "later": rest[1]}
    relayed_k, relayed_v, beside_k, beside_v, text_k, text_v = rest[2:8]
    out, k_all, v_all, bias_all = rest[-4:]
    tok = q.shape[0] // 2
    text = text_k.shape[0]
    scale = LOG2E / math.sqrt(HD)
    near = BLOCKS * tok
    dead = 2 * BLOCKS
    lane = lax.broadcasted_iota(jnp.int32, (8, tok), 1)
    lane_f = lane.astype(jnp.float32)

    def put(block, k, v, v_row):
        for i in range(STEP_HEADS):
            cols = pl.ds(i * HD, HD)
            for c in range(2):
                rows = pl.ds((c * BLOCKS + block) * tok, tok)
                k_all[i, rows, :] = k[pl.ds(c * tok, tok), cols]
                v_all[i, rows, :] = v[pl.ds(v_row + c * tok, tok), cols]

    def put_limits(block, tail):
        limits = tail[...].astype(jnp.float32)
        for c in range(2):
            bias_all[c * BLOCKS + block] = jnp.where(lane_f < limits[c : c + 1, :], 0.0, -jnp.inf)

    def put_counts(block, at):
        for c in range(2):
            bias_all[c * BLOCKS + block] = jnp.where(lane < table[at + c], 0.0, -jnp.inf)

    put(0, k_own, v_own, 0)
    put_counts(0, TABLE_COUNTS)
    tail = (pl.ds(2 * tok, PAD_ROWS), pl.ds(0, HD))
    options = {1: ("earlier",), 2: ("later",), 3: ("earlier",), 4: ("later",)}
    zeros = jnp.zeros((tok, HD), k_all.dtype)
    for block in range(1, BLOCKS):
        chosen = table[TABLE_CHOICE + block - 1]
        for name in options[block]:

            @pl.when(chosen == SOURCES.index(name))
            def _(ref=packed[name], block=block):
                put(block, ref, ref, 2 * tok + PAD_ROWS)
                put_limits(block, ref.at[tail])

        @pl.when(chosen == SOURCES.index("relayed"))
        def _(block=block):
            put(block, relayed_k, relayed_v, 0)
            put_limits(block, relayed_k.at[tail])

        if block > 2:

            @pl.when(chosen == SOURCES.index("beside"))
            def _(block=block):
                put(block, beside_k, beside_v, 0)
                put_counts(block, TABLE_BESIDE)

        @pl.when(chosen < 0)
        def _(block=block):
            for c in range(2):
                bias_all[c * BLOCKS + block] = jnp.full((8, tok), -jnp.inf, jnp.float32)
                for i in range(STEP_HEADS):
                    rows = pl.ds((c * BLOCKS + block) * tok, tok)
                    k_all[i, rows, :] = zeros
                    v_all[i, rows, :] = zeros

    bias_all[dead] = jnp.full((8, tok), -jnp.inf, jnp.float32)
    for i in range(STEP_HEADS):
        k_all[i, pl.ds(dead * tok, tok), :] = zeros
        v_all[i, pl.ds(dead * tok, tok), :] = zeros

    text_lane = lax.broadcasted_iota(jnp.int32, (1, text), 1)
    text_bias = jnp.where(text_lane < table[TABLE_TEXT], 0.0, -jnp.inf)
    slot = lax.broadcasted_iota(jnp.int32, (tok, 1), 0)
    for i in range(STEP_HEADS):
        cols = pl.ds(i * HD, HD)
        for c in range(2):
            query = q[pl.ds(c * tok, tok), cols]
            fixed = pl.ds(c * near, near)
            fixed_bias = jnp.concatenate(
                [bias_all[c * BLOCKS + b][0:1] for b in range(BLOCKS)], axis=1
            )
            scores = [dot_nt(query, k_all[i, fixed, :]) + fixed_bias]
            values = [v_all[i, fixed, :]]
            for j in range(2):
                cell = table[2 * c + j]
                rows = pl.ds(pl.multiple_of(cell * tok, tok), tok)
                scores.append(dot_nt(query, k_all[i, rows, :]) + bias_all[cell][0:1])
                values.append(v_all[i, rows, :])
            scores.append(dot_nt(query, text_k[:, cols]) + text_bias)
            values.append(text_v[:, cols])
            top = row_reduce(jnp.maximum, jnp.max, scores)
            probs = [jnp.exp2((s - top) * scale) for s in scores]
            denom = row_reduce(jnp.add, jnp.sum, probs)
            acc = sum(dot_nn(p.astype(jnp.bfloat16), v) for p, v in zip(probs, values))
            valid = slot < table[TABLE_COUNTS + c]
            out[pl.ds(c * tok, tok), cols] = jnp.where(valid, acc / denom, 0.0).astype(out.dtype)


def video_call(first, heads, table, q, k, v, near, text_k, text_v, carried):
    rows, width = q.shape
    text = text_k.shape[0]
    tok = rows // 2
    step = STEP_HEADS * HD
    base = first // STEP_HEADS
    whole = lambda h: (0, base + h)
    part = lambda h: (0, h)
    own_spec = pl.BlockSpec((rows, step), whole)
    part_spec = pl.BlockSpec((2 * rows + PAD_ROWS, step), part)
    text_spec = pl.BlockSpec((text, step), whole)
    in_specs = [pl.BlockSpec(memory_space=pltpu.SMEM), own_spec, own_spec, own_spec]
    in_specs += [part_spec] * 2
    in_specs += [pl.BlockSpec((rows + PAD_ROWS, step), part), pl.BlockSpec((rows, step), part)]
    in_specs += [own_spec] * 2 + [text_spec] * 2
    operands = [table, q, k, v, *near, text_k, text_v]
    aliases = {}
    if carried is not None:
        aliases = {len(operands): 0}
        operands.append(carried)
        in_specs.append(pl.BlockSpec(memory_space=pl.ANY))
    cells = 2 * BLOCKS + 1
    keys = 7 * tok + text
    return pl.pallas_call(
        video_kernel,
        grid=(heads // STEP_HEADS,),
        in_specs=in_specs,
        out_specs=own_spec,
        out_shape=jax.ShapeDtypeStruct((rows, width), q.dtype),
        scratch_shapes=[
            pltpu.VMEM((STEP_HEADS, cells * tok, HD), q.dtype),
            pltpu.VMEM((STEP_HEADS, cells * tok, HD), q.dtype),
            pltpu.VMEM((cells, 8, tok), jnp.float32),
        ],
        input_output_aliases=aliases,
        compiler_params=pltpu.CompilerParams(vmem_limit_bytes=VMEM_BYTES),
        cost_estimate=pl.CostEstimate(
            flops=heads * rows * keys * HD // 4,
            bytes_accessed=heads * rows * HD,
            transcendentals=0,
        ),
        name="video_attention",
    )(*operands)


STAT_SUMS = 32
PAIR_HEADS = HEADS // 2


def text_kernel(order, counts, q, k, v, k_beside, v_beside, keep, send, top, denom):
    step = pl.program_id(0)
    rows = k.shape[0]
    text = q.shape[0]
    half = text // 2
    places = order.shape[0] - 1
    share = text // places
    lane = lax.broadcasted_iota(jnp.int32, (text, HD), 1)

    @pl.when(step == 0)
    def _():
        top[...] = jnp.zeros_like(top)
        denom[...] = jnp.zeros_like(denom)

    @pl.when(step < PAIR_HEADS // STEP_HEADS)
    def _():
        slot = lax.broadcasted_iota(jnp.int32, (1, rows // 2), 1)
        bias = [
            jnp.concatenate(
                [jnp.where(slot < counts[at + c], 0.0, -jnp.inf) for c in range(2)], axis=1
            )
            for at in (0, 2)
        ]
        for i in range(STEP_HEADS):
            cols = pl.ds(i * HD, HD)
            head = step * STEP_HEADS + i
            query = jnp.concatenate(
                [
                    q[pl.ds(pl.multiple_of(order[j] * share, share), share), cols]
                    for j in range(places)
                ],
                axis=0,
            )
            scores = [
                dot_nt(query, keys[:, cols]) * (1.0 / math.sqrt(HD)) + bound
                for keys, bound in zip((k, k_beside), bias)
            ]
            m = row_reduce(jnp.maximum, jnp.max, scores)
            weights = [jnp.exp(s - m) for s in scores]
            l = row_reduce(jnp.add, jnp.sum, weights)
            acc = 0.0
            for w, values in zip(weights, (v, v_beside)):
                high = w.astype(jnp.bfloat16)
                low = (w - high.astype(jnp.float32)).astype(jnp.bfloat16)
                acc = acc + dot_nn(high, values[:, cols]) + dot_nn(low, values[:, cols])
            top[...] = jnp.where(lane == head, m, top[...])
            denom[...] = jnp.where(lane == head + STAT_SUMS, l, denom[...])
            keep[:, cols] = acc[:half]
            send[:, cols] = acc[half:]

    @pl.when(step == PAIR_HEADS // STEP_HEADS)
    def _():
        stats = top[...] + denom[...]
        keep[:, pl.ds(0, HD)] = stats[:half]
        send[:, pl.ds(0, HD)] = stats[half:]


def text_local(order, counts, q, k, v, k_beside, v_beside):
    text = q.shape[0]
    rows = k.shape[0]
    step = STEP_HEADS * HD
    last = PAIR_HEADS // STEP_HEADS - 1
    at = lambda h, order, counts: (0, order[order.shape[0] - 1] + jnp.minimum(h, last))
    k_spec = pl.BlockSpec((rows, step), at)
    out_spec = pl.BlockSpec((text // 2, step), lambda h, order, counts: (0, h))
    shape = jax.ShapeDtypeStruct((text // 2, PAIR_HEADS * HD + step), jnp.float32)
    return pl.pallas_call(
        text_kernel,
        grid_spec=pltpu.PrefetchScalarGridSpec(
            num_scalar_prefetch=2,
            grid=(last + 2,),
            in_specs=[pl.BlockSpec((text, step), at)] + [k_spec] * 4,
            out_specs=[out_spec, out_spec],
            scratch_shapes=[pltpu.VMEM((text, HD), jnp.float32)] * 2,
        ),
        out_shape=[shape, shape],
        compiler_params=pltpu.CompilerParams(vmem_limit_bytes=VMEM_BYTES),
        cost_estimate=pl.CostEstimate(
            flops=text * rows * HD, bytes_accessed=text * HEADS * HD, transcendentals=0
        ),
        name="text_partials",
    )(order, counts, q, k, v, k_beside, v_beside)


def merge_kernel(finish, *refs):
    width = PAIR_HEADS * HD
    stat_cols = pl.ds(width, HD)
    keep, got = refs[:2]
    mine = keep[:, stat_cols]
    theirs = got[:, stat_cols]
    lane = lax.broadcasted_iota(jnp.int32, mine.shape, 1)
    is_top = lane < STAT_SUMS
    top = jnp.maximum(mine, theirs)
    a = jnp.exp(jnp.where(is_top, mine - top, 0.0))
    b = jnp.exp(jnp.where(is_top, theirs - top, 0.0))
    first, second = refs[-2:]
    half = first.shape[0]
    stats = jnp.where(is_top, top, 0.0)
    if finish:
        limits = refs[2]
        row = lax.broadcasted_iota(jnp.int32, (2 * half, 1), 0)
        valid = row < jnp.where(row < half, limits[0], limits[1] + half)
    for h in range(PAIR_HEADS):
        cols = pl.ds(h * HD, HD)
        at = slice(h, h + 1)
        to = slice(STAT_SUMS + h, STAT_SUMS + h + 1)
        total = mine[:, to] * a[:, at] + theirs[:, to] * b[:, at]
        acc = keep[:, cols] * a[:, at] + got[:, cols] * b[:, at]
        if finish:
            acc = jnp.where(valid, acc / total, 0.0)
        else:
            stats = jnp.where(lane == STAT_SUMS + h, total, stats)
        first[:, cols] = acc[:half].astype(first.dtype)
        second[:, cols] = acc[half:].astype(second.dtype)
    if not finish:
        first[:, stat_cols] = stats[:half]
        second[:, stat_cols] = stats[half:]


def text_merge(keep, got):
    shape = jax.ShapeDtypeStruct((keep.shape[0] // 2, (PAIR_HEADS + 1) * HD), jnp.float32)
    return pl.pallas_call(
        functools.partial(merge_kernel, False),
        out_shape=[shape, shape],
        compiler_params=pltpu.CompilerParams(vmem_limit_bytes=VMEM_BYTES),
        name="text_merge",
    )(keep, got)


def text_finish(keep, got, limits):
    shape = jax.ShapeDtypeStruct((keep.shape[0] // 2, PAIR_HEADS * HD), jnp.bfloat16)
    vmem = pl.BlockSpec(memory_space=pltpu.VMEM)
    return pl.pallas_call(
        functools.partial(merge_kernel, True),
        in_specs=[vmem, vmem, pl.BlockSpec(memory_space=pltpu.SMEM)],
        out_shape=[shape, shape],
        compiler_params=pltpu.CompilerParams(vmem_limit_bytes=VMEM_BYTES),
        name="text_finish",
    )(keep, got, limits)


def text_order(n, position):
    bits = n.bit_length() - 1
    masks = [1 << b for b in (*range(1, bits), 0)]
    owners = [
        sum(mask for j, mask in enumerate(masks) if i >> (bits - 1 - j) & 1) for i in range(n)
    ]
    order = jnp.array(owners, jnp.int32) ^ position
    first = position % 2 * (PAIR_HEADS // STEP_HEADS)
    return jnp.concatenate([order, first[None]])


def text_plain(position, n, text_count, q, k, v, counts):
    text, width = q.shape
    share = text // n
    keys = k.reshape(-1, HEADS, HD)
    values = v.reshape(-1, HEADS, HD)
    slots = jnp.arange(k.shape[0] // counts.shape[0], dtype=jnp.int32)
    valid = (slots[None, :] < counts[:, None]).reshape(-1)
    scores = jnp.einsum(
        "qhd,khd->hqk", q.reshape(text, HEADS, HD), keys, preferred_element_type=jnp.float32
    ) * (1.0 / math.sqrt(HD))
    scores = jnp.where(valid[None, None, :], scores, -jnp.inf)
    top = lax.pmax(jnp.max(scores, axis=-1), "tiles")
    weights = jnp.exp(scores - top[..., None])
    denom = jnp.sum(weights, axis=-1).T
    numer = jnp.einsum(
        "hqk,khd->qhd", weights.astype(jnp.bfloat16), values, preferred_element_type=jnp.float32
    ).reshape(text, width)
    numer = lax.psum_scatter(numer, "tiles", scatter_dimension=0, tiled=True)
    denom = lax.psum_scatter(denom, "tiles", scatter_dimension=0, tiled=True)
    result = numer.reshape(share, HEADS, HD) / denom[:, :, None]
    row_ids = position * share + jnp.arange(share, dtype=jnp.int32)
    result = jnp.where((row_ids < text_count[0])[:, None, None], result, 0.0)
    return result.astype(jnp.bfloat16).reshape(share, width)


def make_table(window, counts, counts_beside, text_count, choices, position):
    columns = counts.shape[0]
    extra = (window % 3 != 0) | (window == 0)
    rank = jnp.cumsum(extra.astype(jnp.int32), axis=1) * extra
    codes = jnp.stack([jnp.sum(jnp.where(rank == j, window, 0), axis=1) for j in (1, 2)], axis=1)
    cells = codes + (codes >= 1)
    own = jnp.arange(columns, dtype=jnp.int32)[:, None]
    column = own + cells % 3 - 1
    inside = (column >= 0) & (column < columns)
    extra_cells = jnp.where(inside, column * BLOCKS + cells // 3, columns * BLOCKS)
    chosen = lax.dynamic_index_in_dim(jnp.array(choices, jnp.int32), position, 0, False)
    parts = [extra_cells.reshape(-1), counts, counts_beside, text_count, chosen]
    return jnp.concatenate([part.astype(jnp.int32) for part in parts])


def tie(value, *others):
    return lax.optimization_barrier((value, *others))[0]


def per_device(n, video_q, video_k, video_v, text_q, text_k, text_v, window, counts, text_count):
    rows, width = video_q.shape
    text = text_q.shape[0]
    position = lax.axis_index("tiles").astype(jnp.int32)
    pairs, relays_later, choices = plan_moves(n)
    sends_later = jnp.array(relays_later, jnp.int32)[position][None]

    starts = [sum(CHUNK_HEADS[:i]) for i in range(len(CHUNK_HEADS))]
    direct, outs = [], []

    def send(i, *before):
        chunk = pack(starts[i] * HD, CHUNK_HEADS[i] * HD, counts, video_k, video_v)
        mine = tie(chunk, *before)
        direct.append([lax.ppermute(mine, "tiles", pairs[x]) for x in ("earlier", "later")])

    send(0)
    beside = [
        lax.ppermute(x, "tiles", pairs["beside"]) for x in (counts, video_k, video_v)
    ]
    table = make_table(window, counts, beside[0], text_count, choices, position)
    halving = text % (PAD_ROWS * n) == 0 and n & (n - 1) == 0
    stages = n.bit_length() - 1
    parts = []
    if halving:
        order = text_order(n, position)
        both = jnp.concatenate([counts, beside[0]])
        parts.append(text_local(order, both, text_q, video_k, video_v, *beside[1:]))

    def exchanged(i):
        return lax.ppermute(parts[i][1], "tiles", [(d, d ^ (2 << i)) for d in range(n)])

    def merge(*before):
        i = len(parts) - 1
        if 0 <= i < stages - 2:
            parts.append(text_merge(tie(parts[i][0], *before), exchanged(i)))
        elif i == stages - 2:
            share = text // n
            limits = [text_count - place * share for place in (position, position ^ 1)]
            limits = jnp.concatenate(limits)
            parts.append(text_finish(tie(parts[i][0], *before), exchanged(i), limits))

    merge()
    count = len(CHUNK_HEADS)
    for i in range(count):
        before = outs[i - 1 : i] + ([parts[-1][0]] if halving and i == 0 else [])
        if i + 1 < count:
            send(i + 1, *direct[i], *before)
        up, down = tie(direct[i][0], *before), tie(direct[i][1], *before)
        relays = [
            lax.ppermute(half, "tiles", pairs["relayed"])
            for half in choose(sends_later, up, down, rows + PAD_ROWS)
        ]
        outs.append(
            video_call(
                starts[i], CHUNK_HEADS[i], table, video_q, video_k, video_v,
                [*direct[i], *relays, *beside[1:]], text_k, text_v, outs[-1] if outs else None,
            )
        )
        if i == 0:
            merge(outs[0])
        elif i == 1:
            merge(outs[1])
    if halving:
        mine, leave = parts[-1]
        got = lax.ppermute(leave, "tiles", [(d, d ^ 1) for d in range(n)])
        low, high = jnp.concatenate([mine, got], axis=1), jnp.concatenate([got, mine], axis=1)
        text_out = jnp.where(position % 2 == 0, low, high)
    if not halving:
        text_out = text_plain(position, n, text_count, text_q, video_k, video_v, counts)
    return (outs[-1], text_out)


def solution(mesh):
    tiles = mesh.shape["tiles"]
    return jax.shard_map(
        functools.partial(per_device, tiles),
        mesh=mesh,
        in_specs=(
            P(("groups", "tiles"), None),
            P(("groups", "tiles"), None),
            P(("groups", "tiles"), None),
            P("groups", None),
            P("groups", None),
            P("groups", None),
            P("tiles", None),
            P(("groups", "tiles")),
            P("groups"),
        ),
        out_specs=(P(("groups", "tiles"), None), P(("groups", "tiles"), None)),
        check_vma=False,
    )
```

```python
import functools
import math

import jax
import jax.numpy as jnp
from jax import lax
from jax.experimental import pallas as pl
from jax.experimental.pallas import tpu as pltpu
from jax.sharding import PartitionSpec as P

HEADS = 24
HD = 128
NR = 4
BLOCKS = 5
STEP_HEADS = 2
CHUNK_HEADS = (10, 8, 6)
PAD_ROWS = 16
VMEM_BYTES = 48 * 1024 * 1024
LOG2E = 1.4426950408889634
SOURCES = ("own", "earlier", "later", "relayed", "beside")


def spot_shift(n):
    return n // 2 + NR + NR // 2


def plan_moves(n):
    shift, times = spot_shift(n), n // NR
    last = times - 1

    def at(t, r):
        return (t * NR + r - shift) % n

    moves = {
        "earlier": {at(t - 1, r): at(t, r) for t in range(1, times) for r in range(NR)},
        "later": {at(t + 1, r): at(t, r) for t in range(last) for r in range(NR)},
        "beside": {at(t, r): at(t, r ^ 1) for t in range(times) for r in range(NR)},
    }
    relay_earlier = {at(t + 1, 1): at(t, 2) for t in range(last)}
    relay_later = {at(t - 1, 2): at(t, 1) for t in range(1, times)}
    moves["later"][at(0, 2)] = at(last, 2)
    relay_later[at(last, 2)] = at(0, 1)
    moves["earlier"][at(last, 1)] = at(0, 1)
    relay_earlier[at(0, 1)] = at(last, 2)
    assert not set(relay_earlier) & set(relay_later)
    moves["relayed"] = {**relay_earlier, **relay_later}
    held = {"own": {d: d for d in range(n)}}
    for name in ("earlier", "later", "beside"):
        held[name] = {dst: src for src, dst in moves[name].items()}
    held["relayed"] = {dst: held["earlier"].get(src) for src, dst in relay_earlier.items()}
    held["relayed"].update({dst: held["later"].get(src) for src, dst in relay_later.items()})
    choice = []
    for device in range(n):
        spot = (device + shift) % n
        t, r = spot // NR, spot % NR
        row = []
        for dt, dr in ((-1, 0), (1, 0), (0, -1), (0, 1)):
            found = -1
            if 0 <= t + dt < times and 0 <= r + dr < NR:
                wanted = at(t + dt, r + dr)
                found = [i for i, s in enumerate(SOURCES) if held[s].get(device) == wanted][0]
            row.append(found)
        choice.append(row)
    for move in moves.values():
        assert len(set(move.values())) == len(move)
    pairs = {name: sorted(move.items()) for name, move in moves.items()}
    return pairs, [int(d in relay_later) for d in range(n)], choice


def pack_kernel(start, counts, k, v, out, limits, sems):
    rows, width = k.shape[0], out.shape[1]
    cols = pl.ds(start, width)
    copies = [
        pltpu.make_async_copy(k.at[:, cols], out.at[pl.ds(0, rows)], sems.at[0]),
        pltpu.make_async_copy(v.at[:, cols], out.at[pl.ds(rows + PAD_ROWS, rows)], sems.at[1]),
        pltpu.make_async_copy(limits, out.at[pl.ds(rows, PAD_ROWS)], sems.at[2]),
    ]
    copies[0].start()
    copies[1].start()
    row = lax.broadcasted_iota(jnp.int32, limits.shape, 0)
    value = jnp.where(row == 0, counts[0], jnp.where(row == 1, counts[1], 0))
    limits[...] = value.astype(jnp.float32).astype(limits.dtype)
    copies[2].start()
    for copy in copies:
        copy.wait()


def pack(start, width, counts, k, v):
    rows = k.shape[0]
    anywhere = pl.BlockSpec(memory_space=pl.ANY)
    return pl.pallas_call(
        functools.partial(pack_kernel, start),
        in_specs=[pl.BlockSpec(memory_space=pltpu.SMEM), anywhere, anywhere],
        out_specs=anywhere,
        out_shape=jax.ShapeDtypeStruct((2 * rows + PAD_ROWS, width), k.dtype),
        scratch_shapes=[pltpu.VMEM((PAD_ROWS, width), k.dtype), pltpu.SemaphoreType.DMA((3,))],
        compiler_params=pltpu.CompilerParams(vmem_limit_bytes=VMEM_BYTES),
        name="pack_chunk",
    )(counts, k, v)


def choose_kernel(second, a, b, first_out, last_out, sems):
    rows = first_out.shape[0]

    def move(ref):
        copies = [
            pltpu.make_async_copy(ref.at[pl.ds(0, rows)], first_out, sems.at[0]),
            pltpu.make_async_copy(ref.at[pl.ds(rows, last_out.shape[0])], last_out, sems.at[1]),
        ]
        for copy in copies:
            copy.start()
        for copy in copies:
            copy.wait()

    pl.when(second[0] == 0)(lambda: move(a))
    pl.when(second[0] != 0)(lambda: move(b))


def choose(second, a, b, rows):
    anywhere = pl.BlockSpec(memory_space=pl.ANY)
    shapes = [
        jax.ShapeDtypeStruct((part, a.shape[1]), a.dtype) for part in (rows, a.shape[0] - rows)
    ]
    return pl.pallas_call(
        choose_kernel,
        in_specs=[pl.BlockSpec(memory_space=pltpu.SMEM), anywhere, anywhere],
        out_specs=[pl.BlockSpec(memory_space=pltpu.VMEM)] * 2,
        out_shape=shapes,
        scratch_shapes=[pltpu.SemaphoreType.DMA((2,))],
        compiler_params=pltpu.CompilerParams(vmem_limit_bytes=VMEM_BYTES),
        name="choose_relayed",
    )(second, a, b)


def dot_nt(a, b):
    return lax.dot_general(a, b, (((1,), (1,)), ((), ())), preferred_element_type=jnp.float32)


def dot_nn(a, b):
    return jnp.dot(a, b, preferred_element_type=jnp.float32)


def lane_tiles(x):
    return [x[:, i : i + HD] for i in range(0, x.shape[1], HD)]


def row_reduce(op, final, pieces):
    tiles = [tile for piece in pieces for tile in lane_tiles(piece)]
    return final(functools.reduce(op, tiles), axis=1, keepdims=True)


TABLE_COUNTS, TABLE_BESIDE, TABLE_TEXT, TABLE_CHOICE = 4, 6, 8, 9


def video_kernel(table, q, k_own, v_own, *rest):
    packed = {"earlier": rest[0], "later": rest[1]}
    relayed_k, relayed_v, beside_k, beside_v, text_k, text_v = rest[2:8]
    out, k_all, v_all, bias_all = rest[-4:]
    tok = q.shape[0] // 2
    text = text_k.shape[0]
    scale = LOG2E / math.sqrt(HD)
    near = BLOCKS * tok
    dead = 2 * BLOCKS
    lane = lax.broadcasted_iota(jnp.int32, (8, tok), 1)
    lane_f = lane.astype(jnp.float32)

    def put(block, k, v, v_row):
        for i in range(STEP_HEADS):
            cols = pl.ds(i * HD, HD)
            for c in range(2):
                rows = pl.ds((c * BLOCKS + block) * tok, tok)
                k_all[i, rows, :] = k[pl.ds(c * tok, tok), cols]
                v_all[i, rows, :] = v[pl.ds(v_row + c * tok, tok), cols]

    def put_limits(block, tail):
        limits = tail[...].astype(jnp.float32)
        for c in range(2):
            bias_all[c * BLOCKS + block] = jnp.where(lane_f < limits[c : c + 1, :], 0.0, -jnp.inf)

    def put_counts(block, at):
        for c in range(2):
            bias_all[c * BLOCKS + block] = jnp.where(lane < table[at + c], 0.0, -jnp.inf)

    put(0, k_own, v_own, 0)
    put_counts(0, TABLE_COUNTS)
    tail = (pl.ds(2 * tok, PAD_ROWS), pl.ds(0, HD))
    options = {1: ("earlier",), 2: ("later",), 3: ("earlier",), 4: ("later",)}
    zeros = jnp.zeros((tok, HD), k_all.dtype)
    for block in range(1, BLOCKS):
        chosen = table[TABLE_CHOICE + block - 1]
        for name in options[block]:

            @pl.when(chosen == SOURCES.index(name))
            def _(ref=packed[name], block=block):
                put(block, ref, ref, 2 * tok + PAD_ROWS)
                put_limits(block, ref.at[tail])

        @pl.when(chosen == SOURCES.index("relayed"))
        def _(block=block):
            put(block, relayed_k, relayed_v, 0)
            put_limits(block, relayed_k.at[tail])

        if block > 2:

            @pl.when(chosen == SOURCES.index("beside"))
            def _(block=block):
                put(block, beside_k, beside_v, 0)
                put_counts(block, TABLE_BESIDE)

        @pl.when(chosen < 0)
        def _(block=block):
            for c in range(2):
                bias_all[c * BLOCKS + block] = jnp.full((8, tok), -jnp.inf, jnp.float32)
                for i in range(STEP_HEADS):
                    rows = pl.ds((c * BLOCKS + block) * tok, tok)
                    k_all[i, rows, :] = zeros
                    v_all[i, rows, :] = zeros

    bias_all[dead] = jnp.full((8, tok), -jnp.inf, jnp.float32)
    for i in range(STEP_HEADS):
        k_all[i, pl.ds(dead * tok, tok), :] = zeros
        v_all[i, pl.ds(dead * tok, tok), :] = zeros

    text_lane = lax.broadcasted_iota(jnp.int32, (1, text), 1)
    text_bias = jnp.where(text_lane < table[TABLE_TEXT], 0.0, -jnp.inf)
    slot = lax.broadcasted_iota(jnp.int32, (tok, 1), 0)
    for i in range(STEP_HEADS):
        cols = pl.ds(i * HD, HD)
        for c in range(2):
            query = q[pl.ds(c * tok, tok), cols]
            fixed = pl.ds(c * near, near)
            fixed_bias = jnp.concatenate(
                [bias_all[c * BLOCKS + b][0:1] for b in range(BLOCKS)], axis=1
            )
            scores = [dot_nt(query, k_all[i, fixed, :]) + fixed_bias]
            values = [v_all[i, fixed, :]]
            for j in range(2):
                cell = table[2 * c + j]
                rows = pl.ds(pl.multiple_of(cell * tok, tok), tok)
                scores.append(dot_nt(query, k_all[i, rows, :]) + bias_all[cell][0:1])
                values.append(v_all[i, rows, :])
            scores.append(dot_nt(query, text_k[:, cols]) + text_bias)
            values.append(text_v[:, cols])
            top = row_reduce(jnp.maximum, jnp.max, scores)
            probs = [jnp.exp2((s - top) * scale) for s in scores]
            denom = row_reduce(jnp.add, jnp.sum, probs)
            acc = sum(dot_nn(p.astype(jnp.bfloat16), v) for p, v in zip(probs, values))
            valid = slot < table[TABLE_COUNTS + c]
            out[pl.ds(c * tok, tok), cols] = jnp.where(valid, acc / denom, 0.0).astype(out.dtype)


def video_call(first, heads, table, q, k, v, near, text_k, text_v, carried):
    rows, width = q.shape
    text = text_k.shape[0]
    tok = rows // 2
    step = STEP_HEADS * HD
    base = first // STEP_HEADS
    whole = lambda h: (0, base + h)
    part = lambda h: (0, h)
    own_spec = pl.BlockSpec((rows, step), whole)
    part_spec = pl.BlockSpec((2 * rows + PAD_ROWS, step), part)
    text_spec = pl.BlockSpec((text, step), whole)
    in_specs = [pl.BlockSpec(memory_space=pltpu.SMEM), own_spec, own_spec, own_spec]
    in_specs += [part_spec] * 2
    in_specs += [pl.BlockSpec((rows + PAD_ROWS, step), part), pl.BlockSpec((rows, step), part)]
    in_specs += [own_spec] * 2 + [text_spec] * 2
    operands = [table, q, k, v, *near, text_k, text_v]
    aliases = {}
    if carried is not None:
        aliases = {len(operands): 0}
        operands.append(carried)
        in_specs.append(pl.BlockSpec(memory_space=pl.ANY))
    cells = 2 * BLOCKS + 1
    keys = 7 * tok + text
    return pl.pallas_call(
        video_kernel,
        grid=(heads // STEP_HEADS,),
        in_specs=in_specs,
        out_specs=own_spec,
        out_shape=jax.ShapeDtypeStruct((rows, width), q.dtype),
        scratch_shapes=[
            pltpu.VMEM((STEP_HEADS, cells * tok, HD), q.dtype),
            pltpu.VMEM((STEP_HEADS, cells * tok, HD), q.dtype),
            pltpu.VMEM((cells, 8, tok), jnp.float32),
        ],
        input_output_aliases=aliases,
        compiler_params=pltpu.CompilerParams(vmem_limit_bytes=VMEM_BYTES),
        cost_estimate=pl.CostEstimate(
            flops=heads * rows * keys * HD // 4,
            bytes_accessed=heads * rows * HD,
            transcendentals=0,
        ),
        name="video_attention",
    )(*operands)


STAT_SUMS = 32
PAIR_HEADS = HEADS // 2


def text_kernel(order, counts, q, k, v, k_beside, v_beside, keep, send, top, denom):
    step = pl.program_id(0)
    rows = k.shape[0]
    text = q.shape[0]
    half = text // 2
    places = order.shape[0] - 1
    share = text // places
    lane = lax.broadcasted_iota(jnp.int32, (text, HD), 1)

    @pl.when(step == 0)
    def _():
        top[...] = jnp.zeros_like(top)
        denom[...] = jnp.zeros_like(denom)

    @pl.when(step < PAIR_HEADS // STEP_HEADS)
    def _():
        slot = lax.broadcasted_iota(jnp.int32, (1, rows // 2), 1)
        bias = [
            jnp.concatenate(
                [jnp.where(slot < counts[at + c], 0.0, -jnp.inf) for c in range(2)], axis=1
            )
            for at in (0, 2)
        ]
        for i in range(STEP_HEADS):
            cols = pl.ds(i * HD, HD)
            head = step * STEP_HEADS + i
            query = jnp.concatenate(
                [
                    q[pl.ds(pl.multiple_of(order[j] * share, share), share), cols]
                    for j in range(places)
                ],
                axis=0,
            )
            scores = [
                dot_nt(query, keys[:, cols]) * (1.0 / math.sqrt(HD)) + bound
                for keys, bound in zip((k, k_beside), bias)
            ]
            m = row_reduce(jnp.maximum, jnp.max, scores)
            weights = [jnp.exp(s - m) for s in scores]
            l = row_reduce(jnp.add, jnp.sum, weights)
            acc = 0.0
            for w, values in zip(weights, (v, v_beside)):
                high = w.astype(jnp.bfloat16)
                low = (w - high.astype(jnp.float32)).astype(jnp.bfloat16)
                acc = acc + dot_nn(high, values[:, cols]) + dot_nn(low, values[:, cols])
            top[...] = jnp.where(lane == head, m, top[...])
            denom[...] = jnp.where(lane == head + STAT_SUMS, l, denom[...])
            keep[:, cols] = acc[:half]
            send[:, cols] = acc[half:]

    @pl.when(step == PAIR_HEADS // STEP_HEADS)
    def _():
        stats = top[...] + denom[...]
        keep[:, pl.ds(0, HD)] = stats[:half]
        send[:, pl.ds(0, HD)] = stats[half:]


def text_local(order, counts, q, k, v, k_beside, v_beside):
    text = q.shape[0]
    rows = k.shape[0]
    step = STEP_HEADS * HD
    last = PAIR_HEADS // STEP_HEADS - 1
    at = lambda h, order, counts: (0, order[order.shape[0] - 1] + jnp.minimum(h, last))
    k_spec = pl.BlockSpec((rows, step), at)
    out_spec = pl.BlockSpec((text // 2, step), lambda h, order, counts: (0, h))
    shape = jax.ShapeDtypeStruct((text // 2, PAIR_HEADS * HD + step), jnp.float32)
    return pl.pallas_call(
        text_kernel,
        grid_spec=pltpu.PrefetchScalarGridSpec(
            num_scalar_prefetch=2,
            grid=(last + 2,),
            in_specs=[pl.BlockSpec((text, step), at)] + [k_spec] * 4,
            out_specs=[out_spec, out_spec],
            scratch_shapes=[pltpu.VMEM((text, HD), jnp.float32)] * 2,
        ),
        out_shape=[shape, shape],
        compiler_params=pltpu.CompilerParams(vmem_limit_bytes=VMEM_BYTES),
        cost_estimate=pl.CostEstimate(
            flops=text * rows * HD, bytes_accessed=text * HEADS * HD, transcendentals=0
        ),
        name="text_partials",
    )(order, counts, q, k, v, k_beside, v_beside)


def merge_kernel(finish, *refs):
    width = PAIR_HEADS * HD
    stat_cols = pl.ds(width, HD)
    keep, got = refs[:2]
    mine = keep[:, stat_cols]
    theirs = got[:, stat_cols]
    lane = lax.broadcasted_iota(jnp.int32, mine.shape, 1)
    is_top = lane < STAT_SUMS
    top = jnp.maximum(mine, theirs)
    a = jnp.exp(jnp.where(is_top, mine - top, 0.0))
    b = jnp.exp(jnp.where(is_top, theirs - top, 0.0))
    first, second = refs[-2:]
    half = first.shape[0]
    stats = jnp.where(is_top, top, 0.0)
    if finish:
        limits = refs[2]
        row = lax.broadcasted_iota(jnp.int32, (2 * half, 1), 0)
        valid = row < jnp.where(row < half, limits[0], limits[1] + half)
    for h in range(PAIR_HEADS):
        cols = pl.ds(h * HD, HD)
        at = slice(h, h + 1)
        to = slice(STAT_SUMS + h, STAT_SUMS + h + 1)
        total = mine[:, to] * a[:, at] + theirs[:, to] * b[:, at]
        acc = keep[:, cols] * a[:, at] + got[:, cols] * b[:, at]
        if finish:
            acc = jnp.where(valid, acc / total, 0.0)
        else:
            stats = jnp.where(lane == STAT_SUMS + h, total, stats)
        first[:, cols] = acc[:half].astype(first.dtype)
        second[:, cols] = acc[half:].astype(second.dtype)
    if not finish:
        first[:, stat_cols] = stats[:half]
        second[:, stat_cols] = stats[half:]


def text_merge(keep, got):
    shape = jax.ShapeDtypeStruct((keep.shape[0] // 2, (PAIR_HEADS + 1) * HD), jnp.float32)
    return pl.pallas_call(
        functools.partial(merge_kernel, False),
        out_shape=[shape, shape],
        compiler_params=pltpu.CompilerParams(vmem_limit_bytes=VMEM_BYTES),
        name="text_merge",
    )(keep, got)


def text_finish(keep, got, limits):
    shape = jax.ShapeDtypeStruct((keep.shape[0] // 2, PAIR_HEADS * HD), jnp.bfloat16)
    vmem = pl.BlockSpec(memory_space=pltpu.VMEM)
    return pl.pallas_call(
        functools.partial(merge_kernel, True),
        in_specs=[vmem, vmem, pl.BlockSpec(memory_space=pltpu.SMEM)],
        out_shape=[shape, shape],
        compiler_params=pltpu.CompilerParams(vmem_limit_bytes=VMEM_BYTES),
        name="text_finish",
    )(keep, got, limits)


def text_order(n, position):
    bits = n.bit_length() - 1
    masks = [1 << b for b in (*range(1, bits), 0)]
    owners = [
        sum(mask for j, mask in enumerate(masks) if i >> (bits - 1 - j) & 1) for i in range(n)
    ]
    order = jnp.array(owners, jnp.int32) ^ position
    first = position % 2 * (PAIR_HEADS // STEP_HEADS)
    return jnp.concatenate([order, first[None]])


def text_plain(position, n, text_count, q, k, v, counts):
    text, width = q.shape
    share = text // n
    keys = k.reshape(-1, HEADS, HD)
    values = v.reshape(-1, HEADS, HD)
    slots = jnp.arange(k.shape[0] // counts.shape[0], dtype=jnp.int32)
    valid = (slots[None, :] < counts[:, None]).reshape(-1)
    scores = jnp.einsum(
        "qhd,khd->hqk", q.reshape(text, HEADS, HD), keys, preferred_element_type=jnp.float32
    ) * (1.0 / math.sqrt(HD))
    scores = jnp.where(valid[None, None, :], scores, -jnp.inf)
    top = lax.pmax(jnp.max(scores, axis=-1), "tiles")
    weights = jnp.exp(scores - top[..., None])
    denom = jnp.sum(weights, axis=-1).T
    numer = jnp.einsum(
        "hqk,khd->qhd", weights.astype(jnp.bfloat16), values, preferred_element_type=jnp.float32
    ).reshape(text, width)
    numer = lax.psum_scatter(numer, "tiles", scatter_dimension=0, tiled=True)
    denom = lax.psum_scatter(denom, "tiles", scatter_dimension=0, tiled=True)
    result = numer.reshape(share, HEADS, HD) / denom[:, :, None]
    row_ids = position * share + jnp.arange(share, dtype=jnp.int32)
    result = jnp.where((row_ids < text_count[0])[:, None, None], result, 0.0)
    return result.astype(jnp.bfloat16).reshape(share, width)


def make_table(window, counts, counts_beside, text_count, choices, position):
    columns = counts.shape[0]
    extra = (window % 3 != 0) | (window == 0)
    rank = jnp.cumsum(extra.astype(jnp.int32), axis=1) * extra
    codes = jnp.stack([jnp.sum(jnp.where(rank == j, window, 0), axis=1) for j in (1, 2)], axis=1)
    cells = codes + (codes >= 1)
    own = jnp.arange(columns, dtype=jnp.int32)[:, None]
    column = own + cells % 3 - 1
    inside = (column >= 0) & (column < columns)
    extra_cells = jnp.where(inside, column * BLOCKS + cells // 3, columns * BLOCKS)
    chosen = lax.dynamic_index_in_dim(jnp.array(choices, jnp.int32), position, 0, False)
    parts = [extra_cells.reshape(-1), counts, counts_beside, text_count, chosen]
    return jnp.concatenate([part.astype(jnp.int32) for part in parts])


def tie(value, *others):
    return lax.optimization_barrier((value, *others))[0]


def per_device(n, video_q, video_k, video_v, text_q, text_k, text_v, window, counts, text_count):
    rows, width = video_q.shape
    text = text_q.shape[0]
    position = lax.axis_index("tiles").astype(jnp.int32)
    pairs, relays_later, choices = plan_moves(n)
    sends_later = jnp.array(relays_later, jnp.int32)[position][None]

    starts = [sum(CHUNK_HEADS[:i]) for i in range(len(CHUNK_HEADS))]
    direct, outs = [], []

    def send(i, *before):
        chunk = pack(starts[i] * HD, CHUNK_HEADS[i] * HD, counts, video_k, video_v)
        mine = tie(chunk, *before)
        direct.append([lax.ppermute(mine, "tiles", pairs[x]) for x in ("earlier", "later")])

    send(0)
    beside = [
        lax.ppermute(x, "tiles", pairs["beside"]) for x in (counts, video_k, video_v)
    ]
    table = make_table(window, counts, beside[0], text_count, choices, position)
    halving = text % (PAD_ROWS * n) == 0 and n & (n - 1) == 0
    stages = n.bit_length() - 1
    parts = []
    if halving:
        order = text_order(n, position)
        both = jnp.concatenate([counts, beside[0]])
        parts.append(text_local(order, both, text_q, video_k, video_v, *beside[1:]))

    def exchanged(i):
        return lax.ppermute(parts[i][1], "tiles", [(d, d ^ (2 << i)) for d in range(n)])

    def merge(*before):
        i = len(parts) - 1
        if 0 <= i < stages - 2:
            parts.append(text_merge(tie(parts[i][0], *before), exchanged(i)))
        elif i == stages - 2:
            share = text // n
            limits = [text_count - place * share for place in (position, position ^ 1)]
            limits = jnp.concatenate(limits)
            parts.append(text_finish(tie(parts[i][0], *before), exchanged(i), limits))

    merge()
    count = len(CHUNK_HEADS)
    for i in range(count):
        before = outs[i - 1 : i] + ([parts[-1][0]] if halving and i < 2 else [])
        if i + 1 < count:
            send(i + 1, *direct[i], *before)
        up, down = tie(direct[i][0], *before), tie(direct[i][1], *before)
        relays = [
            lax.ppermute(half, "tiles", pairs["relayed"])
            for half in choose(sends_later, up, down, rows + PAD_ROWS)
        ]
        outs.append(
            video_call(
                starts[i], CHUNK_HEADS[i], table, video_q, video_k, video_v,
                [*direct[i], *relays, *beside[1:]], text_k, text_v, outs[-1] if outs else None,
            )
        )
        if i == 0:
            merge(outs[0])
        elif i + 1 == count:
            merge(*relays)
    if halving:
        mine, leave = parts[-1]
        got = lax.ppermute(leave, "tiles", [(d, d ^ 1) for d in range(n)])
        low, high = jnp.concatenate([mine, got], axis=1), jnp.concatenate([got, mine], axis=1)
        text_out = jnp.where(position % 2 == 0, low, high)
    if not halving:
        text_out = text_plain(position, n, text_count, text_q, video_k, video_v, counts)
    return (outs[-1], text_out)


def solution(mesh):
    tiles = mesh.shape["tiles"]
    return jax.shard_map(
        functools.partial(per_device, tiles),
        mesh=mesh,
        in_specs=(
            P(("groups", "tiles"), None),
            P(("groups", "tiles"), None),
            P(("groups", "tiles"), None),
            P("groups", None),
            P("groups", None),
            P("groups", None),
            P("tiles", None),
            P(("groups", "tiles")),
            P("groups"),
        ),
        out_specs=(P(("groups", "tiles"), None), P(("groups", "tiles"), None)),
        check_vma=False,
    )
```

```python
import functools
import math

import jax
import jax.numpy as jnp
from jax import lax
from jax.experimental import pallas as pl
from jax.experimental.pallas import tpu as pltpu
from jax.sharding import PartitionSpec as P

HEADS = 24
HD = 128
NR = 4
BLOCKS = 5
STEP_HEADS = 2
CHUNK_HEADS = (12, 8, 4)
PAD_ROWS = 16
VMEM_BYTES = 48 * 1024 * 1024
LOG2E = 1.4426950408889634
SOURCES = ("own", "earlier", "later", "relayed", "beside")


def spot_shift(n):
    return n // 2 + NR + NR // 2


def plan_moves(n):
    shift, times = spot_shift(n), n // NR
    last = times - 1

    def at(t, r):
        return (t * NR + r - shift) % n

    moves = {
        "earlier": {at(t - 1, r): at(t, r) for t in range(1, times) for r in range(NR)},
        "later": {at(t + 1, r): at(t, r) for t in range(last) for r in range(NR)},
        "beside": {at(t, r): at(t, r ^ 1) for t in range(times) for r in range(NR)},
    }
    relay_earlier = {at(t + 1, 1): at(t, 2) for t in range(last)}
    relay_later = {at(t - 1, 2): at(t, 1) for t in range(1, times)}
    moves["later"][at(0, 2)] = at(last, 2)
    relay_later[at(last, 2)] = at(0, 1)
    moves["earlier"][at(last, 1)] = at(0, 1)
    relay_earlier[at(0, 1)] = at(last, 2)
    assert not set(relay_earlier) & set(relay_later)
    moves["relayed"] = {**relay_earlier, **relay_later}
    held = {"own": {d: d for d in range(n)}}
    for name in ("earlier", "later", "beside"):
        held[name] = {dst: src for src, dst in moves[name].items()}
    held["relayed"] = {dst: held["earlier"].get(src) for src, dst in relay_earlier.items()}
    held["relayed"].update({dst: held["later"].get(src) for src, dst in relay_later.items()})
    choice = []
    for device in range(n):
        spot = (device + shift) % n
        t, r = spot // NR, spot % NR
        row = []
        for dt, dr in ((-1, 0), (1, 0), (0, -1), (0, 1)):
            found = -1
            if 0 <= t + dt < times and 0 <= r + dr < NR:
                wanted = at(t + dt, r + dr)
                found = [i for i, s in enumerate(SOURCES) if held[s].get(device) == wanted][0]
            row.append(found)
        choice.append(row)
    for move in moves.values():
        assert len(set(move.values())) == len(move)
    pairs = {name: sorted(move.items()) for name, move in moves.items()}
    return pairs, [int(d in relay_later) for d in range(n)], choice


def pack_kernel(start, counts, k, v, out, limits, sems):
    rows, width = k.shape[0], out.shape[1]
    cols = pl.ds(start, width)
    copies = [
        pltpu.make_async_copy(k.at[:, cols], out.at[pl.ds(0, rows)], sems.at[0]),
        pltpu.make_async_copy(v.at[:, cols], out.at[pl.ds(rows + PAD_ROWS, rows)], sems.at[1]),
        pltpu.make_async_copy(limits, out.at[pl.ds(rows, PAD_ROWS)], sems.at[2]),
    ]
    copies[0].start()
    copies[1].start()
    row = lax.broadcasted_iota(jnp.int32, limits.shape, 0)
    value = jnp.where(row == 0, counts[0], jnp.where(row == 1, counts[1], 0))
    limits[...] = value.astype(jnp.float32).astype(limits.dtype)
    copies[2].start()
    for copy in copies:
        copy.wait()


def pack(start, width, counts, k, v):
    rows = k.shape[0]
    anywhere = pl.BlockSpec(memory_space=pl.ANY)
    return pl.pallas_call(
        functools.partial(pack_kernel, start),
        in_specs=[pl.BlockSpec(memory_space=pltpu.SMEM), anywhere, anywhere],
        out_specs=anywhere,
        out_shape=jax.ShapeDtypeStruct((2 * rows + PAD_ROWS, width), k.dtype),
        scratch_shapes=[pltpu.VMEM((PAD_ROWS, width), k.dtype), pltpu.SemaphoreType.DMA((3,))],
        compiler_params=pltpu.CompilerParams(vmem_limit_bytes=VMEM_BYTES),
        name="pack_chunk",
    )(counts, k, v)


def choose_kernel(second, a, b, first_out, last_out, sems):
    rows = first_out.shape[0]

    def move(ref):
        copies = [
            pltpu.make_async_copy(ref.at[pl.ds(0, rows)], first_out, sems.at[0]),
            pltpu.make_async_copy(ref.at[pl.ds(rows, last_out.shape[0])], last_out, sems.at[1]),
        ]
        for copy in copies:
            copy.start()
        for copy in copies:
            copy.wait()

    pl.when(second[0] == 0)(lambda: move(a))
    pl.when(second[0] != 0)(lambda: move(b))


def choose(second, a, b, rows):
    anywhere = pl.BlockSpec(memory_space=pl.ANY)
    shapes = [
        jax.ShapeDtypeStruct((part, a.shape[1]), a.dtype) for part in (rows, a.shape[0] - rows)
    ]
    return pl.pallas_call(
        choose_kernel,
        in_specs=[pl.BlockSpec(memory_space=pltpu.SMEM), anywhere, anywhere],
        out_specs=[pl.BlockSpec(memory_space=pltpu.VMEM)] * 2,
        out_shape=shapes,
        scratch_shapes=[pltpu.SemaphoreType.DMA((2,))],
        compiler_params=pltpu.CompilerParams(vmem_limit_bytes=VMEM_BYTES),
        name="choose_relayed",
    )(second, a, b)


def dot_nt(a, b):
    return lax.dot_general(a, b, (((1,), (1,)), ((), ())), preferred_element_type=jnp.float32)


def dot_nn(a, b):
    return jnp.dot(a, b, preferred_element_type=jnp.float32)


def lane_tiles(x):
    return [x[:, i : i + HD] for i in range(0, x.shape[1], HD)]


def row_reduce(op, final, pieces):
    tiles = [tile for piece in pieces for tile in lane_tiles(piece)]
    return final(functools.reduce(op, tiles), axis=1, keepdims=True)


TABLE_COUNTS, TABLE_BESIDE, TABLE_TEXT, TABLE_CHOICE = 4, 6, 8, 9


def video_kernel(table, q, k_own, v_own, *rest):
    packed = {"earlier": rest[0], "later": rest[1]}
    relayed_k, relayed_v, beside_k, beside_v, text_k, text_v = rest[2:8]
    out, k_all, v_all, bias_all = rest[-4:]
    tok = q.shape[0] // 2
    text = text_k.shape[0]
    scale = LOG2E / math.sqrt(HD)
    near = BLOCKS * tok
    dead = 2 * BLOCKS
    lane = lax.broadcasted_iota(jnp.int32, (8, tok), 1)
    lane_f = lane.astype(jnp.float32)

    def put(block, k, v, v_row):
        for i in range(STEP_HEADS):
            cols = pl.ds(i * HD, HD)
            for c in range(2):
                rows = pl.ds((c * BLOCKS + block) * tok, tok)
                k_all[i, rows, :] = k[pl.ds(c * tok, tok), cols]
                v_all[i, rows, :] = v[pl.ds(v_row + c * tok, tok), cols]

    def put_limits(block, tail):
        limits = tail[...].astype(jnp.float32)
        for c in range(2):
            bias_all[c * BLOCKS + block] = jnp.where(lane_f < limits[c : c + 1, :], 0.0, -jnp.inf)

    def put_counts(block, at):
        for c in range(2):
            bias_all[c * BLOCKS + block] = jnp.where(lane < table[at + c], 0.0, -jnp.inf)

    put(0, k_own, v_own, 0)
    put_counts(0, TABLE_COUNTS)
    tail = (pl.ds(2 * tok, PAD_ROWS), pl.ds(0, HD))
    options = {1: ("earlier",), 2: ("later",), 3: ("earlier",), 4: ("later",)}
    zeros = jnp.zeros((tok, HD), k_all.dtype)
    for block in range(1, BLOCKS):
        chosen = table[TABLE_CHOICE + block - 1]
        for name in options[block]:

            @pl.when(chosen == SOURCES.index(name))
            def _(ref=packed[name], block=block):
                put(block, ref, ref, 2 * tok + PAD_ROWS)
                put_limits(block, ref.at[tail])

        @pl.when(chosen == SOURCES.index("relayed"))
        def _(block=block):
            put(block, relayed_k, relayed_v, 0)
            put_limits(block, relayed_k.at[tail])

        if block > 2:

            @pl.when(chosen == SOURCES.index("beside"))
            def _(block=block):
                put(block, beside_k, beside_v, 0)
                put_counts(block, TABLE_BESIDE)

        @pl.when(chosen < 0)
        def _(block=block):
            for c in range(2):
                bias_all[c * BLOCKS + block] = jnp.full((8, tok), -jnp.inf, jnp.float32)
                for i in range(STEP_HEADS):
                    rows = pl.ds((c * BLOCKS + block) * tok, tok)
                    k_all[i, rows, :] = zeros
                    v_all[i, rows, :] = zeros

    bias_all[dead] = jnp.full((8, tok), -jnp.inf, jnp.float32)
    for i in range(STEP_HEADS):
        k_all[i, pl.ds(dead * tok, tok), :] = zeros
        v_all[i, pl.ds(dead * tok, tok), :] = zeros

    text_lane = lax.broadcasted_iota(jnp.int32, (1, text), 1)
    text_bias = jnp.where(text_lane < table[TABLE_TEXT], 0.0, -jnp.inf)
    slot = lax.broadcasted_iota(jnp.int32, (tok, 1), 0)
    for i in range(STEP_HEADS):
        cols = pl.ds(i * HD, HD)
        for c in range(2):
            query = q[pl.ds(c * tok, tok), cols]
            fixed = pl.ds(c * near, near)
            fixed_bias = jnp.concatenate(
                [bias_all[c * BLOCKS + b][0:1] for b in range(BLOCKS)], axis=1
            )
            scores = [dot_nt(query, k_all[i, fixed, :]) + fixed_bias]
            values = [v_all[i, fixed, :]]
            for j in range(2):
                cell = table[2 * c + j]
                rows = pl.ds(pl.multiple_of(cell * tok, tok), tok)
                scores.append(dot_nt(query, k_all[i, rows, :]) + bias_all[cell][0:1])
                values.append(v_all[i, rows, :])
            scores.append(dot_nt(query, text_k[:, cols]) + text_bias)
            values.append(text_v[:, cols])
            top = row_reduce(jnp.maximum, jnp.max, scores)
            probs = [jnp.exp2((s - top) * scale) for s in scores]
            denom = row_reduce(jnp.add, jnp.sum, probs)
            acc = sum(dot_nn(p.astype(jnp.bfloat16), v) for p, v in zip(probs, values))
            valid = slot < table[TABLE_COUNTS + c]
            out[pl.ds(c * tok, tok), cols] = jnp.where(valid, acc / denom, 0.0).astype(out.dtype)


def video_call(first, heads, table, q, k, v, near, text_k, text_v, carried):
    rows, width = q.shape
    text = text_k.shape[0]
    tok = rows // 2
    step = STEP_HEADS * HD
    base = first // STEP_HEADS
    whole = lambda h: (0, base + h)
    part = lambda h: (0, h)
    own_spec = pl.BlockSpec((rows, step), whole)
    part_spec = pl.BlockSpec((2 * rows + PAD_ROWS, step), part)
    text_spec = pl.BlockSpec((text, step), whole)
    in_specs = [pl.BlockSpec(memory_space=pltpu.SMEM), own_spec, own_spec, own_spec]
    in_specs += [part_spec] * 2
    in_specs += [pl.BlockSpec((rows + PAD_ROWS, step), part), pl.BlockSpec((rows, step), part)]
    in_specs += [own_spec] * 2 + [text_spec] * 2
    operands = [table, q, k, v, *near, text_k, text_v]
    aliases = {}
    if carried is not None:
        aliases = {len(operands): 0}
        operands.append(carried)
        in_specs.append(pl.BlockSpec(memory_space=pl.ANY))
    cells = 2 * BLOCKS + 1
    keys = 7 * tok + text
    return pl.pallas_call(
        video_kernel,
        grid=(heads // STEP_HEADS,),
        in_specs=in_specs,
        out_specs=own_spec,
        out_shape=jax.ShapeDtypeStruct((rows, width), q.dtype),
        scratch_shapes=[
            pltpu.VMEM((STEP_HEADS, cells * tok, HD), q.dtype),
            pltpu.VMEM((STEP_HEADS, cells * tok, HD), q.dtype),
            pltpu.VMEM((cells, 8, tok), jnp.float32),
        ],
        input_output_aliases=aliases,
        compiler_params=pltpu.CompilerParams(vmem_limit_bytes=VMEM_BYTES),
        cost_estimate=pl.CostEstimate(
            flops=heads * rows * keys * HD // 4,
            bytes_accessed=heads * rows * HD,
            transcendentals=0,
        ),
        name="video_attention",
    )(*operands)


STAT_SUMS = 32
PAIR_HEADS = HEADS // 2


def text_kernel(order, counts, q, k, v, k_beside, v_beside, keep, send, top, denom):
    step = pl.program_id(0)
    rows = k.shape[0]
    text = q.shape[0]
    half = text // 2
    places = order.shape[0] - 1
    share = text // places
    lane = lax.broadcasted_iota(jnp.int32, (text, HD), 1)

    @pl.when(step == 0)
    def _():
        top[...] = jnp.zeros_like(top)
        denom[...] = jnp.zeros_like(denom)

    @pl.when(step < PAIR_HEADS // STEP_HEADS)
    def _():
        slot = lax.broadcasted_iota(jnp.int32, (1, rows // 2), 1)
        bias = [
            jnp.concatenate(
                [jnp.where(slot < counts[at + c], 0.0, -jnp.inf) for c in range(2)], axis=1
            )
            for at in (0, 2)
        ]
        for i in range(STEP_HEADS):
            cols = pl.ds(i * HD, HD)
            head = step * STEP_HEADS + i
            query = jnp.concatenate(
                [
                    q[pl.ds(pl.multiple_of(order[j] * share, share), share), cols]
                    for j in range(places)
                ],
                axis=0,
            )
            scores = [
                dot_nt(query, keys[:, cols]) * (1.0 / math.sqrt(HD)) + bound
                for keys, bound in zip((k, k_beside), bias)
            ]
            m = row_reduce(jnp.maximum, jnp.max, scores)
            weights = [jnp.exp(s - m) for s in scores]
            l = row_reduce(jnp.add, jnp.sum, weights)
            acc = 0.0
            for w, values in zip(weights, (v, v_beside)):
                high = w.astype(jnp.bfloat16)
                low = (w - high.astype(jnp.float32)).astype(jnp.bfloat16)
                acc = acc + dot_nn(high, values[:, cols]) + dot_nn(low, values[:, cols])
            top[...] = jnp.where(lane == head, m, top[...])
            denom[...] = jnp.where(lane == head + STAT_SUMS, l, denom[...])
            keep[:, cols] = acc[:half]
            send[:, cols] = acc[half:]

    @pl.when(step == PAIR_HEADS // STEP_HEADS)
    def _():
        stats = top[...] + denom[...]
        keep[:, pl.ds(0, HD)] = stats[:half]
        send[:, pl.ds(0, HD)] = stats[half:]


def text_local(order, counts, q, k, v, k_beside, v_beside):
    text = q.shape[0]
    rows = k.shape[0]
    step = STEP_HEADS * HD
    last = PAIR_HEADS // STEP_HEADS - 1
    at = lambda h, order, counts: (0, order[order.shape[0] - 1] + jnp.minimum(h, last))
    k_spec = pl.BlockSpec((rows, step), at)
    out_spec = pl.BlockSpec((text // 2, step), lambda h, order, counts: (0, h))
    shape = jax.ShapeDtypeStruct((text // 2, PAIR_HEADS * HD + step), jnp.float32)
    return pl.pallas_call(
        text_kernel,
        grid_spec=pltpu.PrefetchScalarGridSpec(
            num_scalar_prefetch=2,
            grid=(last + 2,),
            in_specs=[pl.BlockSpec((text, step), at)] + [k_spec] * 4,
            out_specs=[out_spec, out_spec],
            scratch_shapes=[pltpu.VMEM((text, HD), jnp.float32)] * 2,
        ),
        out_shape=[shape, shape],
        compiler_params=pltpu.CompilerParams(vmem_limit_bytes=VMEM_BYTES),
        cost_estimate=pl.CostEstimate(
            flops=text * rows * HD, bytes_accessed=text * HEADS * HD, transcendentals=0
        ),
        name="text_partials",
    )(order, counts, q, k, v, k_beside, v_beside)


def merge_kernel(finish, *refs):
    width = PAIR_HEADS * HD
    stat_cols = pl.ds(width, HD)
    keep, got = refs[:2]
    mine = keep[:, stat_cols]
    theirs = got[:, stat_cols]
    lane = lax.broadcasted_iota(jnp.int32, mine.shape, 1)
    is_top = lane < STAT_SUMS
    top = jnp.maximum(mine, theirs)
    a = jnp.exp(jnp.where(is_top, mine - top, 0.0))
    b = jnp.exp(jnp.where(is_top, theirs - top, 0.0))
    first, second = refs[-2:]
    half = first.shape[0]
    stats = jnp.where(is_top, top, 0.0)
    if finish:
        limits = refs[2]
        row = lax.broadcasted_iota(jnp.int32, (2 * half, 1), 0)
        valid = row < jnp.where(row < half, limits[0], limits[1] + half)
    for h in range(PAIR_HEADS):
        cols = pl.ds(h * HD, HD)
        at = slice(h, h + 1)
        to = slice(STAT_SUMS + h, STAT_SUMS + h + 1)
        total = mine[:, to] * a[:, at] + theirs[:, to] * b[:, at]
        acc = keep[:, cols] * a[:, at] + got[:, cols] * b[:, at]
        if finish:
            acc = jnp.where(valid, acc / total, 0.0)
        else:
            stats = jnp.where(lane == STAT_SUMS + h, total, stats)
        first[:, cols] = acc[:half].astype(first.dtype)
        second[:, cols] = acc[half:].astype(second.dtype)
    if not finish:
        first[:, stat_cols] = stats[:half]
        second[:, stat_cols] = stats[half:]


def text_merge(keep, got):
    shape = jax.ShapeDtypeStruct((keep.shape[0] // 2, (PAIR_HEADS + 1) * HD), jnp.float32)
    return pl.pallas_call(
        functools.partial(merge_kernel, False),
        out_shape=[shape, shape],
        compiler_params=pltpu.CompilerParams(vmem_limit_bytes=VMEM_BYTES),
        name="text_merge",
    )(keep, got)


def text_finish(keep, got, limits):
    shape = jax.ShapeDtypeStruct((keep.shape[0] // 2, PAIR_HEADS * HD), jnp.bfloat16)
    vmem = pl.BlockSpec(memory_space=pltpu.VMEM)
    return pl.pallas_call(
        functools.partial(merge_kernel, True),
        in_specs=[vmem, vmem, pl.BlockSpec(memory_space=pltpu.SMEM)],
        out_shape=[shape, shape],
        compiler_params=pltpu.CompilerParams(vmem_limit_bytes=VMEM_BYTES),
        name="text_finish",
    )(keep, got, limits)


def text_order(n, position):
    bits = n.bit_length() - 1
    masks = [1 << b for b in (*range(1, bits), 0)]
    owners = [
        sum(mask for j, mask in enumerate(masks) if i >> (bits - 1 - j) & 1) for i in range(n)
    ]
    order = jnp.array(owners, jnp.int32) ^ position
    first = position % 2 * (PAIR_HEADS // STEP_HEADS)
    return jnp.concatenate([order, first[None]])


def text_plain(position, n, text_count, q, k, v, counts):
    text, width = q.shape
    share = text // n
    keys = k.reshape(-1, HEADS, HD)
    values = v.reshape(-1, HEADS, HD)
    slots = jnp.arange(k.shape[0] // counts.shape[0], dtype=jnp.int32)
    valid = (slots[None, :] < counts[:, None]).reshape(-1)
    scores = jnp.einsum(
        "qhd,khd->hqk", q.reshape(text, HEADS, HD), keys, preferred_element_type=jnp.float32
    ) * (1.0 / math.sqrt(HD))
    scores = jnp.where(valid[None, None, :], scores, -jnp.inf)
    top = lax.pmax(jnp.max(scores, axis=-1), "tiles")
    weights = jnp.exp(scores - top[..., None])
    denom = jnp.sum(weights, axis=-1).T
    numer = jnp.einsum(
        "hqk,khd->qhd", weights.astype(jnp.bfloat16), values, preferred_element_type=jnp.float32
    ).reshape(text, width)
    numer = lax.psum_scatter(numer, "tiles", scatter_dimension=0, tiled=True)
    denom = lax.psum_scatter(denom, "tiles", scatter_dimension=0, tiled=True)
    result = numer.reshape(share, HEADS, HD) / denom[:, :, None]
    row_ids = position * share + jnp.arange(share, dtype=jnp.int32)
    result = jnp.where((row_ids < text_count[0])[:, None, None], result, 0.0)
    return result.astype(jnp.bfloat16).reshape(share, width)


def make_table(window, counts, counts_beside, text_count, choices, position):
    columns = counts.shape[0]
    extra = (window % 3 != 0) | (window == 0)
    rank = jnp.cumsum(extra.astype(jnp.int32), axis=1) * extra
    codes = jnp.stack([jnp.sum(jnp.where(rank == j, window, 0), axis=1) for j in (1, 2)], axis=1)
    cells = codes + (codes >= 1)
    own = jnp.arange(columns, dtype=jnp.int32)[:, None]
    column = own + cells % 3 - 1
    inside = (column >= 0) & (column < columns)
    extra_cells = jnp.where(inside, column * BLOCKS + cells // 3, columns * BLOCKS)
    chosen = lax.dynamic_index_in_dim(jnp.array(choices, jnp.int32), position, 0, False)
    parts = [extra_cells.reshape(-1), counts, counts_beside, text_count, chosen]
    return jnp.concatenate([part.astype(jnp.int32) for part in parts])


def tie(value, *others):
    return lax.optimization_barrier((value, *others))[0]


def per_device(n, video_q, video_k, video_v, text_q, text_k, text_v, window, counts, text_count):
    rows, width = video_q.shape
    text = text_q.shape[0]
    position = lax.axis_index("tiles").astype(jnp.int32)
    pairs, relays_later, choices = plan_moves(n)
    sends_later = jnp.array(relays_later, jnp.int32)[position][None]

    starts = [sum(CHUNK_HEADS[:i]) for i in range(len(CHUNK_HEADS))]
    direct, outs = [], []

    def send(i, *before):
        chunk = pack(starts[i] * HD, CHUNK_HEADS[i] * HD, counts, video_k, video_v)
        mine = tie(chunk, *before)
        direct.append([lax.ppermute(mine, "tiles", pairs[x]) for x in ("earlier", "later")])

    send(0)
    beside = [
        lax.ppermute(x, "tiles", pairs["beside"]) for x in (counts, video_k, video_v)
    ]
    table = make_table(window, counts, beside[0], text_count, choices, position)
    halving = text % (PAD_ROWS * n) == 0 and n & (n - 1) == 0
    stages = n.bit_length() - 1
    parts = []
    if halving:
        order = text_order(n, position)
        both = jnp.concatenate([counts, beside[0]])
        parts.append(text_local(order, both, text_q, video_k, video_v, *beside[1:]))

    def exchanged(i):
        return lax.ppermute(parts[i][1], "tiles", [(d, d ^ (2 << i)) for d in range(n)])

    def merge(*before):
        i = len(parts) - 1
        if 0 <= i < stages - 2:
            parts.append(text_merge(tie(parts[i][0], *before), exchanged(i)))
        elif i == stages - 2:
            share = text // n
            limits = [text_count - place * share for place in (position, position ^ 1)]
            limits = jnp.concatenate(limits)
            parts.append(text_finish(tie(parts[i][0], *before), exchanged(i), limits))

    merge()
    count = len(CHUNK_HEADS)
    for i in range(count):
        before = outs[i - 1 : i] + ([parts[-1][0]] if halving and i == 0 else [])
        if i + 1 < count:
            send(i + 1, *direct[i], *before)
        up, down = tie(direct[i][0], *before), tie(direct[i][1], *before)
        relays = [
            lax.ppermute(half, "tiles", pairs["relayed"])
            for half in choose(sends_later, up, down, rows + PAD_ROWS)
        ]
        outs.append(
            video_call(
                starts[i], CHUNK_HEADS[i], table, video_q, video_k, video_v,
                [*direct[i], *relays, *beside[1:]], text_k, text_v, outs[-1] if outs else None,
            )
        )
        if i == 0:
            merge(outs[0])
        elif i + 1 == count:
            merge(*relays)
    if halving:
        mine, leave = parts[-1]
        got = lax.ppermute(leave, "tiles", [(d, d ^ 1) for d in range(n)])
        low, high = jnp.concatenate([mine, got], axis=1), jnp.concatenate([got, mine], axis=1)
        text_out = jnp.where(position % 2 == 0, low, high)
    if not halving:
        text_out = text_plain(position, n, text_count, text_q, video_k, video_v, counts)
    return (outs[-1], text_out)


def solution(mesh):
    tiles = mesh.shape["tiles"]
    return jax.shard_map(
        functools.partial(per_device, tiles),
        mesh=mesh,
        in_specs=(
            P(("groups", "tiles"), None),
            P(("groups", "tiles"), None),
            P(("groups", "tiles"), None),
            P("groups", None),
            P("groups", None),
            P("groups", None),
            P("tiles", None),
            P(("groups", "tiles")),
            P("groups"),
        ),
        out_specs=(P(("groups", "tiles"), None), P(("groups", "tiles"), None)),
        check_vma=False,
    )
```

```python
import functools
import math

import jax
import jax.numpy as jnp
from jax import lax
from jax.experimental import pallas as pl
from jax.experimental.pallas import tpu as pltpu
from jax.sharding import PartitionSpec as P

HEADS = 24
HD = 128
NR = 4
BLOCKS = 5
STEP_HEADS = 2
CHUNK_HEADS = (12, 8, 4)
PAD_ROWS = 16
VMEM_BYTES = 48 * 1024 * 1024
LOG2E = 1.4426950408889634
SOURCES = ("own", "earlier", "later", "relayed", "beside")


def spot_shift(n):
    return n // 2 + NR + NR // 2


def plan_moves(n):
    shift, times = spot_shift(n), n // NR
    last = times - 1

    def at(t, r):
        return (t * NR + r - shift) % n

    moves = {
        "earlier": {at(t - 1, r): at(t, r) for t in range(1, times) for r in range(NR)},
        "later": {at(t + 1, r): at(t, r) for t in range(last) for r in range(NR)},
        "beside": {at(t, r): at(t, r ^ 1) for t in range(times) for r in range(NR)},
    }
    relay_earlier = {at(t + 1, 1): at(t, 2) for t in range(last)}
    relay_later = {at(t - 1, 2): at(t, 1) for t in range(1, times)}
    moves["later"][at(0, 2)] = at(last, 2)
    relay_later[at(last, 2)] = at(0, 1)
    moves["earlier"][at(last, 1)] = at(0, 1)
    relay_earlier[at(0, 1)] = at(last, 2)
    assert not set(relay_earlier) & set(relay_later)
    moves["relayed"] = {**relay_earlier, **relay_later}
    held = {"own": {d: d for d in range(n)}}
    for name in ("earlier", "later", "beside"):
        held[name] = {dst: src for src, dst in moves[name].items()}
    held["relayed"] = {dst: held["earlier"].get(src) for src, dst in relay_earlier.items()}
    held["relayed"].update({dst: held["later"].get(src) for src, dst in relay_later.items()})
    choice = []
    for device in range(n):
        spot = (device + shift) % n
        t, r = spot // NR, spot % NR
        row = []
        for dt, dr in ((-1, 0), (1, 0), (0, -1), (0, 1)):
            found = -1
            if 0 <= t + dt < times and 0 <= r + dr < NR:
                wanted = at(t + dt, r + dr)
                found = [i for i, s in enumerate(SOURCES) if held[s].get(device) == wanted][0]
            row.append(found)
        choice.append(row)
    for move in moves.values():
        assert len(set(move.values())) == len(move)
    pairs = {name: sorted(move.items()) for name, move in moves.items()}
    return pairs, [int(d in relay_later) for d in range(n)], choice


def pack_kernel(start, counts, k, v, out, limits, sems):
    rows, width = k.shape[0], out.shape[1]
    cols = pl.ds(start, width)
    copies = [
        pltpu.make_async_copy(k.at[:, cols], out.at[pl.ds(0, rows)], sems.at[0]),
        pltpu.make_async_copy(v.at[:, cols], out.at[pl.ds(rows + PAD_ROWS, rows)], sems.at[1]),
        pltpu.make_async_copy(limits, out.at[pl.ds(rows, PAD_ROWS)], sems.at[2]),
    ]
    copies[0].start()
    copies[1].start()
    row = lax.broadcasted_iota(jnp.int32, limits.shape, 0)
    value = jnp.where(row == 0, counts[0], jnp.where(row == 1, counts[1], 0))
    limits[...] = value.astype(jnp.float32).astype(limits.dtype)
    copies[2].start()
    for copy in copies:
        copy.wait()


def pack(start, width, counts, k, v):
    rows = k.shape[0]
    anywhere = pl.BlockSpec(memory_space=pl.ANY)
    return pl.pallas_call(
        functools.partial(pack_kernel, start),
        in_specs=[pl.BlockSpec(memory_space=pltpu.SMEM), anywhere, anywhere],
        out_specs=anywhere,
        out_shape=jax.ShapeDtypeStruct((2 * rows + PAD_ROWS, width), k.dtype),
        scratch_shapes=[pltpu.VMEM((PAD_ROWS, width), k.dtype), pltpu.SemaphoreType.DMA((3,))],
        compiler_params=pltpu.CompilerParams(vmem_limit_bytes=VMEM_BYTES),
        name="pack_chunk",
    )(counts, k, v)


def choose_kernel(second, a, b, first_out, last_out, sems):
    rows = first_out.shape[0]

    def move(ref):
        copies = [
            pltpu.make_async_copy(ref.at[pl.ds(0, rows)], first_out, sems.at[0]),
            pltpu.make_async_copy(ref.at[pl.ds(rows, last_out.shape[0])], last_out, sems.at[1]),
        ]
        for copy in copies:
            copy.start()
        for copy in copies:
            copy.wait()

    pl.when(second[0] == 0)(lambda: move(a))
    pl.when(second[0] != 0)(lambda: move(b))


def choose(second, a, b, rows):
    anywhere = pl.BlockSpec(memory_space=pl.ANY)
    shapes = [
        jax.ShapeDtypeStruct((part, a.shape[1]), a.dtype) for part in (rows, a.shape[0] - rows)
    ]
    return pl.pallas_call(
        choose_kernel,
        in_specs=[pl.BlockSpec(memory_space=pltpu.SMEM), anywhere, anywhere],
        out_specs=[pl.BlockSpec(memory_space=pltpu.VMEM)] * 2,
        out_shape=shapes,
        scratch_shapes=[pltpu.SemaphoreType.DMA((2,))],
        compiler_params=pltpu.CompilerParams(vmem_limit_bytes=VMEM_BYTES),
        name="choose_relayed",
    )(second, a, b)


def dot_nt(a, b):
    return lax.dot_general(a, b, (((1,), (1,)), ((), ())), preferred_element_type=jnp.float32)


def dot_nn(a, b):
    return jnp.dot(a, b, preferred_element_type=jnp.float32)


def lane_tiles(x):
    return [x[:, i : i + HD] for i in range(0, x.shape[1], HD)]


def row_reduce(op, final, pieces):
    tiles = [tile for piece in pieces for tile in lane_tiles(piece)]
    return final(functools.reduce(op, tiles), axis=1, keepdims=True)


TABLE_COUNTS, TABLE_BESIDE, TABLE_TEXT, TABLE_CHOICE = 4, 6, 8, 9


def video_kernel(table, q, k_own, v_own, *rest):
    packed = {"earlier": rest[0], "later": rest[1]}
    relayed_k, relayed_v, beside_k, beside_v, text_k, text_v = rest[2:8]
    out, k_all, v_all, bias_all = rest[-4:]
    tok = q.shape[0] // 2
    text = text_k.shape[0]
    scale = LOG2E / math.sqrt(HD)
    near = BLOCKS * tok
    dead = 2 * BLOCKS
    lane = lax.broadcasted_iota(jnp.int32, (8, tok), 1)
    lane_f = lane.astype(jnp.float32)

    def put(block, k, v, v_row):
        for i in range(STEP_HEADS):
            cols = pl.ds(i * HD, HD)
            for c in range(2):
                rows = pl.ds((c * BLOCKS + block) * tok, tok)
                k_all[i, rows, :] = k[pl.ds(c * tok, tok), cols]
                v_all[i, rows, :] = v[pl.ds(v_row + c * tok, tok), cols]

    def put_limits(block, tail):
        limits = tail[...].astype(jnp.float32)
        for c in range(2):
            bias_all[c * BLOCKS + block] = jnp.where(lane_f < limits[c : c + 1, :], 0.0, -jnp.inf)

    def put_counts(block, at):
        for c in range(2):
            bias_all[c * BLOCKS + block] = jnp.where(lane < table[at + c], 0.0, -jnp.inf)

    put(0, k_own, v_own, 0)
    put_counts(0, TABLE_COUNTS)
    tail = (pl.ds(2 * tok, PAD_ROWS), pl.ds(0, HD))
    options = {1: ("earlier",), 2: ("later",), 3: ("earlier",), 4: ("later",)}
    zeros = jnp.zeros((tok, HD), k_all.dtype)
    for block in range(1, BLOCKS):
        chosen = table[TABLE_CHOICE + block - 1]
        for name in options[block]:

            @pl.when(chosen == SOURCES.index(name))
            def _(ref=packed[name], block=block):
                put(block, ref, ref, 2 * tok + PAD_ROWS)
                put_limits(block, ref.at[tail])

        @pl.when(chosen == SOURCES.index("relayed"))
        def _(block=block):
            put(block, relayed_k, relayed_v, 0)
            put_limits(block, relayed_k.at[tail])

        if block > 2:

            @pl.when(chosen == SOURCES.index("beside"))
            def _(block=block):
                put(block, beside_k, beside_v, 0)
                put_counts(block, TABLE_BESIDE)

        @pl.when(chosen < 0)
        def _(block=block):
            for c in range(2):
                bias_all[c * BLOCKS + block] = jnp.full((8, tok), -jnp.inf, jnp.float32)
                for i in range(STEP_HEADS):
                    rows = pl.ds((c * BLOCKS + block) * tok, tok)
                    k_all[i, rows, :] = zeros
                    v_all[i, rows, :] = zeros

    bias_all[dead] = jnp.full((8, tok), -jnp.inf, jnp.float32)
    for i in range(STEP_HEADS):
        k_all[i, pl.ds(dead * tok, tok), :] = zeros
        v_all[i, pl.ds(dead * tok, tok), :] = zeros

    text_lane = lax.broadcasted_iota(jnp.int32, (1, text), 1)
    text_bias = jnp.where(text_lane < table[TABLE_TEXT], 0.0, -jnp.inf)
    slot = lax.broadcasted_iota(jnp.int32, (tok, 1), 0)
    for i in range(STEP_HEADS):
        cols = pl.ds(i * HD, HD)
        for c in range(2):
            query = q[pl.ds(c * tok, tok), cols]
            fixed = pl.ds(c * near, near)
            fixed_bias = jnp.concatenate(
                [bias_all[c * BLOCKS + b][0:1] for b in range(BLOCKS)], axis=1
            )
            scores = [dot_nt(query, k_all[i, fixed, :]) + fixed_bias]
            values = [v_all[i, fixed, :]]
            for j in range(2):
                cell = table[2 * c + j]
                rows = pl.ds(pl.multiple_of(cell * tok, tok), tok)
                scores.append(dot_nt(query, k_all[i, rows, :]) + bias_all[cell][0:1])
                values.append(v_all[i, rows, :])
            scores.append(dot_nt(query, text_k[:, cols]) + text_bias)
            values.append(text_v[:, cols])
            top = row_reduce(jnp.maximum, jnp.max, scores)
            probs = [jnp.exp2((s - top) * scale) for s in scores]
            denom = row_reduce(jnp.add, jnp.sum, probs)
            acc = sum(dot_nn(p.astype(jnp.bfloat16), v) for p, v in zip(probs, values))
            valid = slot < table[TABLE_COUNTS + c]
            out[pl.ds(c * tok, tok), cols] = jnp.where(valid, acc / denom, 0.0).astype(out.dtype)


def video_call(first, heads, table, q, k, v, near, text_k, text_v, carried):
    rows, width = q.shape
    text = text_k.shape[0]
    tok = rows // 2
    step = STEP_HEADS * HD
    base = first // STEP_HEADS
    whole = lambda h: (0, base + h)
    part = lambda h: (0, h)
    own_spec = pl.BlockSpec((rows, step), whole)
    part_spec = pl.BlockSpec((2 * rows + PAD_ROWS, step), part)
    text_spec = pl.BlockSpec((text, step), whole)
    in_specs = [pl.BlockSpec(memory_space=pltpu.SMEM), own_spec, own_spec, own_spec]
    in_specs += [part_spec] * 2
    in_specs += [pl.BlockSpec((rows + PAD_ROWS, step), part), pl.BlockSpec((rows, step), part)]
    in_specs += [own_spec] * 2 + [text_spec] * 2
    operands = [table, q, k, v, *near, text_k, text_v]
    aliases = {}
    if carried is not None:
        aliases = {len(operands): 0}
        operands.append(carried)
        in_specs.append(pl.BlockSpec(memory_space=pl.ANY))
    cells = 2 * BLOCKS + 1
    keys = 7 * tok + text
    return pl.pallas_call(
        video_kernel,
        grid=(heads // STEP_HEADS,),
        in_specs=in_specs,
        out_specs=own_spec,
        out_shape=jax.ShapeDtypeStruct((rows, width), q.dtype),
        scratch_shapes=[
            pltpu.VMEM((STEP_HEADS, cells * tok, HD), q.dtype),
            pltpu.VMEM((STEP_HEADS, cells * tok, HD), q.dtype),
            pltpu.VMEM((cells, 8, tok), jnp.float32),
        ],
        input_output_aliases=aliases,
        compiler_params=pltpu.CompilerParams(vmem_limit_bytes=VMEM_BYTES),
        cost_estimate=pl.CostEstimate(
            flops=heads * rows * keys * HD // 4,
            bytes_accessed=heads * rows * HD,
            transcendentals=0,
        ),
        name="video_attention",
    )(*operands)


STAT_SUMS = 32
PAIR_HEADS = HEADS // 2


def text_kernel(order, counts, q, k, v, k_beside, v_beside, keep, send, top, denom):
    step = pl.program_id(0)
    rows = k.shape[0]
    text = q.shape[0]
    half = text // 2
    places = order.shape[0] - 1
    share = text // places
    lane = lax.broadcasted_iota(jnp.int32, (text, HD), 1)

    @pl.when(step == 0)
    def _():
        top[...] = jnp.zeros_like(top)
        denom[...] = jnp.zeros_like(denom)

    @pl.when(step < PAIR_HEADS // STEP_HEADS)
    def _():
        slot = lax.broadcasted_iota(jnp.int32, (1, rows // 2), 1)
        bias = [
            jnp.concatenate(
                [jnp.where(slot < counts[at + c], 0.0, -jnp.inf) for c in range(2)], axis=1
            )
            for at in (0, 2)
        ]
        for i in range(STEP_HEADS):
            cols = pl.ds(i * HD, HD)
            head = step * STEP_HEADS + i
            query = jnp.concatenate(
                [
                    q[pl.ds(pl.multiple_of(order[j] * share, share), share), cols]
                    for j in range(places)
                ],
                axis=0,
            )
            scores = [
                dot_nt(query, keys[:, cols]) * (1.0 / math.sqrt(HD)) + bound
                for keys, bound in zip((k, k_beside), bias)
            ]
            m = row_reduce(jnp.maximum, jnp.max, scores)
            weights = [jnp.exp(s - m) for s in scores]
            l = row_reduce(jnp.add, jnp.sum, weights)
            acc = 0.0
            for w, values in zip(weights, (v, v_beside)):
                high = w.astype(jnp.bfloat16)
                low = (w - high.astype(jnp.float32)).astype(jnp.bfloat16)
                acc = acc + dot_nn(high, values[:, cols]) + dot_nn(low, values[:, cols])
            top[...] = jnp.where(lane == head, m, top[...])
            denom[...] = jnp.where(lane == head + STAT_SUMS, l, denom[...])
            keep[:, cols] = acc[:half]
            send[:, cols] = acc[half:]

    @pl.when(step == PAIR_HEADS // STEP_HEADS)
    def _():
        stats = top[...] + denom[...]
        keep[:, pl.ds(0, HD)] = stats[:half]
        send[:, pl.ds(0, HD)] = stats[half:]


def text_local(order, counts, q, k, v, k_beside, v_beside):
    text = q.shape[0]
    rows = k.shape[0]
    step = STEP_HEADS * HD
    last = PAIR_HEADS // STEP_HEADS - 1
    at = lambda h, order, counts: (0, order[order.shape[0] - 1] + jnp.minimum(h, last))
    k_spec = pl.BlockSpec((rows, step), at)
    out_spec = pl.BlockSpec((text // 2, step), lambda h, order, counts: (0, h))
    shape = jax.ShapeDtypeStruct((text // 2, PAIR_HEADS * HD + step), jnp.float32)
    return pl.pallas_call(
        text_kernel,
        grid_spec=pltpu.PrefetchScalarGridSpec(
            num_scalar_prefetch=2,
            grid=(last + 2,),
            in_specs=[pl.BlockSpec((text, step), at)] + [k_spec] * 4,
            out_specs=[out_spec, out_spec],
            scratch_shapes=[pltpu.VMEM((text, HD), jnp.float32)] * 2,
        ),
        out_shape=[shape, shape],
        compiler_params=pltpu.CompilerParams(vmem_limit_bytes=VMEM_BYTES),
        cost_estimate=pl.CostEstimate(
            flops=text * rows * HD, bytes_accessed=text * HEADS * HD, transcendentals=0
        ),
        name="text_partials",
    )(order, counts, q, k, v, k_beside, v_beside)


def merge_kernel(finish, *refs):
    width = PAIR_HEADS * HD
    stat_cols = pl.ds(width, HD)
    keep, got = refs[:2]
    mine = keep[:, stat_cols]
    theirs = got[:, stat_cols]
    lane = lax.broadcasted_iota(jnp.int32, mine.shape, 1)
    is_top = lane < STAT_SUMS
    top = jnp.maximum(mine, theirs)
    a = jnp.exp(jnp.where(is_top, mine - top, 0.0))
    b = jnp.exp(jnp.where(is_top, theirs - top, 0.0))
    first, second = refs[-2:]
    half = first.shape[0]
    stats = jnp.where(is_top, top, 0.0)
    for h in range(PAIR_HEADS):
        cols = pl.ds(h * HD, HD)
        at = slice(h, h + 1)
        to = slice(STAT_SUMS + h, STAT_SUMS + h + 1)
        total = mine[:, to] * a[:, at] + theirs[:, to] * b[:, at]
        acc = keep[:, cols] * a[:, at] + got[:, cols] * b[:, at]
        if finish:
            acc = acc / total
        else:
            stats = jnp.where(lane == STAT_SUMS + h, total, stats)
        first[:, cols] = acc[:half].astype(first.dtype)
        second[:, cols] = acc[half:].astype(second.dtype)
    if not finish:
        first[:, stat_cols] = stats[:half]
        second[:, stat_cols] = stats[half:]


def text_merge(keep, got):
    shape = jax.ShapeDtypeStruct((keep.shape[0] // 2, (PAIR_HEADS + 1) * HD), jnp.float32)
    return pl.pallas_call(
        functools.partial(merge_kernel, False),
        out_shape=[shape, shape],
        compiler_params=pltpu.CompilerParams(vmem_limit_bytes=VMEM_BYTES),
        name="text_merge",
    )(keep, got)


def text_finish(keep, got):
    shape = jax.ShapeDtypeStruct((keep.shape[0] // 2, PAIR_HEADS * HD), jnp.bfloat16)
    return pl.pallas_call(
        functools.partial(merge_kernel, True),
        out_shape=[shape, shape],
        compiler_params=pltpu.CompilerParams(vmem_limit_bytes=VMEM_BYTES),
        name="text_finish",
    )(keep, got)


def text_order(n, base):
    masks = (4, 8, 1, 2)
    owners = [sum(mask for j, mask in enumerate(masks) if i >> (3 - j) & 1) for i in range(n)]
    order = jnp.array(owners, jnp.int32) ^ base
    first = base % 2 * (PAIR_HEADS // STEP_HEADS)
    return jnp.concatenate([order, first[None]])


def text_plain(position, n, text_count, q, k, v, counts):
    text, width = q.shape
    share = text // n
    keys = k.reshape(-1, HEADS, HD)
    values = v.reshape(-1, HEADS, HD)
    slots = jnp.arange(k.shape[0] // counts.shape[0], dtype=jnp.int32)
    valid = (slots[None, :] < counts[:, None]).reshape(-1)
    scores = jnp.einsum(
        "qhd,khd->hqk", q.reshape(text, HEADS, HD), keys, preferred_element_type=jnp.float32
    ) * (1.0 / math.sqrt(HD))
    scores = jnp.where(valid[None, None, :], scores, -jnp.inf)
    top = lax.pmax(jnp.max(scores, axis=-1), "tiles")
    weights = jnp.exp(scores - top[..., None])
    denom = jnp.sum(weights, axis=-1).T
    numer = jnp.einsum(
        "hqk,khd->qhd", weights.astype(jnp.bfloat16), values, preferred_element_type=jnp.float32
    ).reshape(text, width)
    numer = lax.psum_scatter(numer, "tiles", scatter_dimension=0, tiled=True)
    denom = lax.psum_scatter(denom, "tiles", scatter_dimension=0, tiled=True)
    result = numer.reshape(share, HEADS, HD) / denom[:, :, None]
    row_ids = position * share + jnp.arange(share, dtype=jnp.int32)
    result = jnp.where((row_ids < text_count[0])[:, None, None], result, 0.0)
    return result.astype(jnp.bfloat16).reshape(share, width)


def make_table(window, counts, counts_beside, text_count, choices, position):
    columns = counts.shape[0]
    extra = (window % 3 != 0) | (window == 0)
    rank = jnp.cumsum(extra.astype(jnp.int32), axis=1) * extra
    codes = jnp.stack([jnp.sum(jnp.where(rank == j, window, 0), axis=1) for j in (1, 2)], axis=1)
    cells = codes + (codes >= 1)
    own = jnp.arange(columns, dtype=jnp.int32)[:, None]
    column = own + cells % 3 - 1
    inside = (column >= 0) & (column < columns)
    extra_cells = jnp.where(inside, column * BLOCKS + cells // 3, columns * BLOCKS)
    chosen = lax.dynamic_index_in_dim(jnp.array(choices, jnp.int32), position, 0, False)
    parts = [extra_cells.reshape(-1), counts, counts_beside, text_count, chosen]
    return jnp.concatenate([part.astype(jnp.int32) for part in parts])


def tie(value, *others):
    return lax.optimization_barrier((value, *others))[0]


def per_device(n, video_q, video_k, video_v, text_q, text_k, text_v, window, counts, text_count):
    rows, width = video_q.shape
    text = text_q.shape[0]
    position = lax.axis_index("tiles").astype(jnp.int32)
    pairs, relays_later, choices = plan_moves(n)
    sends_later = jnp.array(relays_later, jnp.int32)[position][None]

    starts = [sum(CHUNK_HEADS[:i]) for i in range(len(CHUNK_HEADS))]
    direct, outs = [], []

    def send(i, *before):
        chunk = pack(starts[i] * HD, CHUNK_HEADS[i] * HD, counts, video_k, video_v)
        mine = tie(chunk, *before)
        direct.append([lax.ppermute(mine, "tiles", pairs[x]) for x in ("earlier", "later")])

    send(0)
    beside = [
        lax.ppermute(x, "tiles", pairs["beside"]) for x in (counts, video_k, video_v)
    ]
    table = make_table(window, counts, beside[0], text_count, choices, position)
    halving = text % (PAD_ROWS * n) == 0 and n == 16
    lower = [d for d in range(n) if not d & 2]
    upper = [d for d in range(n) if d & 2]
    parts = []
    if halving:
        both = jnp.concatenate([counts, beside[0]])
        order = text_order(n, position | 2)
        partial = text_local(order, both, text_q, video_k, video_v, *beside[1:])
        halves = []
        for half in partial:
            got = lax.ppermute(half, "tiles", [(d, d | 2) for d in lower])
            halves.append(jnp.concatenate(text_merge(half, got), axis=0))
        parts.append(halves)

    def merge(*before):
        i = len(parts)
        if 0 < i < 3:
            got = lax.ppermute(parts[-1][1], "tiles", [(d, d ^ (2 << i)) for d in upper])
            keep = tie(parts[-1][0], *before)
            parts.append(text_merge(keep, got) if i == 1 else text_finish(keep, got))

    count = len(CHUNK_HEADS)
    for i in range(count):
        before = outs[i - 1 : i] + ([parts[-1][0]] if halving and i == 0 else [])
        if i + 1 < count:
            send(i + 1, *direct[i], *before)
        up, down = tie(direct[i][0], *before), tie(direct[i][1], *before)
        relays = [
            lax.ppermute(half, "tiles", pairs["relayed"])
            for half in choose(sends_later, up, down, rows + PAD_ROWS)
        ]
        outs.append(
            video_call(
                starts[i], CHUNK_HEADS[i], table, video_q, video_k, video_v,
                [*direct[i], *relays, *beside[1:]], text_k, text_v, outs[-1] if outs else None,
            )
        )
        if i == 0:
            merge(*relays)
        elif i + 1 == count:
            merge(*relays)
    if halving:
        mine, leave = parts[-1]
        got = lax.ppermute(leave, "tiles", [(d, d ^ 1) for d in range(n)])
        low, high = jnp.concatenate([mine, got], axis=1), jnp.concatenate([got, mine], axis=1)
        ready = jnp.where(position % 2 == 0, low, high)
        share = text // n
        handed = lax.ppermute(ready[share:], "tiles", [(d, d ^ 2) for d in upper])
        rows_valid = position * share + jnp.arange(share, dtype=jnp.int32) < text_count[0]
        text_out = jnp.where((position & 2) == 0, handed, ready[:share])
        text_out = jnp.where(rows_valid[:, None], text_out, 0)
    if not halving:
        text_out = text_plain(position, n, text_count, text_q, video_k, video_v, counts)
    return (outs[-1], text_out)


def solution(mesh):
    tiles = mesh.shape["tiles"]
    return jax.shard_map(
        functools.partial(per_device, tiles),
        mesh=mesh,
        in_specs=(
            P(("groups", "tiles"), None),
            P(("groups", "tiles"), None),
            P(("groups", "tiles"), None),
            P("groups", None),
            P("groups", None),
            P("groups", None),
            P("tiles", None),
            P(("groups", "tiles")),
            P("groups"),
        ),
        out_specs=(P(("groups", "tiles"), None), P(("groups", "tiles"), None)),
        check_vma=False,
    )
```

```python
import functools
import math

import jax
import jax.numpy as jnp
from jax import lax
from jax.experimental import pallas as pl
from jax.experimental.pallas import tpu as pltpu
from jax.sharding import PartitionSpec as P

HEADS = 24
HD = 128
NR = 4
BLOCKS = 5
STEP_HEADS = 2
CHUNK_HEADS = (14, 8, 2)
PAD_ROWS = 16
VMEM_BYTES = 48 * 1024 * 1024
LOG2E = 1.4426950408889634
SOURCES = ("own", "earlier", "later", "relayed", "beside")


def spot_shift(n):
    return n // 2 + NR + NR // 2


def plan_moves(n):
    shift, times = spot_shift(n), n // NR
    last = times - 1

    def at(t, r):
        return (t * NR + r - shift) % n

    moves = {
        "earlier": {at(t - 1, r): at(t, r) for t in range(1, times) for r in range(NR)},
        "later": {at(t + 1, r): at(t, r) for t in range(last) for r in range(NR)},
        "beside": {at(t, r): at(t, r ^ 1) for t in range(times) for r in range(NR)},
    }
    relay_earlier = {at(t + 1, 1): at(t, 2) for t in range(last)}
    relay_later = {at(t - 1, 2): at(t, 1) for t in range(1, times)}
    moves["later"][at(0, 2)] = at(last, 2)
    relay_later[at(last, 2)] = at(0, 1)
    moves["earlier"][at(last, 1)] = at(0, 1)
    relay_earlier[at(0, 1)] = at(last, 2)
    assert not set(relay_earlier) & set(relay_later)
    moves["relayed"] = {**relay_earlier, **relay_later}
    held = {"own": {d: d for d in range(n)}}
    for name in ("earlier", "later", "beside"):
        held[name] = {dst: src for src, dst in moves[name].items()}
    held["relayed"] = {dst: held["earlier"].get(src) for src, dst in relay_earlier.items()}
    held["relayed"].update({dst: held["later"].get(src) for src, dst in relay_later.items()})
    choice = []
    for device in range(n):
        spot = (device + shift) % n
        t, r = spot // NR, spot % NR
        row = []
        for dt, dr in ((-1, 0), (1, 0), (0, -1), (0, 1)):
            found = -1
            if 0 <= t + dt < times and 0 <= r + dr < NR:
                wanted = at(t + dt, r + dr)
                found = [i for i, s in enumerate(SOURCES) if held[s].get(device) == wanted][0]
            row.append(found)
        choice.append(row)
    for move in moves.values():
        assert len(set(move.values())) == len(move)
    pairs = {name: sorted(move.items()) for name, move in moves.items()}
    return pairs, [int(d in relay_later) for d in range(n)], choice


def pack_kernel(start, counts, k, v, out, limits, sems):
    rows, width = k.shape[0], out.shape[1]
    cols = pl.ds(start, width)
    copies = [
        pltpu.make_async_copy(k.at[:, cols], out.at[pl.ds(0, rows)], sems.at[0]),
        pltpu.make_async_copy(v.at[:, cols], out.at[pl.ds(rows + PAD_ROWS, rows)], sems.at[1]),
        pltpu.make_async_copy(limits, out.at[pl.ds(rows, PAD_ROWS)], sems.at[2]),
    ]
    copies[0].start()
    copies[1].start()
    row = lax.broadcasted_iota(jnp.int32, limits.shape, 0)
    value = jnp.where(row == 0, counts[0], jnp.where(row == 1, counts[1], 0))
    limits[...] = value.astype(jnp.float32).astype(limits.dtype)
    copies[2].start()
    for copy in copies:
        copy.wait()


def pack(start, width, counts, k, v):
    rows = k.shape[0]
    anywhere = pl.BlockSpec(memory_space=pl.ANY)
    return pl.pallas_call(
        functools.partial(pack_kernel, start),
        in_specs=[pl.BlockSpec(memory_space=pltpu.SMEM), anywhere, anywhere],
        out_specs=anywhere,
        out_shape=jax.ShapeDtypeStruct((2 * rows + PAD_ROWS, width), k.dtype),
        scratch_shapes=[pltpu.VMEM((PAD_ROWS, width), k.dtype), pltpu.SemaphoreType.DMA((3,))],
        compiler_params=pltpu.CompilerParams(vmem_limit_bytes=VMEM_BYTES),
        name="pack_chunk",
    )(counts, k, v)


def choose_kernel(second, a, b, first_out, last_out, sems):
    rows = first_out.shape[0]

    def move(ref):
        copies = [
            pltpu.make_async_copy(ref.at[pl.ds(0, rows)], first_out, sems.at[0]),
            pltpu.make_async_copy(ref.at[pl.ds(rows, last_out.shape[0])], last_out, sems.at[1]),
        ]
        for copy in copies:
            copy.start()
        for copy in copies:
            copy.wait()

    pl.when(second[0] == 0)(lambda: move(a))
    pl.when(second[0] != 0)(lambda: move(b))


def choose(second, a, b, rows):
    anywhere = pl.BlockSpec(memory_space=pl.ANY)
    shapes = [
        jax.ShapeDtypeStruct((part, a.shape[1]), a.dtype) for part in (rows, a.shape[0] - rows)
    ]
    return pl.pallas_call(
        choose_kernel,
        in_specs=[pl.BlockSpec(memory_space=pltpu.SMEM), anywhere, anywhere],
        out_specs=[pl.BlockSpec(memory_space=pltpu.VMEM)] * 2,
        out_shape=shapes,
        scratch_shapes=[pltpu.SemaphoreType.DMA((2,))],
        compiler_params=pltpu.CompilerParams(vmem_limit_bytes=VMEM_BYTES),
        name="choose_relayed",
    )(second, a, b)


def dot_nt(a, b):
    return lax.dot_general(a, b, (((1,), (1,)), ((), ())), preferred_element_type=jnp.float32)


def dot_nn(a, b):
    return jnp.dot(a, b, preferred_element_type=jnp.float32)


def lane_tiles(x):
    return [x[:, i : i + HD] for i in range(0, x.shape[1], HD)]


def row_reduce(op, final, pieces):
    tiles = [tile for piece in pieces for tile in lane_tiles(piece)]
    return final(functools.reduce(op, tiles), axis=1, keepdims=True)


TABLE_COUNTS, TABLE_BESIDE, TABLE_TEXT, TABLE_CHOICE = 4, 6, 8, 9


def video_kernel(table, q, k_own, v_own, *rest):
    packed = {"earlier": rest[0], "later": rest[1]}
    relayed_k, relayed_v, beside_k, beside_v, text_k, text_v = rest[2:8]
    out, k_all, v_all, bias_all = rest[-4:]
    tok = q.shape[0] // 2
    text = text_k.shape[0]
    scale = LOG2E / math.sqrt(HD)
    near = BLOCKS * tok
    dead = 2 * BLOCKS
    lane = lax.broadcasted_iota(jnp.int32, (8, tok), 1)
    lane_f = lane.astype(jnp.float32)

    def put(block, k, v, v_row):
        for i in range(STEP_HEADS):
            cols = pl.ds(i * HD, HD)
            for c in range(2):
                rows = pl.ds((c * BLOCKS + block) * tok, tok)
                k_all[i, rows, :] = k[pl.ds(c * tok, tok), cols]
                v_all[i, rows, :] = v[pl.ds(v_row + c * tok, tok), cols]

    def put_limits(block, tail):
        limits = tail[...].astype(jnp.float32)
        for c in range(2):
            bias_all[c * BLOCKS + block] = jnp.where(lane_f < limits[c : c + 1, :], 0.0, -jnp.inf)

    def put_counts(block, at):
        for c in range(2):
            bias_all[c * BLOCKS + block] = jnp.where(lane < table[at + c], 0.0, -jnp.inf)

    put(0, k_own, v_own, 0)
    put_counts(0, TABLE_COUNTS)
    tail = (pl.ds(2 * tok, PAD_ROWS), pl.ds(0, HD))
    options = {1: ("earlier",), 2: ("later",), 3: ("earlier",), 4: ("later",)}
    zeros = jnp.zeros((tok, HD), k_all.dtype)
    for block in range(1, BLOCKS):
        chosen = table[TABLE_CHOICE + block - 1]
        for name in options[block]:

            @pl.when(chosen == SOURCES.index(name))
            def _(ref=packed[name], block=block):
                put(block, ref, ref, 2 * tok + PAD_ROWS)
                put_limits(block, ref.at[tail])

        @pl.when(chosen == SOURCES.index("relayed"))
        def _(block=block):
            put(block, relayed_k, relayed_v, 0)
            put_limits(block, relayed_k.at[tail])

        if block > 2:

            @pl.when(chosen == SOURCES.index("beside"))
            def _(block=block):
                put(block, beside_k, beside_v, 0)
                put_counts(block, TABLE_BESIDE)

        @pl.when(chosen < 0)
        def _(block=block):
            for c in range(2):
                bias_all[c * BLOCKS + block] = jnp.full((8, tok), -jnp.inf, jnp.float32)
                for i in range(STEP_HEADS):
                    rows = pl.ds((c * BLOCKS + block) * tok, tok)
                    k_all[i, rows, :] = zeros
                    v_all[i, rows, :] = zeros

    bias_all[dead] = jnp.full((8, tok), -jnp.inf, jnp.float32)
    for i in range(STEP_HEADS):
        k_all[i, pl.ds(dead * tok, tok), :] = zeros
        v_all[i, pl.ds(dead * tok, tok), :] = zeros

    text_lane = lax.broadcasted_iota(jnp.int32, (1, text), 1)
    text_bias = jnp.where(text_lane < table[TABLE_TEXT], 0.0, -jnp.inf)
    slot = lax.broadcasted_iota(jnp.int32, (tok, 1), 0)
    for i in range(STEP_HEADS):
        cols = pl.ds(i * HD, HD)
        for c in range(2):
            query = q[pl.ds(c * tok, tok), cols]
            fixed = pl.ds(c * near, near)
            fixed_bias = jnp.concatenate(
                [bias_all[c * BLOCKS + b][0:1] for b in range(BLOCKS)], axis=1
            )
            scores = [dot_nt(query, k_all[i, fixed, :]) + fixed_bias]
            values = [v_all[i, fixed, :]]
            for j in range(2):
                cell = table[2 * c + j]
                rows = pl.ds(pl.multiple_of(cell * tok, tok), tok)
                scores.append(dot_nt(query, k_all[i, rows, :]) + bias_all[cell][0:1])
                values.append(v_all[i, rows, :])
            scores.append(dot_nt(query, text_k[:, cols]) + text_bias)
            values.append(text_v[:, cols])
            top = row_reduce(jnp.maximum, jnp.max, scores)
            probs = [jnp.exp2((s - top) * scale) for s in scores]
            denom = row_reduce(jnp.add, jnp.sum, probs)
            acc = sum(dot_nn(p.astype(jnp.bfloat16), v) for p, v in zip(probs, values))
            valid = slot < table[TABLE_COUNTS + c]
            out[pl.ds(c * tok, tok), cols] = jnp.where(valid, acc / denom, 0.0).astype(out.dtype)


def video_call(first, heads, table, q, k, v, near, text_k, text_v, carried):
    rows, width = q.shape
    text = text_k.shape[0]
    tok = rows // 2
    step = STEP_HEADS * HD
    base = first // STEP_HEADS
    whole = lambda h: (0, base + h)
    part = lambda h: (0, h)
    own_spec = pl.BlockSpec((rows, step), whole)
    part_spec = pl.BlockSpec((2 * rows + PAD_ROWS, step), part)
    text_spec = pl.BlockSpec((text, step), whole)
    in_specs = [pl.BlockSpec(memory_space=pltpu.SMEM), own_spec, own_spec, own_spec]
    in_specs += [part_spec] * 2
    in_specs += [pl.BlockSpec((rows + PAD_ROWS, step), part), pl.BlockSpec((rows, step), part)]
    in_specs += [own_spec] * 2 + [text_spec] * 2
    operands = [table, q, k, v, *near, text_k, text_v]
    aliases = {}
    if carried is not None:
        aliases = {len(operands): 0}
        operands.append(carried)
        in_specs.append(pl.BlockSpec(memory_space=pl.ANY))
    cells = 2 * BLOCKS + 1
    keys = 7 * tok + text
    return pl.pallas_call(
        video_kernel,
        grid=(heads // STEP_HEADS,),
        in_specs=in_specs,
        out_specs=own_spec,
        out_shape=jax.ShapeDtypeStruct((rows, width), q.dtype),
        scratch_shapes=[
            pltpu.VMEM((STEP_HEADS, cells * tok, HD), q.dtype),
            pltpu.VMEM((STEP_HEADS, cells * tok, HD), q.dtype),
            pltpu.VMEM((cells, 8, tok), jnp.float32),
        ],
        input_output_aliases=aliases,
        compiler_params=pltpu.CompilerParams(vmem_limit_bytes=VMEM_BYTES),
        cost_estimate=pl.CostEstimate(
            flops=heads * rows * keys * HD // 4,
            bytes_accessed=heads * rows * HD,
            transcendentals=0,
        ),
        name="video_attention",
    )(*operands)


STAT_SUMS = 32
PAIR_HEADS = HEADS // 2


def text_kernel(order, counts, q, k, v, k_beside, v_beside, keep, send, top, denom):
    step = pl.program_id(0)
    rows = k.shape[0]
    text = q.shape[0]
    half = text // 2
    places = order.shape[0] - 1
    share = text // places
    lane = lax.broadcasted_iota(jnp.int32, (text, HD), 1)

    @pl.when(step == 0)
    def _():
        top[...] = jnp.zeros_like(top)
        denom[...] = jnp.zeros_like(denom)

    @pl.when(step < PAIR_HEADS // STEP_HEADS)
    def _():
        slot = lax.broadcasted_iota(jnp.int32, (1, rows // 2), 1)
        bias = [
            jnp.concatenate(
                [jnp.where(slot < counts[at + c], 0.0, -jnp.inf) for c in range(2)], axis=1
            )
            for at in (0, 2)
        ]
        for i in range(STEP_HEADS):
            cols = pl.ds(i * HD, HD)
            head = step * STEP_HEADS + i
            query = jnp.concatenate(
                [
                    q[pl.ds(pl.multiple_of(order[j] * share, share), share), cols]
                    for j in range(places)
                ],
                axis=0,
            )
            scores = [
                dot_nt(query, keys[:, cols]) * (1.0 / math.sqrt(HD)) + bound
                for keys, bound in zip((k, k_beside), bias)
            ]
            m = row_reduce(jnp.maximum, jnp.max, scores)
            weights = [jnp.exp(s - m) for s in scores]
            l = row_reduce(jnp.add, jnp.sum, weights)
            acc = 0.0
            for w, values in zip(weights, (v, v_beside)):
                high = w.astype(jnp.bfloat16)
                low = (w - high.astype(jnp.float32)).astype(jnp.bfloat16)
                acc = acc + dot_nn(high, values[:, cols]) + dot_nn(low, values[:, cols])
            top[...] = jnp.where(lane == head, m, top[...])
            denom[...] = jnp.where(lane == head + STAT_SUMS, l, denom[...])
            keep[:, cols] = acc[:half]
            send[:, cols] = acc[half:]

    @pl.when(step == PAIR_HEADS // STEP_HEADS)
    def _():
        stats = top[...] + denom[...]
        keep[:, pl.ds(0, HD)] = stats[:half]
        send[:, pl.ds(0, HD)] = stats[half:]


def text_local(order, counts, q, k, v, k_beside, v_beside):
    text = q.shape[0]
    rows = k.shape[0]
    step = STEP_HEADS * HD
    last = PAIR_HEADS // STEP_HEADS - 1
    at = lambda h, order, counts: (0, order[order.shape[0] - 1] + jnp.minimum(h, last))
    k_spec = pl.BlockSpec((rows, step), at)
    out_spec = pl.BlockSpec((text // 2, step), lambda h, order, counts: (0, h))
    shape = jax.ShapeDtypeStruct((text // 2, PAIR_HEADS * HD + step), jnp.float32)
    return pl.pallas_call(
        text_kernel,
        grid_spec=pltpu.PrefetchScalarGridSpec(
            num_scalar_prefetch=2,
            grid=(last + 2,),
            in_specs=[pl.BlockSpec((text, step), at)] + [k_spec] * 4,
            out_specs=[out_spec, out_spec],
            scratch_shapes=[pltpu.VMEM((text, HD), jnp.float32)] * 2,
        ),
        out_shape=[shape, shape],
        compiler_params=pltpu.CompilerParams(vmem_limit_bytes=VMEM_BYTES),
        cost_estimate=pl.CostEstimate(
            flops=text * rows * HD, bytes_accessed=text * HEADS * HD, transcendentals=0
        ),
        name="text_partials",
    )(order, counts, q, k, v, k_beside, v_beside)


def merge_kernel(finish, *refs):
    width = PAIR_HEADS * HD
    stat_cols = pl.ds(width, HD)
    keep, got = refs[:2]
    mine = keep[:, stat_cols]
    theirs = got[:, stat_cols]
    lane = lax.broadcasted_iota(jnp.int32, mine.shape, 1)
    is_top = lane < STAT_SUMS
    top = jnp.maximum(mine, theirs)
    a = jnp.exp(jnp.where(is_top, mine - top, 0.0))
    b = jnp.exp(jnp.where(is_top, theirs - top, 0.0))
    first, second = refs[-2:]
    half = first.shape[0]
    stats = jnp.where(is_top, top, 0.0)
    for h in range(PAIR_HEADS):
        cols = pl.ds(h * HD, HD)
        at = slice(h, h + 1)
        to = slice(STAT_SUMS + h, STAT_SUMS + h + 1)
        total = mine[:, to] * a[:, at] + theirs[:, to] * b[:, at]
        acc = keep[:, cols] * a[:, at] + got[:, cols] * b[:, at]
        if finish:
            acc = acc / total
        else:
            stats = jnp.where(lane == STAT_SUMS + h, total, stats)
        first[:, cols] = acc[:half].astype(first.dtype)
        second[:, cols] = acc[half:].astype(second.dtype)
    if not finish:
        first[:, stat_cols] = stats[:half]
        second[:, stat_cols] = stats[half:]


def text_merge(keep, got):
    shape = jax.ShapeDtypeStruct((keep.shape[0] // 2, (PAIR_HEADS + 1) * HD), jnp.float32)
    return pl.pallas_call(
        functools.partial(merge_kernel, False),
        out_shape=[shape, shape],
        compiler_params=pltpu.CompilerParams(vmem_limit_bytes=VMEM_BYTES),
        name="text_merge",
    )(keep, got)


def text_finish(keep, got):
    shape = jax.ShapeDtypeStruct((keep.shape[0] // 2, PAIR_HEADS * HD), jnp.bfloat16)
    return pl.pallas_call(
        functools.partial(merge_kernel, True),
        out_shape=[shape, shape],
        compiler_params=pltpu.CompilerParams(vmem_limit_bytes=VMEM_BYTES),
        name="text_finish",
    )(keep, got)


def text_order(n, base):
    masks = (4, 8, 1, 2)
    owners = [sum(mask for j, mask in enumerate(masks) if i >> (3 - j) & 1) for i in range(n)]
    order = jnp.array(owners, jnp.int32) ^ base
    first = base % 2 * (PAIR_HEADS // STEP_HEADS)
    return jnp.concatenate([order, first[None]])


def text_plain(position, n, text_count, q, k, v, counts):
    text, width = q.shape
    share = text // n
    keys = k.reshape(-1, HEADS, HD)
    values = v.reshape(-1, HEADS, HD)
    slots = jnp.arange(k.shape[0] // counts.shape[0], dtype=jnp.int32)
    valid = (slots[None, :] < counts[:, None]).reshape(-1)
    scores = jnp.einsum(
        "qhd,khd->hqk", q.reshape(text, HEADS, HD), keys, preferred_element_type=jnp.float32
    ) * (1.0 / math.sqrt(HD))
    scores = jnp.where(valid[None, None, :], scores, -jnp.inf)
    top = lax.pmax(jnp.max(scores, axis=-1), "tiles")
    weights = jnp.exp(scores - top[..., None])
    denom = jnp.sum(weights, axis=-1).T
    numer = jnp.einsum(
        "hqk,khd->qhd", weights.astype(jnp.bfloat16), values, preferred_element_type=jnp.float32
    ).reshape(text, width)
    numer = lax.psum_scatter(numer, "tiles", scatter_dimension=0, tiled=True)
    denom = lax.psum_scatter(denom, "tiles", scatter_dimension=0, tiled=True)
    result = numer.reshape(share, HEADS, HD) / denom[:, :, None]
    row_ids = position * share + jnp.arange(share, dtype=jnp.int32)
    result = jnp.where((row_ids < text_count[0])[:, None, None], result, 0.0)
    return result.astype(jnp.bfloat16).reshape(share, width)


def make_table(window, counts, counts_beside, text_count, choices, position):
    columns = counts.shape[0]
    extra = (window % 3 != 0) | (window == 0)
    rank = jnp.cumsum(extra.astype(jnp.int32), axis=1) * extra
    codes = jnp.stack([jnp.sum(jnp.where(rank == j, window, 0), axis=1) for j in (1, 2)], axis=1)
    cells = codes + (codes >= 1)
    own = jnp.arange(columns, dtype=jnp.int32)[:, None]
    column = own + cells % 3 - 1
    inside = (column >= 0) & (column < columns)
    extra_cells = jnp.where(inside, column * BLOCKS + cells // 3, columns * BLOCKS)
    chosen = lax.dynamic_index_in_dim(jnp.array(choices, jnp.int32), position, 0, False)
    parts = [extra_cells.reshape(-1), counts, counts_beside, text_count, chosen]
    return jnp.concatenate([part.astype(jnp.int32) for part in parts])


def tie(value, *others):
    return lax.optimization_barrier((value, *others))[0]


def per_device(n, video_q, video_k, video_v, text_q, text_k, text_v, window, counts, text_count):
    rows, width = video_q.shape
    text = text_q.shape[0]
    position = lax.axis_index("tiles").astype(jnp.int32)
    pairs, relays_later, choices = plan_moves(n)
    sends_later = jnp.array(relays_later, jnp.int32)[position][None]

    starts = [sum(CHUNK_HEADS[:i]) for i in range(len(CHUNK_HEADS))]
    direct, outs = [], []

    def send(i, *before):
        chunk = pack(starts[i] * HD, CHUNK_HEADS[i] * HD, counts, video_k, video_v)
        mine = tie(chunk, *before)
        direct.append([lax.ppermute(mine, "tiles", pairs[x]) for x in ("earlier", "later")])

    send(0)
    beside = [
        lax.ppermute(x, "tiles", pairs["beside"]) for x in (counts, video_k, video_v)
    ]
    table = make_table(window, counts, beside[0], text_count, choices, position)
    halving = text % (PAD_ROWS * n) == 0 and n == 16
    lower = [d for d in range(n) if not d & 2]
    upper = [d for d in range(n) if d & 2]
    parts = []
    if halving:
        both = jnp.concatenate([counts, beside[0]])
        order = text_order(n, position | 2)
        partial = text_local(order, both, text_q, video_k, video_v, *beside[1:])
        halves = []
        for half in partial:
            got = lax.ppermute(half, "tiles", [(d, d | 2) for d in lower])
            halves.append(jnp.concatenate(text_merge(half, got), axis=0))
        parts.append(halves)

    def merge(*before):
        i = len(parts)
        if 0 < i < 3:
            got = lax.ppermute(parts[-1][1], "tiles", [(d, d ^ (2 << i)) for d in upper])
            keep = tie(parts[-1][0], *before)
            parts.append(text_merge(keep, got) if i == 1 else text_finish(keep, got))

    count = len(CHUNK_HEADS)
    for i in range(count):
        before = outs[i - 1 : i] + (list(parts[-1]) if halving and i == 0 else [])
        if i + 1 < count:
            send(i + 1, *direct[i], *before)
        up, down = tie(direct[i][0], *before), tie(direct[i][1], *before)
        chosen = choose(sends_later, up, down, rows + PAD_ROWS)
        relays = [lax.ppermute(half, "tiles", pairs["relayed"]) for half in chosen]
        if halving and i < 2:
            merge(*chosen)
        if halving and i == 1:
            table = tie(table, parts[-1][0])
        outs.append(
            video_call(
                starts[i], CHUNK_HEADS[i], table, video_q, video_k, video_v,
                [*direct[i], *relays, *beside[1:]], text_k, text_v, outs[-1] if outs else None,
            )
        )
    if halving:
        mine, leave = parts[-1]
        got = lax.ppermute(leave, "tiles", [(d, d ^ 1) for d in range(n)])
        low, high = jnp.concatenate([mine, got], axis=1), jnp.concatenate([got, mine], axis=1)
        ready = jnp.where(position % 2 == 0, low, high)
        share = text // n
        handed = lax.ppermute(ready[share:], "tiles", [(d, d ^ 2) for d in upper])
        rows_valid = position * share + jnp.arange(share, dtype=jnp.int32) < text_count[0]
        text_out = jnp.where((position & 2) == 0, handed, ready[:share])
        text_out = jnp.where(rows_valid[:, None], text_out, 0)
    if not halving:
        text_out = text_plain(position, n, text_count, text_q, video_k, video_v, counts)
    return (outs[-1], text_out)


def solution(mesh):
    tiles = mesh.shape["tiles"]
    return jax.shard_map(
        functools.partial(per_device, tiles),
        mesh=mesh,
        in_specs=(
            P(("groups", "tiles"), None),
            P(("groups", "tiles"), None),
            P(("groups", "tiles"), None),
            P("groups", None),
            P("groups", None),
            P("groups", None),
            P("tiles", None),
            P(("groups", "tiles")),
            P("groups"),
        ),
        out_specs=(P(("groups", "tiles"), None), P(("groups", "tiles"), None)),
        check_vma=False,
    )
```

```python
import functools
import math

import jax
import jax.numpy as jnp
from jax import lax
from jax.experimental import pallas as pl
from jax.experimental.pallas import tpu as pltpu
from jax.sharding import PartitionSpec as P

HEADS = 24
HD = 128
NR = 4
BLOCKS = 5
STEP_HEADS = 2
CHUNK_HEADS = (14, 10)
PAD_ROWS = 16
VMEM_BYTES = 48 * 1024 * 1024
LOG2E = 1.4426950408889634
SOURCES = ("own", "earlier", "later", "relayed", "beside")


def spot_shift(n):
    return n // 2 + NR + NR // 2


def plan_moves(n):
    shift, times = spot_shift(n), n // NR
    last = times - 1

    def at(t, r):
        return (t * NR + r - shift) % n

    moves = {
        "earlier": {at(t - 1, r): at(t, r) for t in range(1, times) for r in range(NR)},
        "later": {at(t + 1, r): at(t, r) for t in range(last) for r in range(NR)},
        "beside": {at(t, r): at(t, r ^ 1) for t in range(times) for r in range(NR)},
    }
    relay_earlier = {at(t + 1, 1): at(t, 2) for t in range(last)}
    relay_later = {at(t - 1, 2): at(t, 1) for t in range(1, times)}
    moves["later"][at(0, 2)] = at(last, 2)
    relay_later[at(last, 2)] = at(0, 1)
    moves["earlier"][at(last, 1)] = at(0, 1)
    relay_earlier[at(0, 1)] = at(last, 2)
    assert not set(relay_earlier) & set(relay_later)
    moves["relayed"] = {**relay_earlier, **relay_later}
    held = {"own": {d: d for d in range(n)}}
    for name in ("earlier", "later", "beside"):
        held[name] = {dst: src for src, dst in moves[name].items()}
    held["relayed"] = {dst: held["earlier"].get(src) for src, dst in relay_earlier.items()}
    held["relayed"].update({dst: held["later"].get(src) for src, dst in relay_later.items()})
    choice = []
    for device in range(n):
        spot = (device + shift) % n
        t, r = spot // NR, spot % NR
        row = []
        for dt, dr in ((-1, 0), (1, 0), (0, -1), (0, 1)):
            found = -1
            if 0 <= t + dt < times and 0 <= r + dr < NR:
                wanted = at(t + dt, r + dr)
                found = [i for i, s in enumerate(SOURCES) if held[s].get(device) == wanted][0]
            row.append(found)
        choice.append(row)
    for move in moves.values():
        assert len(set(move.values())) == len(move)
    pairs = {name: sorted(move.items()) for name, move in moves.items()}
    return pairs, [int(d in relay_later) for d in range(n)], choice


def pack_kernel(start, counts, k, v, out, limits, sems):
    rows, width = k.shape[0], out.shape[1]
    cols = pl.ds(start, width)
    copies = [
        pltpu.make_async_copy(k.at[:, cols], out.at[pl.ds(0, rows)], sems.at[0]),
        pltpu.make_async_copy(v.at[:, cols], out.at[pl.ds(rows + PAD_ROWS, rows)], sems.at[1]),
        pltpu.make_async_copy(limits, out.at[pl.ds(rows, PAD_ROWS)], sems.at[2]),
    ]
    copies[0].start()
    copies[1].start()
    row = lax.broadcasted_iota(jnp.int32, limits.shape, 0)
    value = jnp.where(row == 0, counts[0], jnp.where(row == 1, counts[1], 0))
    limits[...] = value.astype(jnp.float32).astype(limits.dtype)
    copies[2].start()
    for copy in copies:
        copy.wait()


def pack(start, width, counts, k, v):
    rows = k.shape[0]
    anywhere = pl.BlockSpec(memory_space=pl.ANY)
    return pl.pallas_call(
        functools.partial(pack_kernel, start),
        in_specs=[pl.BlockSpec(memory_space=pltpu.SMEM), anywhere, anywhere],
        out_specs=anywhere,
        out_shape=jax.ShapeDtypeStruct((2 * rows + PAD_ROWS, width), k.dtype),
        scratch_shapes=[pltpu.VMEM((PAD_ROWS, width), k.dtype), pltpu.SemaphoreType.DMA((3,))],
        compiler_params=pltpu.CompilerParams(vmem_limit_bytes=VMEM_BYTES),
        name="pack_chunk",
    )(counts, k, v)


def choose_kernel(second, a, b, first_out, last_out, sems):
    rows = first_out.shape[0]

    def move(ref):
        copies = [
            pltpu.make_async_copy(ref.at[pl.ds(0, rows)], first_out, sems.at[0]),
            pltpu.make_async_copy(ref.at[pl.ds(rows, last_out.shape[0])], last_out, sems.at[1]),
        ]
        for copy in copies:
            copy.start()
        for copy in copies:
            copy.wait()

    pl.when(second[0] == 0)(lambda: move(a))
    pl.when(second[0] != 0)(lambda: move(b))


def choose(second, a, b, rows):
    anywhere = pl.BlockSpec(memory_space=pl.ANY)
    shapes = [
        jax.ShapeDtypeStruct((part, a.shape[1]), a.dtype) for part in (rows, a.shape[0] - rows)
    ]
    return pl.pallas_call(
        choose_kernel,
        in_specs=[pl.BlockSpec(memory_space=pltpu.SMEM), anywhere, anywhere],
        out_specs=[pl.BlockSpec(memory_space=pltpu.VMEM)] * 2,
        out_shape=shapes,
        scratch_shapes=[pltpu.SemaphoreType.DMA((2,))],
        compiler_params=pltpu.CompilerParams(vmem_limit_bytes=VMEM_BYTES),
        name="choose_relayed",
    )(second, a, b)


def dot_nt(a, b):
    return lax.dot_general(a, b, (((1,), (1,)), ((), ())), preferred_element_type=jnp.float32)


def dot_nn(a, b):
    return jnp.dot(a, b, preferred_element_type=jnp.float32)


def lane_tiles(x):
    return [x[:, i : i + HD] for i in range(0, x.shape[1], HD)]


def row_reduce(op, final, pieces):
    tiles = [tile for piece in pieces for tile in lane_tiles(piece)]
    return final(functools.reduce(op, tiles), axis=1, keepdims=True)


TABLE_COUNTS, TABLE_BESIDE, TABLE_TEXT, TABLE_CHOICE = 4, 6, 8, 9


def video_kernel(table, q, k_own, v_own, *rest):
    packed = {"earlier": rest[0], "later": rest[1]}
    relayed_k, relayed_v, beside_k, beside_v, text_k, text_v = rest[2:8]
    out, k_all, v_all, bias_all = rest[-4:]
    tok = q.shape[0] // 2
    text = text_k.shape[0]
    scale = LOG2E / math.sqrt(HD)
    near = BLOCKS * tok
    dead = 2 * BLOCKS
    lane = lax.broadcasted_iota(jnp.int32, (8, tok), 1)
    lane_f = lane.astype(jnp.float32)

    def put(block, k, v, v_row):
        for i in range(STEP_HEADS):
            cols = pl.ds(i * HD, HD)
            for c in range(2):
                rows = pl.ds((c * BLOCKS + block) * tok, tok)
                k_all[i, rows, :] = k[pl.ds(c * tok, tok), cols]
                v_all[i, rows, :] = v[pl.ds(v_row + c * tok, tok), cols]

    def put_limits(block, tail):
        limits = tail[...].astype(jnp.float32)
        for c in range(2):
            bias_all[c * BLOCKS + block] = jnp.where(lane_f < limits[c : c + 1, :], 0.0, -jnp.inf)

    def put_counts(block, at):
        for c in range(2):
            bias_all[c * BLOCKS + block] = jnp.where(lane < table[at + c], 0.0, -jnp.inf)

    put(0, k_own, v_own, 0)
    put_counts(0, TABLE_COUNTS)
    tail = (pl.ds(2 * tok, PAD_ROWS), pl.ds(0, HD))
    options = {1: ("earlier",), 2: ("later",), 3: ("earlier",), 4: ("later",)}
    zeros = jnp.zeros((tok, HD), k_all.dtype)
    for block in range(1, BLOCKS):
        chosen = table[TABLE_CHOICE + block - 1]
        for name in options[block]:

            @pl.when(chosen == SOURCES.index(name))
            def _(ref=packed[name], block=block):
                put(block, ref, ref, 2 * tok + PAD_ROWS)
                put_limits(block, ref.at[tail])

        @pl.when(chosen == SOURCES.index("relayed"))
        def _(block=block):
            put(block, relayed_k, relayed_v, 0)
            put_limits(block, relayed_k.at[tail])

        if block > 2:

            @pl.when(chosen == SOURCES.index("beside"))
            def _(block=block):
                put(block, beside_k, beside_v, 0)
                put_counts(block, TABLE_BESIDE)

        @pl.when(chosen < 0)
        def _(block=block):
            for c in range(2):
                bias_all[c * BLOCKS + block] = jnp.full((8, tok), -jnp.inf, jnp.float32)
                for i in range(STEP_HEADS):
                    rows = pl.ds((c * BLOCKS + block) * tok, tok)
                    k_all[i, rows, :] = zeros
                    v_all[i, rows, :] = zeros

    bias_all[dead] = jnp.full((8, tok), -jnp.inf, jnp.float32)
    for i in range(STEP_HEADS):
        k_all[i, pl.ds(dead * tok, tok), :] = zeros
        v_all[i, pl.ds(dead * tok, tok), :] = zeros

    text_lane = lax.broadcasted_iota(jnp.int32, (1, text), 1)
    text_bias = jnp.where(text_lane < table[TABLE_TEXT], 0.0, -jnp.inf)
    slot = lax.broadcasted_iota(jnp.int32, (tok, 1), 0)
    for i in range(STEP_HEADS):
        cols = pl.ds(i * HD, HD)
        for c in range(2):
            query = q[pl.ds(c * tok, tok), cols]
            fixed = pl.ds(c * near, near)
            fixed_bias = jnp.concatenate(
                [bias_all[c * BLOCKS + b][0:1] for b in range(BLOCKS)], axis=1
            )
            scores = [dot_nt(query, k_all[i, fixed, :]) + fixed_bias]
            values = [v_all[i, fixed, :]]
            for j in range(2):
                cell = table[2 * c + j]
                rows = pl.ds(pl.multiple_of(cell * tok, tok), tok)
                scores.append(dot_nt(query, k_all[i, rows, :]) + bias_all[cell][0:1])
                values.append(v_all[i, rows, :])
            scores.append(dot_nt(query, text_k[:, cols]) + text_bias)
            values.append(text_v[:, cols])
            top = row_reduce(jnp.maximum, jnp.max, scores)
            probs = [jnp.exp2((s - top) * scale) for s in scores]
            denom = row_reduce(jnp.add, jnp.sum, probs)
            acc = sum(dot_nn(p.astype(jnp.bfloat16), v) for p, v in zip(probs, values))
            valid = slot < table[TABLE_COUNTS + c]
            out[pl.ds(c * tok, tok), cols] = jnp.where(valid, acc / denom, 0.0).astype(out.dtype)


def video_call(first, heads, table, q, k, v, near, text_k, text_v, carried):
    rows, width = q.shape
    text = text_k.shape[0]
    tok = rows // 2
    step = STEP_HEADS * HD
    base = first // STEP_HEADS
    whole = lambda h: (0, base + h)
    part = lambda h: (0, h)
    own_spec = pl.BlockSpec((rows, step), whole)
    part_spec = pl.BlockSpec((2 * rows + PAD_ROWS, step), part)
    text_spec = pl.BlockSpec((text, step), whole)
    in_specs = [pl.BlockSpec(memory_space=pltpu.SMEM), own_spec, own_spec, own_spec]
    in_specs += [part_spec] * 2
    in_specs += [pl.BlockSpec((rows + PAD_ROWS, step), part), pl.BlockSpec((rows, step), part)]
    in_specs += [own_spec] * 2 + [text_spec] * 2
    operands = [table, q, k, v, *near, text_k, text_v]
    aliases = {}
    if carried is not None:
        aliases = {len(operands): 0}
        operands.append(carried)
        in_specs.append(pl.BlockSpec(memory_space=pl.ANY))
    cells = 2 * BLOCKS + 1
    keys = 7 * tok + text
    return pl.pallas_call(
        video_kernel,
        grid=(heads // STEP_HEADS,),
        in_specs=in_specs,
        out_specs=own_spec,
        out_shape=jax.ShapeDtypeStruct((rows, width), q.dtype),
        scratch_shapes=[
            pltpu.VMEM((STEP_HEADS, cells * tok, HD), q.dtype),
            pltpu.VMEM((STEP_HEADS, cells * tok, HD), q.dtype),
            pltpu.VMEM((cells, 8, tok), jnp.float32),
        ],
        input_output_aliases=aliases,
        compiler_params=pltpu.CompilerParams(vmem_limit_bytes=VMEM_BYTES),
        cost_estimate=pl.CostEstimate(
            flops=heads * rows * keys * HD // 4,
            bytes_accessed=heads * rows * HD,
            transcendentals=0,
        ),
        name="video_attention",
    )(*operands)


STAT_SUMS = 32
PAIR_HEADS = HEADS // 2


def text_kernel(order, counts, q, k, v, k_beside, v_beside, keep, send, top, denom):
    step = pl.program_id(0)
    rows = k.shape[0]
    text = q.shape[0]
    half = text // 2
    places = order.shape[0] - 1
    share = text // places
    lane = lax.broadcasted_iota(jnp.int32, (text, HD), 1)

    @pl.when(step == 0)
    def _():
        top[...] = jnp.zeros_like(top)
        denom[...] = jnp.zeros_like(denom)

    @pl.when(step < PAIR_HEADS // STEP_HEADS)
    def _():
        slot = lax.broadcasted_iota(jnp.int32, (1, rows // 2), 1)
        bias = [
            jnp.concatenate(
                [jnp.where(slot < counts[at + c], 0.0, -jnp.inf) for c in range(2)], axis=1
            )
            for at in (0, 2)
        ]
        for i in range(STEP_HEADS):
            cols = pl.ds(i * HD, HD)
            head = step * STEP_HEADS + i
            query = jnp.concatenate(
                [
                    q[pl.ds(pl.multiple_of(order[j] * share, share), share), cols]
                    for j in range(places)
                ],
                axis=0,
            )
            scores = [
                dot_nt(query, keys[:, cols]) * (1.0 / math.sqrt(HD)) + bound
                for keys, bound in zip((k, k_beside), bias)
            ]
            m = row_reduce(jnp.maximum, jnp.max, scores)
            weights = [jnp.exp(s - m) for s in scores]
            l = row_reduce(jnp.add, jnp.sum, weights)
            acc = 0.0
            for w, values in zip(weights, (v, v_beside)):
                high = w.astype(jnp.bfloat16)
                low = (w - high.astype(jnp.float32)).astype(jnp.bfloat16)
                acc = acc + dot_nn(high, values[:, cols]) + dot_nn(low, values[:, cols])
            top[...] = jnp.where(lane == head, m, top[...])
            denom[...] = jnp.where(lane == head + STAT_SUMS, l, denom[...])
            keep[:, cols] = acc[:half]
            send[:, cols] = acc[half:]

    @pl.when(step == PAIR_HEADS // STEP_HEADS)
    def _():
        stats = top[...] + denom[...]
        keep[:, pl.ds(0, HD)] = stats[:half]
        send[:, pl.ds(0, HD)] = stats[half:]


def text_local(order, counts, q, k, v, k_beside, v_beside):
    text = q.shape[0]
    rows = k.shape[0]
    step = STEP_HEADS * HD
    last = PAIR_HEADS // STEP_HEADS - 1
    at = lambda h, order, counts: (0, order[order.shape[0] - 1] + jnp.minimum(h, last))
    k_spec = pl.BlockSpec((rows, step), at)
    out_spec = pl.BlockSpec((text // 2, step), lambda h, order, counts: (0, h))
    shape = jax.ShapeDtypeStruct((text // 2, PAIR_HEADS * HD + step), jnp.float32)
    return pl.pallas_call(
        text_kernel,
        grid_spec=pltpu.PrefetchScalarGridSpec(
            num_scalar_prefetch=2,
            grid=(last + 2,),
            in_specs=[pl.BlockSpec((text, step), at)] + [k_spec] * 4,
            out_specs=[out_spec, out_spec],
            scratch_shapes=[pltpu.VMEM((text, HD), jnp.float32)] * 2,
        ),
        out_shape=[shape, shape],
        compiler_params=pltpu.CompilerParams(vmem_limit_bytes=VMEM_BYTES),
        cost_estimate=pl.CostEstimate(
            flops=text * rows * HD, bytes_accessed=text * HEADS * HD, transcendentals=0
        ),
        name="text_partials",
    )(order, counts, q, k, v, k_beside, v_beside)


def merge_kernel(finish, *refs):
    width = PAIR_HEADS * HD
    stat_cols = pl.ds(width, HD)
    keep, got = refs[:2]
    mine = keep[:, stat_cols]
    theirs = got[:, stat_cols]
    lane = lax.broadcasted_iota(jnp.int32, mine.shape, 1)
    is_top = lane < STAT_SUMS
    top = jnp.maximum(mine, theirs)
    a = jnp.exp(jnp.where(is_top, mine - top, 0.0))
    b = jnp.exp(jnp.where(is_top, theirs - top, 0.0))
    first, second = refs[-2:]
    half = first.shape[0]
    stats = jnp.where(is_top, top, 0.0)
    for h in range(PAIR_HEADS):
        cols = pl.ds(h * HD, HD)
        at = slice(h, h + 1)
        to = slice(STAT_SUMS + h, STAT_SUMS + h + 1)
        total = mine[:, to] * a[:, at] + theirs[:, to] * b[:, at]
        acc = keep[:, cols] * a[:, at] + got[:, cols] * b[:, at]
        if finish:
            acc = acc / total
        else:
            stats = jnp.where(lane == STAT_SUMS + h, total, stats)
        first[:, cols] = acc[:half].astype(first.dtype)
        second[:, cols] = acc[half:].astype(second.dtype)
    if not finish:
        first[:, stat_cols] = stats[:half]
        second[:, stat_cols] = stats[half:]


def text_merge(keep, got):
    shape = jax.ShapeDtypeStruct((keep.shape[0] // 2, (PAIR_HEADS + 1) * HD), jnp.float32)
    return pl.pallas_call(
        functools.partial(merge_kernel, False),
        out_shape=[shape, shape],
        compiler_params=pltpu.CompilerParams(vmem_limit_bytes=VMEM_BYTES),
        name="text_merge",
    )(keep, got)


def text_finish(keep, got):
    shape = jax.ShapeDtypeStruct((keep.shape[0] // 2, PAIR_HEADS * HD), jnp.bfloat16)
    return pl.pallas_call(
        functools.partial(merge_kernel, True),
        out_shape=[shape, shape],
        compiler_params=pltpu.CompilerParams(vmem_limit_bytes=VMEM_BYTES),
        name="text_finish",
    )(keep, got)


def text_order(n, base):
    masks = (4, 8, 1, 2)
    owners = [sum(mask for j, mask in enumerate(masks) if i >> (3 - j) & 1) for i in range(n)]
    order = jnp.array(owners, jnp.int32) ^ base
    first = base % 2 * (PAIR_HEADS // STEP_HEADS)
    return jnp.concatenate([order, first[None]])


def text_plain(position, n, text_count, q, k, v, counts):
    text, width = q.shape
    share = text // n
    keys = k.reshape(-1, HEADS, HD)
    values = v.reshape(-1, HEADS, HD)
    slots = jnp.arange(k.shape[0] // counts.shape[0], dtype=jnp.int32)
    valid = (slots[None, :] < counts[:, None]).reshape(-1)
    scores = jnp.einsum(
        "qhd,khd->hqk", q.reshape(text, HEADS, HD), keys, preferred_element_type=jnp.float32
    ) * (1.0 / math.sqrt(HD))
    scores = jnp.where(valid[None, None, :], scores, -jnp.inf)
    top = lax.pmax(jnp.max(scores, axis=-1), "tiles")
    weights = jnp.exp(scores - top[..., None])
    denom = jnp.sum(weights, axis=-1).T
    numer = jnp.einsum(
        "hqk,khd->qhd", weights.astype(jnp.bfloat16), values, preferred_element_type=jnp.float32
    ).reshape(text, width)
    numer = lax.psum_scatter(numer, "tiles", scatter_dimension=0, tiled=True)
    denom = lax.psum_scatter(denom, "tiles", scatter_dimension=0, tiled=True)
    result = numer.reshape(share, HEADS, HD) / denom[:, :, None]
    row_ids = position * share + jnp.arange(share, dtype=jnp.int32)
    result = jnp.where((row_ids < text_count[0])[:, None, None], result, 0.0)
    return result.astype(jnp.bfloat16).reshape(share, width)


def make_table(window, counts, counts_beside, text_count, choices, position):
    columns = counts.shape[0]
    extra = (window % 3 != 0) | (window == 0)
    rank = jnp.cumsum(extra.astype(jnp.int32), axis=1) * extra
    codes = jnp.stack([jnp.sum(jnp.where(rank == j, window, 0), axis=1) for j in (1, 2)], axis=1)
    cells = codes + (codes >= 1)
    own = jnp.arange(columns, dtype=jnp.int32)[:, None]
    column = own + cells % 3 - 1
    inside = (column >= 0) & (column < columns)
    extra_cells = jnp.where(inside, column * BLOCKS + cells // 3, columns * BLOCKS)
    chosen = lax.dynamic_index_in_dim(jnp.array(choices, jnp.int32), position, 0, False)
    parts = [extra_cells.reshape(-1), counts, counts_beside, text_count, chosen]
    return jnp.concatenate([part.astype(jnp.int32) for part in parts])


def tie(value, *others):
    return lax.optimization_barrier((value, *others))[0]


def per_device(n, video_q, video_k, video_v, text_q, text_k, text_v, window, counts, text_count):
    rows, width = video_q.shape
    text = text_q.shape[0]
    position = lax.axis_index("tiles").astype(jnp.int32)
    pairs, relays_later, choices = plan_moves(n)
    sends_later = jnp.array(relays_later, jnp.int32)[position][None]

    starts = [sum(CHUNK_HEADS[:i]) for i in range(len(CHUNK_HEADS))]
    direct, outs = [], []

    def send(i, *before):
        chunk = pack(starts[i] * HD, CHUNK_HEADS[i] * HD, counts, video_k, video_v)
        mine = tie(chunk, *before)
        direct.append([lax.ppermute(mine, "tiles", pairs[x]) for x in ("earlier", "later")])

    send(0)
    beside = [
        lax.ppermute(x, "tiles", pairs["beside"]) for x in (counts, video_k, video_v)
    ]
    table = make_table(window, counts, beside[0], text_count, choices, position)
    halving = text % (PAD_ROWS * n) == 0 and n == 16
    lower = [d for d in range(n) if not d & 2]
    upper = [d for d in range(n) if d & 2]
    parts = []
    if halving:
        both = jnp.concatenate([counts, beside[0]])
        order = text_order(n, position | 2)
        partial = text_local(order, both, text_q, video_k, video_v, *beside[1:])
        halves = []
        for half in partial:
            got = lax.ppermute(half, "tiles", [(d, d | 2) for d in lower])
            halves.append(jnp.concatenate(text_merge(half, got), axis=0))
        parts.append(halves)

    def merge(*before):
        i = len(parts)
        if 0 < i < 3:
            got = lax.ppermute(parts[-1][1], "tiles", [(d, d ^ (2 << i)) for d in upper])
            keep = tie(parts[-1][0], *before)
            parts.append(text_merge(keep, got) if i == 1 else text_finish(keep, got))

    count = len(CHUNK_HEADS)
    for i in range(count):
        before = outs[i - 1 : i] + (list(parts[-1]) if halving and i == 0 else [])
        if i + 1 < count:
            send(i + 1, *direct[i], *before)
        up, down = tie(direct[i][0], *before), tie(direct[i][1], *before)
        chosen = choose(sends_later, up, down, rows + PAD_ROWS)
        relays = [lax.ppermute(half, "tiles", pairs["relayed"]) for half in chosen]
        if halving and i < 2:
            merge(*chosen)
        if halving and i == 1:
            table = tie(table, parts[-1][0])
        outs.append(
            video_call(
                starts[i], CHUNK_HEADS[i], table, video_q, video_k, video_v,
                [*direct[i], *relays, *beside[1:]], text_k, text_v, outs[-1] if outs else None,
            )
        )
    if halving:
        mine, leave = parts[-1]
        got = lax.ppermute(leave, "tiles", [(d, d ^ 1) for d in range(n)])
        low, high = jnp.concatenate([mine, got], axis=1), jnp.concatenate([got, mine], axis=1)
        ready = jnp.where(position % 2 == 0, low, high)
        share = text // n
        handed = lax.ppermute(ready[share:], "tiles", [(d, d ^ 2) for d in upper])
        rows_valid = position * share + jnp.arange(share, dtype=jnp.int32) < text_count[0]
        text_out = jnp.where((position & 2) == 0, handed, ready[:share])
        text_out = jnp.where(rows_valid[:, None], text_out, 0)
    if not halving:
        text_out = text_plain(position, n, text_count, text_q, video_k, video_v, counts)
    return (outs[-1], text_out)


def solution(mesh):
    tiles = mesh.shape["tiles"]
    return jax.shard_map(
        functools.partial(per_device, tiles),
        mesh=mesh,
        in_specs=(
            P(("groups", "tiles"), None),
            P(("groups", "tiles"), None),
            P(("groups", "tiles"), None),
            P("groups", None),
            P("groups", None),
            P("groups", None),
            P("tiles", None),
            P(("groups", "tiles")),
            P("groups"),
        ),
        out_specs=(P(("groups", "tiles"), None), P(("groups", "tiles"), None)),
        check_vma=False,
    )
```
